128 devices in a mesh: leaf: 16 (over x, z), front: 8 (over y, core).
Axes of the slice: x: 4, y: 4, z: 4, core: 2. Of those that a mesh axis runs over, the one named last changes fastest.
Arguments:
- block_now: float32 [64, 266240], P(None, ('leaf', 'front')), may hold values from -18 to 18
- block_before: float32 [64, 266240], P(None, ('leaf', 'front')), may hold values from -6 to 6
- coupling: float32 [64, 64], replicated, may hold values from -1.8 to 1.8, as said below
- vertex_to_tree: int32 [266240], P(('leaf', 'front')), may hold values from 0 to 266239, as said below
- tree_to_vertex: int32 [266240], P(('leaf', 'front')), may hold values from 0 to 266239, as said below
- leaf_inverse: float32 [1024, 256, 256], P(('leaf', 'front')), may hold values from -1 to 2, as said below
- leaf_below: float32 [1024, 256, 256], P(('leaf', 'front')), may hold values from -0.02734375 to 0.02734375
- leaf_rows: int32 [1024, 256], P(('leaf', 'front')), may hold values from 0 to 1279, as said below
- sep_inverse: float32 [16, 256, 256], replicated, may hold values from -1 to 2, as said below
- sep_parent: float32 [15, 256, 256], replicated, may hold values from -0.1875 to 0.1875
Outputs:
- projection: float32 [64, 64], replicated
- factor: float32 [64, 64], replicated
- next_block: float32 [64, 266240], P(None, ('leaf', 'front'))
The draws below stay inside these ranges and needn't reach their ends.
Inputs may be any that keep to these rules, and one draw needn't show every extreme that they name: `vertex_to_tree`: a permutation; the vertices of one device go to every device in near-equal numbers, 16 or 17 to each, and some device sends 17 to some device. `tree_to_vertex`: the inverse permutation of vertex_to_tree. `leaf_rows`: each row holds 256 different path positions in increasing order, and every row includes position 1279. `leaf_inverse`: each block is lower triangular with a positive diagonal. `sep_inverse`: each block is lower triangular with a positive diagonal. `coupling`: upper triangular.
All inputs are finite; a program needn't handle non-finite values.
Results may differ from the reference program's by a relative error of at most 0.0012.
Values sent between devices are 32-bit elements; how exact they have to be, the bound alone decides.
No kernel may reach another device: no remote copies, remote signals or barrier semaphores. Data moves between devices by JAX's collectives and lax.ppermute only.
A program may use at most 64 MiB of HBM per device.

```python
import math
from functools import partial
import jax
import jax.numpy as jnp
import numpy as np
from jax import lax

K = 64
WL = 256
RL = 256
WS = 256
NBD = 8
LEVELS = 5
PATH = 1280
V_DEV = 2080
NV = 266240
LEAVES = 1024
N_LEAF = 16
N_FRONT = 8


def assemble_lower(lower_part, diagonal, block_width):
    row_ids = jnp.arange(block_width)[:, None]
    col_ids = jnp.arange(block_width)[None, :]
    strict = (row_ids > col_ids).astype(jnp.float32)
    on_diagonal = (row_ids == col_ids).astype(jnp.float32)
    return lower_part * strict * (0.6 / math.sqrt(block_width)) + diagonal[:, :, None] * on_diagonal


def draw_leaf_inverse(key, part):
    key = jax.random.fold_in(key, 11)
    key_lower, key_diag = jax.random.split(key)
    block_count = NBD * N_LEAF * N_FRONT
    lower_part = jnp.clip(jax.random.normal(key_lower, (block_count, WL, WL), jnp.float32), -6.0, 6.0)
    diagonal = jnp.exp(jax.random.uniform(key_diag, (block_count, WL), jnp.float32, math.log(0.5), math.log(2.0)))
    return assemble_lower(lower_part, diagonal, WL)


def draw_sep_inverse(key, part):
    key = jax.random.fold_in(key, 12)
    key_lower, key_diag = jax.random.split(key)
    lower_part = jnp.clip(jax.random.normal(key_lower, (N_LEAF, WS, WS), jnp.float32), -6.0, 6.0)
    diagonal = jnp.exp(jax.random.uniform(key_diag, (N_LEAF, WS), jnp.float32, math.log(0.5), math.log(2.0)))
    return assemble_lower(lower_part, diagonal, WS)


def draw_leaf_rows(key, part):
    key = jax.random.fold_in(key, 13)
    block_count = NBD * N_LEAF * N_FRONT
    positions = jnp.arange(PATH, dtype=jnp.int32)[None, :]
    scores = jax.random.randint(key, (block_count, PATH), 0, 2 ** 19, jnp.int32) * PATH + positions
    scores = jnp.where(positions == PATH - 1, jnp.int32(2147483647), scores)
    chosen = lax.top_k(scores, RL)[1]
    return jnp.sort(chosen, axis=1).astype(jnp.int32)


def owner_targets(key):
    devices = N_LEAF * N_FRONT
    key_labels, key_spread, key_within = jax.random.split(key, 3)
    labels = jax.random.permutation(key_labels, devices)
    spread = jax.vmap(partial(jax.random.permutation, x=V_DEV))(jax.random.split(key_spread, devices))
    within = jax.vmap(partial(jax.random.permutation, x=V_DEV))(jax.random.split(key_within, devices))
    global_index = spread * devices + labels[:, None]
    target = global_index // V_DEV * V_DEV + within.reshape(-1)[global_index]
    return target.reshape(-1).astype(jnp.int32)


def draw_vertex_to_tree(key, part):
    return owner_targets(key)


def draw_tree_to_vertex(key, part):
    return jnp.argsort(owner_targets(key)).astype(jnp.int32)


def row_scaled(values, roughness, low_end, high_end, total_rows):
    position = jnp.arange(total_rows, dtype=jnp.float32)[None, :] / total_rows
    mean_square = (high_end ** 3 - low_end ** 3) / (3.0 * (high_end - low_end)) * 8.0 / math.log(9.0)
    return values * roughness * jnp.exp(position * math.log(3.0)) / math.sqrt(mean_square)


def draw_block_now(key, part):
    key = jax.random.fold_in(key, 15)
    key_values, key_rough = jax.random.split(key, 2)
    total_rows = V_DEV * N_LEAF * N_FRONT
    low_end = 0.6
    high_end = 1.4
    values = jnp.clip(jax.random.normal(key_values, (K, total_rows), jnp.float32), -5.0, 5.0)
    roughness = jax.random.uniform(key_rough, (1, total_rows), jnp.float32, low_end, high_end)
    return row_scaled(values, roughness, low_end, high_end, total_rows)


def draw_coupling(key, part):
    key = jax.random.fold_in(key, 16)
    key_upper, key_diag = jax.random.split(key)
    upper_part = jnp.clip(jax.random.normal(key_upper, (K, K), jnp.float32), -6.0, 6.0) * 0.3
    diagonal = jax.random.uniform(key_diag, (K,), jnp.float32, 0.5, 1.2)
    row_ids = jnp.arange(K)[:, None]
    col_ids = jnp.arange(K)[None, :]
    return upper_part * (row_ids < col_ids).astype(jnp.float32) + diagonal[:, None] * (row_ids == col_ids).astype(jnp.float32)


def steps_of(rng, shape, shards, low, largest):
    def one(dim, blocks):
        steps = jax.random.uniform(jax.random.fold_in(jax.random.fold_in(rng, 6), dim), (blocks,), jnp.float32, low / len(shards), largest / len(shards))
        return jnp.repeat(jnp.exp(steps), shape[dim] // blocks).reshape((-1,) + (1,) * (len(shape) - dim - 1))

    level = one(*shards[0])
    for cut in shards[1:]:
        level = level * one(*cut)
    return level


def gaussian(key, dims, scale, limit, shards=(), held_as=jnp.bfloat16):
    array = jax.random.normal(key, dims, jnp.float32) * scale
    if len(shards) > 0:
        array = steps_of(key, dims, shards, -0.22, 0.18) * array
    return jnp.clip(array, min=-limit, max=limit).astype(held_as)


def setup_inputs(seed: int = 0) -> dict:
    seeds = jax.random.split(jax.random.key(seed), 11)
    return {
        "block_now": draw_block_now(jax.random.fold_in(seeds[10], 71), 0),
        "block_before": gaussian(seeds[1], (K, NV), 1.0, 6.0, ((1, 128),), jnp.float32),
        "coupling": draw_coupling(jax.random.fold_in(seeds[10], 71), 0),
        "vertex_to_tree": draw_vertex_to_tree(jax.random.fold_in(seeds[10], 71), 0),
        "tree_to_vertex": draw_tree_to_vertex(jax.random.fold_in(seeds[10], 71), 0),
        "leaf_inverse": draw_leaf_inverse(jax.random.fold_in(seeds[10], 71), 0),
        "leaf_below": gaussian(seeds[6], (LEAVES, RL, WL), (WL * N_LEAF * N_FRONT * NBD * RL // PATH) ** -0.5, 0.02734375, ((0, 128),), jnp.float32),
        "leaf_rows": draw_leaf_rows(jax.random.fold_in(seeds[10], 71), 0),
        "sep_inverse": draw_sep_inverse(jax.random.fold_in(seeds[10], 71), 0),
        "sep_parent": gaussian(seeds[9], (N_LEAF - 1, WS, WS), (4 * WS) ** -0.5, 0.1875, (), jnp.float32),
    }


HIGHEST = lax.Precision.HIGHEST

def home_list(group_count, level_count):
    home_table = np.zeros(group_count, np.int64)
    for height in range(1, level_count):
        sep_count = group_count >> height
        for offset in range(sep_count):
            home_table[sep_count + offset] = offset * (1 << height) + (1 << height - 1)
    return home_table

def ids_at_height(group_count, level_count, height):
    if height < level_count:
        sep_count = group_count >> height
        return np.arange(sep_count) + sep_count
    return np.zeros(1, np.int64)

def reference(block_now, block_before, coupling, vertex_to_tree, tree_to_vertex, leaf_inverse, leaf_below, leaf_rows, sep_inverse, sep_parent):
    group_count = N_LEAF
    front_count = N_FRONT
    devices = group_count * front_count
    sep_share = WS // front_count
    leaf_span = NBD * WL
    tree_in = block_now[:, tree_to_vertex].reshape(K, devices, V_DEV)
    leaf_source = jnp.moveaxis(tree_in[:, :, :leaf_span], 1, 0).reshape(devices, K, NBD, WL)
    sep_home = jnp.moveaxis(tree_in[:, :, leaf_span:].reshape(K, group_count, WS), 1, 0)
    inverse_dev = leaf_inverse.reshape(devices, NBD, WL, WL)
    below_dev = leaf_below.reshape(devices, NBD, RL, WL)
    rows_dev = leaf_rows.reshape(devices, NBD, RL)

    def leaf_forward(pieces):
        inverse, below_block, row_index, source = pieces
        solved = jnp.einsum('bij,kbj->kbi', inverse, source, precision=HIGHEST)
        update = jnp.einsum('brj,kbj->kbr', below_block, solved, precision=HIGHEST)
        pushed = jnp.zeros((K, PATH), jnp.float32).at[:, row_index.reshape(-1)].add(update.reshape(K, NBD * RL))
        return (solved, pushed)
    leaf_solved, pushed_all = lax.map(leaf_forward, (inverse_dev, below_dev, rows_dev, leaf_source))
    group_pushed = pushed_all.reshape(group_count, front_count, K, LEVELS, WS).sum(axis=1)
    home_table = home_list(group_count, LEVELS)
    sep_source = sep_home[home_table]
    solved_levels = []
    carried = None
    for height in range(1, LEVELS + 1):
        sep_ids = ids_at_height(group_count, LEVELS, height)
        sep_count = sep_ids.shape[0]
        source = sep_source[sep_ids] - group_pushed[:, :, height - 1, :].reshape(sep_count, group_count // sep_count, K, WS).sum(axis=1)
        if carried is not None:
            source = source - carried
        solved = jnp.einsum('sij,skj->ski', sep_inverse[sep_ids], source, precision=HIGHEST)
        solved_levels.append(solved)
        if height < LEVELS:
            lifted = jnp.einsum('sij,skj->ski', sep_parent[sep_ids - 1], solved, precision=HIGHEST)
            pairs = max(sep_count // 2, 1)
            carried = lifted.reshape(pairs, sep_count // pairs, K, WS).sum(axis=1)
    back_levels = [None] * LEVELS
    for height in range(LEVELS, 0, -1):
        sep_ids = ids_at_height(group_count, LEVELS, height)
        source = solved_levels[height - 1]
        if height < LEVELS:
            parent_vals = back_levels[height]
            parent_vals = jnp.repeat(parent_vals, sep_ids.shape[0] // parent_vals.shape[0], axis=0)
            source = source - jnp.einsum('sji,skj->ski', sep_parent[sep_ids - 1], parent_vals, precision=HIGHEST)
        back_levels[height - 1] = jnp.einsum('sji,skj->ski', sep_inverse[sep_ids], source, precision=HIGHEST)
    members = np.arange(group_count)
    group_path = jnp.stack([back_levels[height - 1][members >> height] for height in range(1, LEVELS + 1)], axis=2).reshape(group_count, K, PATH)
    owners = jnp.arange(devices, dtype=jnp.int32) // front_count

    def leaf_backward(pieces):
        inverse, below_block, row_index, solved, owner_group = pieces
        known_rows = group_path[owner_group][:, row_index]
        source = solved - jnp.einsum('brj,kbr->kbj', below_block, known_rows, precision=HIGHEST)
        return jnp.einsum('bji,kbj->kbi', inverse, source, precision=HIGHEST)
    leaf_back = lax.map(leaf_backward, (inverse_dev, below_dev, rows_dev, leaf_solved, owners))
    by_number = jnp.zeros((group_count, K, WS), jnp.float32)
    for height in range(1, LEVELS + 1):
        by_number = by_number.at[ids_at_height(group_count, LEVELS, height)].set(back_levels[height - 1])
    at_home = by_number[np.argsort(home_table)]
    sep_part = jnp.moveaxis(at_home, 0, 1).reshape(K, devices, sep_share)
    leaf_part = jnp.moveaxis(leaf_back.reshape(devices, K, leaf_span), 0, 1)
    tree_out = jnp.concatenate([leaf_part, sep_part], axis=2).reshape(K, NV)
    solved_block = tree_out[:, vertex_to_tree]
    projection = jnp.einsum('kn,jn->kj', block_now, solved_block, precision=HIGHEST) / NV
    residual = solved_block - jnp.einsum('jk,jn->kn', projection, block_now, precision=HIGHEST) - jnp.einsum('kj,jn->kn', coupling, block_before, precision=HIGHEST)
    gram_matrix = jnp.einsum('kn,jn->kj', residual, residual, precision=HIGHEST) / NV
    lower_factor = jnp.linalg.cholesky(gram_matrix)
    next_block = jax.scipy.linalg.solve_triangular(lower_factor, residual, lower=True)
    return (projection, lower_factor.T, next_block)
```

```python
import jax
import jax.numpy as jnp
from jax import lax
from jax.experimental import pallas as pl
from jax.experimental.pallas import tpu as pltpu
from jax.sharding import PartitionSpec as P

F32 = jnp.float32
BF16 = jnp.bfloat16
HIGHEST = lax.Precision.HIGHEST
AXES = ("leaf", "front")
DEV = 128
CAP = 17
ROWS = 2080
PAD = 2176
VEC = 64
LEAF = 256
NLEAF = 8
SPAN = 2048
GROUPS = 16
FRONT = 8
SHARE = 32
LEVELS = 5
PATH = 1280
S1 = 18
S2 = 10
S3 = 5
S4 = 10
MIB = 1024 * 1024


def nn(a, b):
    return lax.dot_general(a, b, (((1,), (0,)), ((), ())), preferred_element_type=F32)


def nt(a, b):
    return lax.dot_general(a, b, (((1,), (1,)), ((), ())), preferred_element_type=F32)


def nn32(a, b):
    return lax.dot_general(
        a, b, (((1,), (0,)), ((), ())), preferred_element_type=F32, precision=HIGHEST
    )


def nt32(a, b):
    return lax.dot_general(
        a, b, (((1,), (1,)), ((), ())), preferred_element_type=F32, precision=HIGHEST
    )


def split(x):
    hi = x.astype(BF16)
    lo = (x - hi.astype(F32)).astype(BF16)
    return hi, lo


def iota(shape, dim):
    return lax.broadcasted_iota(jnp.int32, shape, dim)


def onehot(mask):
    return jnp.where(mask, 1.0, 0.0).astype(BF16)


def both(x):
    return x + pltpu.roll(x, 64, 1)


def lanes_split(x):
    hi, lo = split(x)
    return jnp.where(iota(x.shape, 1) < 64, hi.astype(F32), lo.astype(F32)).astype(BF16)


def pack_kernel(vt_ref, now_ref, before_ref, out_ref, key_ref, dest, member, value, mark):
    dest[...] = jnp.full((8, PAD), -1, jnp.int32)
    dest[0:1, 0:ROWS] = vt_ref[...]
    target = dest[0:1, :]
    bucket = ((target.astype(F32) + 0.5) * (1.0 / ROWS)).astype(jnp.int32)
    bucket = jnp.where(target < 0, -1, bucket)
    place = target - bucket * ROWS
    member[...] = onehot(jnp.broadcast_to(bucket, (DEV, PAD)) == iota((DEV, PAD), 0))
    value[...] = jnp.zeros((4 * VEC, PAD), BF16)
    now_hi, now_lo = split(now_ref[...])
    bef_hi, bef_lo = split(before_ref[...])
    value[0:64, 0:ROWS] = now_hi
    value[64:128, 0:ROWS] = bef_hi
    value[128:192, 0:ROWS] = now_lo
    value[192:256, 0:ROWS] = bef_lo
    before = onehot(
        (iota((128, 256), 0) < iota((128, 256), 1)) | (iota((128, 256), 1) >= 128)
    )
    carry = jnp.zeros((DEV, 128), F32)
    ranks = []
    for b in range(CAP):
        part = member[:, b * 128 : (b + 1) * 128]
        counts = nn(part, before)
        ranks.append(
            jnp.sum(part.astype(F32) * (counts[:, 0:128] + carry), axis=0, keepdims=True)
        )
        carry = carry + counts[:, 128:256]
    rank = jnp.concatenate(ranks, axis=1).astype(jnp.int32)
    key = jnp.where(target < 0, -1, rank * DEV + bucket)
    key_ref[...] = key[:, 0:ROWS]
    for k in range(CAP):
        mark[k * DEV : (k + 1) * DEV, :] = onehot(
            jnp.broadcast_to(key, (DEV, PAD)) == iota((DEV, PAD), 0) + k * DEV
        )
    for c in range(CAP):
        block = nt(mark[c * DEV : (c + 1) * DEV, :], value[...])
        out_ref[pl.ds(c, DEV, stride=S1), :] = block[:, 0:128] + block[:, 128:256]
    ranked = jnp.broadcast_to(rank, (32, PAD)) == iota((32, PAD), 0)
    high = place // 64
    marks = jnp.concatenate(
        [
            jnp.where(ranked, jnp.broadcast_to(high, (32, PAD)).astype(F32), 0.0),
            jnp.where(ranked, jnp.broadcast_to(place - high * 64, (32, PAD)).astype(F32), 0.0),
            jnp.zeros((64, PAD), F32),
        ],
        axis=0,
    ).astype(BF16)
    found = nt(member[...], marks)
    where = found * 64.0 + pltpu.roll(found, 96, 1)
    lane = iota((DEV, 128), 1)
    filled = (lane.astype(F32) < carry) & (lane < CAP)
    out_ref[pl.ds(CAP, DEV, stride=S1), :] = jnp.where(filled, where, -1.0)


def own_gram_kernel(now_ref, before_ref, out_ref, value):
    now_hi, now_lo = split(now_ref[...])
    bef_hi, bef_lo = split(before_ref[...])
    value[0:64, :] = now_hi
    value[64:128, :] = bef_hi
    value[128:192, :] = now_lo
    value[192:256, :] = bef_lo
    gram = nt(value[...], value[...])
    rows = gram[0:128] + gram[128:256]
    out_ref[...] = rows[:, 0:128] + rows[:, 128:256]


def forward_kernel(
    home_ref,
    recv_ref,
    inv_ref,
    below_ref,
    rows_ref,
    out_ref,
    solved_ref,
    tree_ref,
    idx_ref,
    mark,
    value,
    moved,
    update,
):
    idx = recv_ref[pl.ds(CAP, DEV, stride=S1), :]
    idx_ref[...] = idx
    slots = idx.T.astype(jnp.int32)
    for k in range(CAP):
        hi, lo = split(recv_ref[pl.ds(k, DEV, stride=S1), :])
        value[k * DEV : (k + 1) * DEV, 0:128] = hi
        value[k * DEV : (k + 1) * DEV, 128:256] = lo
        mark[:, k * DEV : (k + 1) * DEV] = onehot(
            jnp.broadcast_to(slots[k : k + 1, :], (ROWS, DEV)) == iota((ROWS, DEV), 0)
        )
    got = nn(mark[...], value[...])
    tree_ref[...] = got[:, 0:128] + got[:, 128:256]
    for q in range(NLEAF):
        moved[:, q * LEAF : (q + 1) * LEAF] = onehot(
            jnp.broadcast_to(rows_ref[q : q + 1, :], (PATH, LEAF)) == iota((PATH, LEAF), 0)
        )
    low = iota((LEAF, 128), 1) < 64
    for q in range(NLEAF):
        source = tree_ref[q * LEAF : (q + 1) * LEAF, :]
        source = lanes_split(jnp.where(low, source, pltpu.roll(source, 64, 1)))
        hi, lo = split(inv_ref[q])
        solved = both(nn(hi, source) + nn(lo, source))
        solved_ref[:, q * LEAF : (q + 1) * LEAF] = solved.T[0:64, :]
        hi, lo = split(below_ref[q])
        solved = lanes_split(solved)
        update[q * LEAF : (q + 1) * LEAF, :] = lanes_split(both(nn(hi, solved) + nn(lo, solved)))
    pushed = both(nn(moved[...], update[...]))
    own = tree_ref[SPAN:ROWS, :]
    own = jnp.where(iota((SHARE, 128), 1) < 64, own, pltpu.roll(own, 64, 1))
    start = home_ref[0]
    for j in range(S2):
        chunk = -pushed[j * 128 : (j + 1) * 128, :]
        spread = jnp.concatenate([own] * 4, axis=0)
        at = iota((128, 128), 0) + (j * 128 - start)
        chunk = chunk + jnp.where((at >= 0) & (at < SHARE), spread, 0.0)
        out_ref[pl.ds(j, DEV, stride=S2), :] = chunk.T


def to_row(column, eye):
    top = jnp.sum(jnp.where(eye, column[0:128], 0.0), axis=0, keepdims=True)
    bottom = jnp.sum(jnp.where(eye, column[128:256], 0.0), axis=0, keepdims=True)
    return jnp.concatenate([top, bottom], axis=1)


def to_column(row, eye):
    top = jnp.sum(jnp.where(eye, row[:, 0:128], 0.0), axis=1, keepdims=True)
    bottom = jnp.sum(jnp.where(eye, row[:, 128:256], 0.0), axis=1, keepdims=True)
    return jnp.concatenate([top, bottom], axis=0)


def apply(matrix, row, eye):
    product = matrix * row
    return to_row(jnp.sum(product[:, 0:128] + product[:, 128:256], axis=1, keepdims=True), eye)


def apply_t(matrix, row, eye):
    return jnp.sum(matrix * to_column(row, eye), axis=0, keepdims=True)


def separator_kernel(half_ref, recv_ref, inv_ref, parent_ref, out_ref):
    eye = iota((128, 128), 0) == iota((128, 128), 1)
    source = {}
    for height in range(1, LEVELS + 1):
        count = max(GROUPS >> height, 1)
        first = count if height < LEVELS else 0
        span = DEV // count
        left = recv_ref[pl.ds(2 * height - 2, DEV, stride=S2), :]
        right = recv_ref[pl.ds(2 * height - 1, DEV, stride=S2), :]
        for c in range(count):
            at = slice(c * span, (c + 1) * span)
            source[first + c] = jnp.concatenate(
                [
                    jnp.sum(left[at], axis=0, keepdims=True),
                    jnp.sum(right[at], axis=0, keepdims=True),
                ],
                axis=1,
            )
    solved = {}
    for height in range(1, LEVELS + 1):
        count = max(GROUPS >> height, 1)
        first = count if height < LEVELS else 0
        for s in range(first, first + count):
            right = source[s]
            if height > 1:
                children = (1,) if s == 0 else (2 * s, 2 * s + 1)
                for c in children:
                    right = right - apply(parent_ref[c - 1], solved[c], eye)
            solved[s] = apply(inv_ref[s], right, eye)
    back = {}
    for height in range(LEVELS, 0, -1):
        count = max(GROUPS >> height, 1)
        first = count if height < LEVELS else 0
        for s in range(first, first + count):
            right = solved[s]
            if s > 0:
                right = right - apply_t(parent_ref[s - 1], back[s // 2], eye)
            back[s] = apply_t(inv_ref[s], right, eye)
    upper = half_ref[0] == 1
    for jj in range(S3):
        lines = []
        for g in range(GROUPS):
            ends = []
            for j in (jj, S3 + jj):
                s = (GROUPS + g) >> (j // 2 + 1)
                ends.append(back[s][:, (j % 2) * 128 : (j % 2) * 128 + 128])
            line = jnp.where(upper, ends[1], ends[0])
            lines.append(jnp.broadcast_to(line, (FRONT, 128)))
        out_ref[pl.ds(jj, DEV, stride=S3), :] = jnp.concatenate(lines, axis=0)


def backward_kernel(
    home_ref,
    recv_ref,
    inv_ref,
    below_ref,
    rows_ref,
    solved_ref,
    tree_ref,
    idx_ref,
    gram_ref,
    out_ref,
    known,
    parts,
    moved,
    mark,
    result,
    other,
):
    for q in range(NLEAF):
        moved[:, q * LEAF : (q + 1) * LEAF] = onehot(
            jnp.broadcast_to(rows_ref[q : q + 1, :], (PATH, LEAF)) == iota((PATH, LEAF), 0)
        )
    for h in range(2):
        for jj in range(S3):
            j = h * S3 + jj
            chunk = recv_ref[pl.ds(h * 64 * S3 + jj, 64, stride=S3), :]
            known[:, j * 128 : (j + 1) * 128] = chunk
            hi, lo = split(chunk)
            parts[0:64, j * 128 : (j + 1) * 128] = hi
            parts[64:128, j * 128 : (j + 1) * 128] = lo
    picked = nn(parts[...], moved[...])
    result[:, SPAN:PAD] = jnp.zeros((128, PAD - SPAN), BF16)
    start = home_ref[0]
    tile = pl.multiple_of((start // 128) * 128, 128)
    home = pltpu.roll(known[:, pl.ds(tile, 128)], (128 - start % 128) % 128, 1)
    home = jnp.where(iota((64, 128), 1) < SHARE, home, 0.0)
    hi, lo = split(home)
    result[0:64, SPAN:PAD] = hi
    result[64:128, SPAN:PAD] = lo
    for q in range(NLEAF):
        cols = slice(q * LEAF, (q + 1) * LEAF)
        rows = picked[0:64, cols] + picked[64:128, cols]
        hi, lo = split(rows)
        rows = jnp.concatenate([hi, lo], axis=0)
        hi, lo = split(below_ref[q])
        lifted = nn(rows, hi) + nn(rows, lo)
        source = solved_ref[:, cols] - (lifted[0:64] + lifted[64:128])
        hi, lo = split(source)
        source = jnp.concatenate([hi, lo], axis=0)
        hi, lo = split(inv_ref[q])
        solved = nn(source, hi) + nn(source, lo)
        hi, lo = split(solved[0:64] + solved[64:128])
        result[0:64, cols] = hi
        result[64:128, cols] = lo
    hi, lo = split(tree_ref[...])
    other[ROWS:PAD, :] = jnp.zeros((PAD - ROWS, 256), BF16)
    other[0:ROWS, 0:128] = hi
    other[0:ROWS, 128:256] = lo
    cross = nn(result[...], other[...])
    cross = cross[0:64] + cross[64:128]
    cross = cross[:, 0:128] + cross[:, 128:256]
    square = nt(result[...], result[...])
    square = both(square[0:64] + square[64:128])
    idx = idx_ref[...].astype(jnp.int32)
    for k in range(CAP):
        mark[k * DEV : (k + 1) * DEV, :] = onehot(
            jnp.broadcast_to(idx[:, k : k + 1], (DEV, PAD)) == iota((DEV, PAD), 1)
        )
    lane = iota((DEV, 128), 1) < 64
    packed = both(nt(mark[...], result[...]))
    for j in range(8):
        out_ref[pl.ds(j, DEV, stride=S4), :] = jnp.where(
            lane,
            packed[2 * j * DEV : (2 * j + 1) * DEV],
            packed[(2 * j + 1) * DEV : (2 * j + 2) * DEV],
        )
    late = jnp.concatenate([square, gram_ref[64:128, :]], axis=0)
    out_ref[pl.ds(8, DEV, stride=S4), :] = jnp.where(lane, packed[16 * DEV : 17 * DEV], late)
    out_ref[pl.ds(9, DEV, stride=S4), :] = jnp.concatenate([cross, gram_ref[0:64, :]], axis=0)


def total_kernel(recv_ref, out_ref):
    first = jnp.sum(recv_ref[pl.ds(9, DEV, stride=S4), :], axis=0, keepdims=True)
    second = jnp.sum(recv_ref[pl.ds(8, DEV, stride=S4), :], axis=0, keepdims=True)
    out_ref[pl.ds(0, DEV, stride=2), :] = jnp.broadcast_to(first, (DEV, 128))
    out_ref[pl.ds(1, DEV, stride=2), :] = jnp.broadcast_to(second, (DEV, 128))


def unpack_kernel(key_ref, recv_ref, out_ref, mark, value):
    lane = iota((DEV, 128), 1) < 64
    for j in range(9):
        got = recv_ref[pl.ds(j, DEV, stride=S4), :]
        hi, lo = split(got)
        hi, lo = hi.astype(F32), lo.astype(F32)
        value[2 * j * DEV : (2 * j + 1) * DEV, :] = jnp.where(
            lane, hi, pltpu.roll(lo, 64, 1)
        ).astype(BF16)
        if j < 8:
            value[(2 * j + 1) * DEV : (2 * j + 2) * DEV, :] = jnp.where(
                lane, pltpu.roll(hi, 64, 1), lo
            ).astype(BF16)
    key = key_ref[...]
    for k in range(CAP):
        mark[:, k * DEV : (k + 1) * DEV] = onehot(
            jnp.broadcast_to(key, (ROWS, DEV)) == iota((ROWS, DEV), 1) + k * DEV
        )
    solved = both(nn(mark[...], value[...]))
    for c in range(16):
        out_ref[:, c * 128 : (c + 1) * 128] = solved[c * 128 : (c + 1) * 128].T[0:64]
    out_ref[:, SPAN:ROWS] = solved[SPAN:ROWS].T[0:64]


def finish_kernel(
    recv_ref, solved_ref, now_ref, before_ref, coupling_ref, proj_ref, factor_ref, next_ref, value
):
    first = recv_ref[pl.ds(0, DEV, stride=2), :]
    second = recv_ref[pl.ds(1, DEV, stride=2), :]
    count = 1.0 / (ROWS * DEV)
    s_b = first[0:64, 0:64] * count
    s_a = first[0:64, 64:128] * count
    b_b = first[64:128, 0:64] * count
    b_a = first[64:128, 64:128] * count
    s_s = second[0:64, 64:128] * count
    a_a = second[64:128, 64:128] * count
    coupling = coupling_ref[...]
    proj_ref[...] = s_b.T
    line_s = s_s - nt32(s_b, s_b) - nt32(coupling, s_a)
    line_b = s_b - nn32(s_b, b_b) - nt32(coupling, b_a)
    line_a = s_a - nn32(s_b, b_a) - nn32(coupling, a_a)
    gram = line_s - nt32(line_b, s_b) - nt32(line_a, coupling)
    eye = iota((64, 64), 0) == iota((64, 64), 1)
    work = jnp.concatenate([gram, jnp.where(eye, 1.0, 0.0)], axis=1)
    below = iota((64, 128), 0)
    for j in range(63):
        row = work[j : j + 1, :]
        ratio = work[:, j : j + 1] / row[:, j : j + 1]
        work = work - jnp.where(below > j, ratio * row, 0.0)
    scale = lax.rsqrt(jnp.sum(jnp.where(eye, work[:, 0:64], 0.0), axis=1, keepdims=True))
    work = work * scale
    factor_ref[...] = jnp.where(iota((64, 64), 0) <= iota((64, 64), 1), work[:, 0:64], 0.0)
    inverse = work[:, 64:128]
    weight = jnp.concatenate(
        [inverse, -nn32(inverse, s_b), -nn32(inverse, coupling)], axis=1
    )
    hi, lo = split(weight)
    weight = jnp.concatenate([hi, lo], axis=0)
    for b, ref in enumerate((solved_ref, now_ref, before_ref)):
        hi, lo = split(ref[...])
        value[b * 64 : (b + 1) * 64, 0:ROWS] = hi
        value[b * 64 : (b + 1) * 64, PAD : PAD + ROWS] = lo
    high = nn(weight, value[:, 0:ROWS])
    low = nn(weight, value[:, PAD : PAD + ROWS])
    total = high + low
    next_ref[...] = total[0:64] + total[64:128]


def vmem(count):
    return [pl.BlockSpec(memory_space=pltpu.VMEM)] * count


def call(kernel, outs, operands, scratch=(), scalars=0, limit=56):
    return pl.pallas_call(
        kernel,
        out_shape=[jax.ShapeDtypeStruct(shape, dtype) for shape, dtype in outs],
        in_specs=[pl.BlockSpec(memory_space=pltpu.SMEM)] * scalars
        + vmem(len(operands) - scalars),
        out_specs=vmem(len(outs)),
        scratch_shapes=list(scratch),
        compiler_params=pltpu.CompilerParams(vmem_limit_bytes=limit * MIB),
    )(*operands)


def exchange(x, lines):
    return lax.all_to_all(
        x.reshape(DEV, 1, lines * 128), AXES, split_axis=0, concat_axis=0, tiled=True
    ).reshape(DEV * lines, 128)


def per_device(
    block_now,
    block_before,
    coupling,
    vertex_to_tree,
    tree_to_vertex,
    leaf_inverse,
    leaf_below,
    leaf_rows,
    sep_inverse,
    sep_parent,
):
    my_group = lax.axis_index("leaf")
    my_front = lax.axis_index("front")
    home_slot = jnp.zeros((), jnp.int32)
    for bit in range(LEVELS - 1):
        home_slot = home_slot + (my_group % (2 << bit) == 0).astype(jnp.int32)
    home_at = (home_slot * LEAF + my_front * SHARE).astype(jnp.int32).reshape(1)
    half = (my_group // 8).astype(jnp.int32).reshape(1)
    V = pltpu.VMEM
    packed, key = call(
        pack_kernel,
        [((DEV * S1, 128), F32), ((1, ROWS), jnp.int32)],
        (vertex_to_tree.reshape(1, ROWS), block_now, block_before),
        [V((8, PAD), jnp.int32), V((DEV, PAD), BF16), V((256, PAD), BF16), V((PAD, PAD), BF16)],
    )
    (own_gram,) = call(
        own_gram_kernel, [((128, 128), F32)], (block_now, block_before), [V((256, ROWS), BF16)]
    )
    arrived = exchange(packed, S1)
    pushed, leaf_solved, tree, idx = call(
        forward_kernel,
        [((DEV * S2, 128), F32), ((64, SPAN), F32), ((ROWS, 128), F32), ((DEV, 128), F32)],
        (home_at, arrived, leaf_inverse, leaf_below, leaf_rows),
        [V((ROWS, PAD), BF16), V((PAD, 256), BF16), V((PATH, SPAN), BF16), V((SPAN, 128), BF16)],
        1,
    )
    pushed = exchange(pushed, S2)
    (paths,) = call(
        separator_kernel,
        [((DEV * S3, 128), F32)],
        (half, pushed, sep_inverse, sep_parent),
        (),
        1,
    )
    paths = exchange(paths, S3)
    (returning,) = call(
        backward_kernel,
        [((DEV * S4, 128), F32)],
        (home_at, paths, leaf_inverse, leaf_below, leaf_rows, leaf_solved, tree, idx, own_gram),
        [
            V((64, PATH), F32),
            V((128, PATH), BF16),
            V((PATH, SPAN), BF16),
            V((PAD, PAD), BF16),
            V((128, PAD), BF16),
            V((PAD, 256), BF16),
        ],
        1,
    )
    returned = exchange(returning, S4)
    (sums,) = call(total_kernel, [((DEV * 2, 128), F32)], (returned,))
    sums = exchange(sums, 2)
    (solved,) = call(
        unpack_kernel,
        [((64, ROWS), F32)],
        (key.reshape(ROWS, 1), returned),
        [V((ROWS, PAD), BF16), V((PAD, 128), BF16)],
    )
    return tuple(
        call(
            finish_kernel,
            [((64, 64), F32), ((64, 64), F32), ((64, ROWS), F32)],
            (sums, solved, block_now, block_before, coupling),
            [V((192, 2 * PAD), BF16)],
        )
    )


def solution(mesh):
    placed = (
        P(None, AXES),
        P(None, AXES),
        P(),
        P(AXES),
        P(AXES),
        P(AXES, None, None),
        P(AXES, None, None),
        P(AXES, None),
        P(),
        P(),
    )
    return jax.shard_map(
        per_device,
        mesh=mesh,
        in_specs=placed,
        out_specs=(P(), P(), P(None, AXES)),
        check_vma=False,
    )
```

```python
import jax
import jax.numpy as jnp
from jax import lax
from jax.experimental import pallas as pl
from jax.experimental.pallas import tpu as pltpu
from jax.sharding import PartitionSpec as P

F32 = jnp.float32
BF16 = jnp.bfloat16
HIGHEST = lax.Precision.HIGHEST
AXES = ("leaf", "front")
DEV = 128
CAP = 17
ROWS = 2080
PAD = 2176
VEC = 64
LEAF = 256
NLEAF = 8
SPAN = 2048
GROUPS = 16
FRONT = 8
SHARE = 32
LEVELS = 5
PATH = 1280
S1 = 18
S2 = 10
S3 = 5
S4 = 10
MIB = 1024 * 1024


def nn(a, b):
    return lax.dot_general(a, b, (((1,), (0,)), ((), ())), preferred_element_type=F32)


def nt(a, b):
    return lax.dot_general(a, b, (((1,), (1,)), ((), ())), preferred_element_type=F32)


def tn(a, b):
    return lax.dot_general(a, b, (((0,), (0,)), ((), ())), preferred_element_type=F32)


def nn32(a, b):
    return lax.dot_general(
        a, b, (((1,), (0,)), ((), ())), preferred_element_type=F32, precision=HIGHEST
    )


def nt32(a, b):
    return lax.dot_general(
        a, b, (((1,), (1,)), ((), ())), preferred_element_type=F32, precision=HIGHEST
    )


def split(x):
    hi = x.astype(BF16)
    lo = (x - hi.astype(F32)).astype(BF16)
    return hi, lo


def iota(shape, dim):
    return lax.broadcasted_iota(jnp.int32, shape, dim)


I16 = jnp.int16


def onehot(mask):
    return jnp.where(mask, jnp.ones((), BF16), jnp.zeros((), BF16))


def onehot32(mask):
    return jnp.where(mask, 1.0, 0.0).astype(BF16)


def mark_row(row, height, start):
    width = row.shape[1]
    wide = jnp.broadcast_to(row, (16, width)).astype(I16)
    wide = jnp.concatenate([wide] * (height // 16), axis=0)
    return onehot(wide == (iota((height, width), 0) + start).astype(I16))


def mark_column(column, width):
    height = column.shape[0]
    wide = jnp.broadcast_to(column, (height, 128)).astype(I16)
    wide = jnp.concatenate([wide] * (width // 128), axis=1)
    return onehot(wide == iota((height, width), 1).astype(I16))


def stacked(x):
    hi, lo = split(x)
    return jnp.concatenate([hi, lo], axis=0)


def both(x):
    return x + pltpu.roll(x, 64, 1)


def folded(x):
    half = x.shape[0] // 2
    return x[0:half] + x[half:]


def pack_kernel(vt_ref, now_ref, before_ref, out_ref, key_ref, dest, member, value, mark):
    dest[...] = jnp.full((8, PAD), -1, jnp.int32)
    dest[0:1, 0:ROWS] = vt_ref[...]
    target = dest[0:1, :]
    bucket = ((target.astype(F32) + 0.5) * (1.0 / ROWS)).astype(jnp.int32)
    bucket = jnp.where(target < 0, -1, bucket)
    place = target - bucket * ROWS
    member[...] = mark_row(bucket, DEV, 0)
    value[...] = jnp.zeros((4 * VEC, PAD), BF16)
    now_hi, now_lo = split(now_ref[...])
    bef_hi, bef_lo = split(before_ref[...])
    value[0:64, 0:ROWS] = now_hi
    value[64:128, 0:ROWS] = bef_hi
    value[128:192, 0:ROWS] = now_lo
    value[192:256, 0:ROWS] = bef_lo
    before = onehot32(
        (iota((128, 256), 0) < iota((128, 256), 1)) | (iota((128, 256), 1) >= 128)
    )
    carry = jnp.zeros((DEV, 128), F32)
    ranks = []
    for b in range(CAP):
        part = member[:, b * 128 : (b + 1) * 128]
        counts = nn(part, before)
        ranks.append(
            jnp.sum(part.astype(F32) * (counts[:, 0:128] + carry), axis=0, keepdims=True)
        )
        carry = carry + counts[:, 128:256]
    rank = jnp.concatenate(ranks, axis=1).astype(jnp.int32)
    key = jnp.where(target < 0, -1, rank * DEV + bucket)
    key_ref[...] = key
    for k in range(CAP):
        mark[k * DEV : (k + 1) * DEV, :] = mark_row(key, DEV, k * DEV)
    block = nt(mark[...], value[...])
    block = block[:, 0:128] + block[:, 128:256]
    for k in range(CAP):
        out_ref[pl.ds(k, DEV, stride=S1), :] = block[k * DEV : (k + 1) * DEV]
    ranked = jnp.broadcast_to(rank, (32, PAD)) == iota((32, PAD), 0)
    high = place // 64
    marks = jnp.concatenate(
        [
            jnp.where(ranked, jnp.broadcast_to(high, (32, PAD)).astype(F32), 0.0),
            jnp.where(ranked, jnp.broadcast_to(place - high * 64, (32, PAD)).astype(F32), 0.0),
            jnp.zeros((64, PAD), F32),
        ],
        axis=0,
    ).astype(BF16)
    found = nt(member[...], marks)
    where = found * 64.0 + pltpu.roll(found, 96, 1)
    lane = iota((DEV, 128), 1)
    filled = (lane.astype(F32) < carry) & (lane < CAP)
    out_ref[pl.ds(CAP, DEV, stride=S1), :] = jnp.where(filled, where, -1.0)


def forward_kernel(
    home_ref,
    recv_ref,
    inv_ref,
    below_ref,
    rows_ref,
    out_ref,
    solved_ref,
    tree_ref,
    mark,
    value,
    moved,
    update,
):
    idx = recv_ref[pl.ds(CAP, DEV, stride=S1), :].astype(jnp.int32)
    for k in range(CAP):
        got = recv_ref[pl.ds(k, DEV, stride=S1), :].T
        value[:, k * DEV : (k + 1) * DEV] = stacked(got[0:64])
        mark[k * DEV : (k + 1) * DEV, :] = mark_column(idx[:, k : k + 1], PAD)
    tree_ref[...] = folded(nn(value[...], mark[...]))
    rows = rows_ref[...].astype(F32).T.astype(jnp.int32)
    for q in range(NLEAF):
        cols = slice(q * LEAF, (q + 1) * LEAF)
        hi, lo = split(inv_ref[q])
        source = stacked(tree_ref[:, cols])
        solved = folded(nt(source, hi) + nt(source, lo))
        solved_ref[:, cols] = solved
        hi, lo = split(below_ref[q])
        solved = stacked(solved)
        update[:, cols] = stacked(folded(nt(solved, hi) + nt(solved, lo)))
        moved[cols, :] = mark_column(rows[:, q : q + 1], PATH)
    pushed = folded(nn(update[...], moved[...]))
    start = home_ref[0]
    own = pltpu.roll(tree_ref[:, SPAN:PAD], start % 128, 1)
    for j in range(S2):
        chunk = jnp.where(start // 128 == j, own, 0.0) - pushed[:, j * 128 : (j + 1) * 128]
        out_ref[pl.ds(j, DEV, stride=S2), :] = jnp.concatenate([chunk, chunk], axis=0)


def side_kernel(recv_ref, tree_ref, other_ref, gram_ref, mark, value):
    idx = recv_ref[pl.ds(CAP, DEV, stride=S1), :].astype(jnp.int32)
    for k in range(CAP):
        got = recv_ref[pl.ds(k, DEV, stride=S1), :].T
        value[:, k * DEV : (k + 1) * DEV] = stacked(got[64:128])
        mark[k * DEV : (k + 1) * DEV, :] = mark_column(idx[:, k : k + 1], PAD)
    before = folded(nn(value[...], mark[...]))
    hi, lo = split(tree_ref[...])
    other_ref[0:64, :] = hi
    other_ref[128:192, :] = lo
    hi, lo = split(before)
    other_ref[64:128, :] = hi
    other_ref[192:256, :] = lo
    gram = folded(nt(other_ref[...], other_ref[...]))
    gram_ref[...] = gram[:, 0:128] + gram[:, 128:256]


def prepare_kernel(inv_ref, parent_ref, square_ref, link_ref):
    for s in range(GROUPS):
        hi, lo = split(inv_ref[s])
        square_ref[s] = tn(hi, hi) + (tn(hi, lo) + tn(lo, hi))
        if s > 0:
            up, down = split(parent_ref[s - 1])
            link_ref[s - 1] = nn(up, hi) + (nn(up, lo) + nn(down, hi))


def to_row(column, eye):
    top = jnp.sum(jnp.where(eye, column[0:128], 0.0), axis=0, keepdims=True)
    bottom = jnp.sum(jnp.where(eye, column[128:256], 0.0), axis=0, keepdims=True)
    return jnp.concatenate([top, bottom], axis=1)


def to_column(row, eye):
    top = jnp.sum(jnp.where(eye, row[:, 0:128], 0.0), axis=1, keepdims=True)
    bottom = jnp.sum(jnp.where(eye, row[:, 128:256], 0.0), axis=1, keepdims=True)
    return jnp.concatenate([top, bottom], axis=0)


def apply(matrix, row, eye):
    product = matrix * row
    return to_row(jnp.sum(product[:, 0:128] + product[:, 128:256], axis=1, keepdims=True), eye)


def apply_t(matrix, row, eye):
    return jnp.sum(matrix * to_column(row, eye), axis=0, keepdims=True)


def separator_kernel(half_ref, recv_ref, square_ref, link_ref, out_ref):
    eye = iota((128, 128), 0) == iota((128, 128), 1)
    source = {}
    for height in range(1, LEVELS + 1):
        count = max(GROUPS >> height, 1)
        first = count if height < LEVELS else 0
        span = DEV // count
        left = recv_ref[pl.ds(2 * height - 2, DEV, stride=S2), :]
        right = recv_ref[pl.ds(2 * height - 1, DEV, stride=S2), :]
        for c in range(count):
            at = slice(c * span, (c + 1) * span)
            source[first + c] = jnp.concatenate(
                [
                    jnp.sum(left[at], axis=0, keepdims=True),
                    jnp.sum(right[at], axis=0, keepdims=True),
                ],
                axis=1,
            )
    for height in range(2, LEVELS + 1):
        count = max(GROUPS >> height, 1)
        first = count if height < LEVELS else 0
        for s in range(first, first + count):
            for c in (1,) if s == 0 else (2 * s, 2 * s + 1):
                source[s] = source[s] - apply(link_ref[c - 1], source[c], eye)
    back = {}
    for s in range(GROUPS):
        back[s] = apply_t(square_ref[s], source[s], eye)
        if s > 0:
            back[s] = back[s] - apply_t(link_ref[s - 1], back[s // 2], eye)
    upper = half_ref[0] == 1
    for jj in range(S3):
        lines = []
        for g in range(GROUPS):
            ends = []
            for j in (jj, S3 + jj):
                s = (GROUPS + g) >> (j // 2 + 1)
                ends.append(back[s][:, (j % 2) * 128 : (j % 2) * 128 + 128])
            line = jnp.where(upper, ends[1], ends[0])
            lines.append(jnp.broadcast_to(line, (FRONT, 128)))
        out_ref[pl.ds(jj, DEV, stride=S3), :] = jnp.concatenate(lines, axis=0)


def backward_kernel(
    home_ref,
    recv_ref,
    arrived_ref,
    inv_ref,
    below_ref,
    rows_ref,
    solved_ref,
    other_ref,
    gram_ref,
    out_ref,
    known,
    parts,
    moved,
    mark,
    result,
):
    for q in range(NLEAF):
        moved[:, q * LEAF : (q + 1) * LEAF] = mark_row(rows_ref[q : q + 1, :], PATH, 0)
    for h in range(2):
        for jj in range(S3):
            j = h * S3 + jj
            chunk = recv_ref[pl.ds(h * 64 * S3 + jj, 64, stride=S3), :]
            known[:, j * 128 : (j + 1) * 128] = chunk
            parts[:, j * 128 : (j + 1) * 128] = stacked(chunk)
    picked = folded(nn(parts[...], moved[...]))
    start = home_ref[0]
    tile = pl.multiple_of((start // 128) * 128, 128)
    home = pltpu.roll(known[:, pl.ds(tile, 128)], (128 - start % 128) % 128, 1)
    home = jnp.where(iota((64, 128), 1) < SHARE, home, 0.0)
    result[:, SPAN:PAD] = stacked(home)
    for q in range(NLEAF):
        cols = slice(q * LEAF, (q + 1) * LEAF)
        hi, lo = split(below_ref[q])
        rows = stacked(picked[:, cols])
        source = stacked(solved_ref[:, cols] - folded(nn(rows, hi) + nn(rows, lo)))
        hi, lo = split(inv_ref[q])
        result[:, cols] = stacked(folded(nn(source, hi) + nn(source, lo)))
    cross = folded(nt(result[...], other_ref[...]))
    cross = cross[:, 0:128] + cross[:, 128:256]
    square = both(folded(nt(result[...], result[...])))
    slots = arrived_ref[pl.ds(CAP, DEV, stride=S1), :].T.astype(jnp.int32)
    for k in range(CAP):
        mark[:, k * DEV : (k + 1) * DEV] = mark_row(slots[k : k + 1, :], PAD, 0)
    packed = folded(nn(result[...], mark[...]))
    for j in range(8):
        pair = [packed[:, k * DEV : (k + 1) * DEV] for k in (2 * j, 2 * j + 1)]
        out_ref[pl.ds(j, DEV, stride=S4), :] = jnp.concatenate(pair, axis=0).T
    last = packed[:, 16 * DEV : 17 * DEV]
    last = jnp.concatenate([last, last], axis=0).T
    late = jnp.concatenate([square, gram_ref[64:128, :]], axis=0)
    out_ref[pl.ds(8, DEV, stride=S4), :] = jnp.where(iota((DEV, 128), 1) < 64, last, late)
    out_ref[pl.ds(9, DEV, stride=S4), :] = jnp.concatenate([cross, gram_ref[0:64, :]], axis=0)


def total_kernel(recv_ref, out_ref):
    first = jnp.sum(recv_ref[pl.ds(9, DEV, stride=S4), :], axis=0, keepdims=True)
    second = jnp.sum(recv_ref[pl.ds(8, DEV, stride=S4), :], axis=0, keepdims=True)
    out_ref[pl.ds(0, DEV, stride=2), :] = jnp.broadcast_to(first, (DEV, 128))
    out_ref[pl.ds(1, DEV, stride=2), :] = jnp.broadcast_to(second, (DEV, 128))


def unpack_kernel(key_ref, recv_ref, out_ref, mark, value):
    for k in range(CAP):
        mark[k * DEV : (k + 1) * DEV, :] = mark_row(key_ref[...], DEV, k * DEV)
    for j in range(9):
        got = recv_ref[pl.ds(j, DEV, stride=S4), :].T
        value[:, 2 * j * DEV : (2 * j + 1) * DEV] = stacked(got[0:64])
        if j < 8:
            value[:, (2 * j + 1) * DEV : (2 * j + 2) * DEV] = stacked(got[64:128])
    out_ref[...] = folded(nn(value[...], mark[...]))[:, 0:ROWS]


def finish_kernel(
    recv_ref, solved_ref, now_ref, before_ref, coupling_ref, proj_ref, factor_ref, next_ref, value
):
    first = recv_ref[pl.ds(0, DEV, stride=2), :]
    second = recv_ref[pl.ds(1, DEV, stride=2), :]
    count = 1.0 / (ROWS * DEV)
    s_b = first[0:64, 0:64] * count
    s_a = first[0:64, 64:128] * count
    b_b = first[64:128, 0:64] * count
    b_a = first[64:128, 64:128] * count
    s_s = second[0:64, 64:128] * count
    a_a = second[64:128, 64:128] * count
    coupling = coupling_ref[...]
    proj_ref[...] = s_b.T
    line_s = s_s - nt32(s_b, s_b) - nt32(coupling, s_a)
    line_b = s_b - nn32(s_b, b_b) - nt32(coupling, b_a)
    line_a = s_a - nn32(s_b, b_a) - nn32(coupling, a_a)
    gram = line_s - nt32(line_b, s_b) - nt32(line_a, coupling)
    eye = iota((64, 64), 0) == iota((64, 64), 1)
    work = jnp.concatenate([gram, jnp.where(eye, 1.0, 0.0)], axis=1)
    done = []
    for b in range(8):
        height = 64 - 8 * b
        at = 8 * b
        columns = [
            jnp.broadcast_to(work[:, at + c : at + c + 1], (height, 128)) for c in range(8)
        ]
        below = iota((height, 128), 0)
        for c in range(8):
            ratio = jnp.where(below > c, columns[c] * (1.0 / columns[c][c : c + 1, :]), 0.0)
            work = work - ratio * work[c : c + 1, :]
            for e in range(c + 1, 8):
                columns[e] = columns[e] - ratio * columns[e][c : c + 1, :]
        done.append(work[0:8])
        work = work[8:]
    work = jnp.concatenate(done, axis=0)
    scale = lax.rsqrt(jnp.sum(jnp.where(eye, work[:, 0:64], 0.0), axis=1, keepdims=True))
    work = work * scale
    factor_ref[...] = jnp.where(iota((64, 64), 0) <= iota((64, 64), 1), work[:, 0:64], 0.0)
    inverse = work[:, 64:128]
    weight = jnp.concatenate(
        [inverse, -nn32(inverse, s_b), -nn32(inverse, coupling)], axis=1
    )
    hi, lo = split(weight)
    weight = jnp.concatenate([hi, lo], axis=0)
    for b, ref in enumerate((solved_ref, now_ref, before_ref)):
        hi, lo = split(ref[...])
        value[b * 64 : (b + 1) * 64, 0:ROWS] = hi
        value[b * 64 : (b + 1) * 64, PAD : PAD + ROWS] = lo
    high = nn(weight, value[:, 0:ROWS])
    low = nn(weight, value[:, PAD : PAD + ROWS])
    total = high + low
    next_ref[...] = total[0:64] + total[64:128]


def vmem(count):
    return [pl.BlockSpec(memory_space=pltpu.VMEM)] * count


def call(kernel, outs, operands, scratch=(), scalars=0, limit=24, micros=4):
    return pl.pallas_call(
        kernel,
        out_shape=[jax.ShapeDtypeStruct(shape, dtype) for shape, dtype in outs],
        in_specs=[pl.BlockSpec(memory_space=pltpu.SMEM)] * scalars
        + vmem(len(operands) - scalars),
        out_specs=vmem(len(outs)),
        scratch_shapes=list(scratch),
        cost_estimate=pl.CostEstimate(
            flops=micros * 1000000000, bytes_accessed=micros * 3000000, transcendentals=0
        ),
        compiler_params=pltpu.CompilerParams(vmem_limit_bytes=limit * MIB),
    )(*operands)


def exchange(x, lines):
    return lax.all_to_all(
        x.reshape(DEV, 1, lines * 128), AXES, split_axis=0, concat_axis=0, tiled=True
    ).reshape(DEV * lines, 128)


def per_device(
    block_now,
    block_before,
    coupling,
    vertex_to_tree,
    tree_to_vertex,
    leaf_inverse,
    leaf_below,
    leaf_rows,
    sep_inverse,
    sep_parent,
):
    my_group = lax.axis_index("leaf")
    my_front = lax.axis_index("front")
    home_slot = jnp.zeros((), jnp.int32)
    for bit in range(LEVELS - 1):
        home_slot = home_slot + (my_group % (2 << bit) == 0).astype(jnp.int32)
    home_at = (home_slot * LEAF + my_front * SHARE).astype(jnp.int32).reshape(1)
    half = (my_group // 8).astype(jnp.int32).reshape(1)
    V = pltpu.VMEM
    packed, key = call(
        pack_kernel,
        [((DEV * S1, 128), F32), ((1, PAD), jnp.int32)],
        (vertex_to_tree.reshape(1, ROWS), block_now, block_before),
        [V((8, PAD), jnp.int32), V((DEV, PAD), BF16), V((256, PAD), BF16), V((PAD, PAD), BF16)],
    )
    arrived = exchange(packed, S1)
    square, link = call(
        prepare_kernel,
        [((GROUPS, LEAF, LEAF), F32), ((GROUPS - 1, LEAF, LEAF), F32)],
        (sep_inverse, sep_parent),
    )
    pushed, leaf_solved, tree = call(
        forward_kernel,
        [((DEV * S2, 128), F32), ((64, SPAN), F32), ((64, PAD), F32)],
        (home_at, arrived, leaf_inverse, leaf_below, leaf_rows),
        [V((PAD, PAD), BF16), V((128, PAD), BF16), V((SPAN, PATH), BF16), V((128, SPAN), BF16)],
        1,
    )
    pushed = exchange(pushed, S2)
    other, gram = call(
        side_kernel,
        [((256, PAD), BF16), ((128, 128), F32)],
        (arrived, tree),
        [V((PAD, PAD), BF16), V((128, PAD), BF16)],
    )
    (paths,) = call(
        separator_kernel,
        [((DEV * S3, 128), F32)],
        (half, pushed, square, link),
        (),
        1,
    )
    paths = exchange(paths, S3)
    (returning,) = call(
        backward_kernel,
        [((DEV * S4, 128), F32)],
        (
            home_at,
            paths,
            arrived,
            leaf_inverse,
            leaf_below,
            leaf_rows,
            leaf_solved,
            other,
            gram,
        ),
        [
            V((64, PATH), F32),
            V((128, PATH), BF16),
            V((PATH, SPAN), BF16),
            V((PAD, PAD), BF16),
            V((128, PAD), BF16),
        ],
        1,
    )
    returned = exchange(returning, S4)
    (sums,) = call(total_kernel, [((DEV * 2, 128), F32)], (returned,), micros=1)
    sums = exchange(sums, 2)
    (solved,) = call(
        unpack_kernel,
        [((64, ROWS), F32)],
        (key, returned),
        [V((PAD, PAD), BF16), V((128, PAD), BF16)],
    )
    return tuple(
        call(
            finish_kernel,
            [((64, 64), F32), ((64, 64), F32), ((64, ROWS), F32)],
            (sums, solved, block_now, block_before, coupling),
            [V((192, 2 * PAD), BF16)],
        )
    )


def solution(mesh):
    placed = (
        P(None, AXES),
        P(None, AXES),
        P(),
        P(AXES),
        P(AXES),
        P(AXES, None, None),
        P(AXES, None, None),
        P(AXES, None),
        P(),
        P(),
    )
    return jax.shard_map(
        per_device,
        mesh=mesh,
        in_specs=placed,
        out_specs=(P(), P(), P(None, AXES)),
        check_vma=False,
    )
```

```python
import jax
import jax.numpy as jnp
from jax import lax
from jax.experimental import pallas as pl
from jax.experimental.pallas import tpu as pltpu
from jax.sharding import PartitionSpec as P

F32 = jnp.float32
BF16 = jnp.bfloat16
HIGHEST = lax.Precision.HIGHEST
AXES = ("leaf", "front")
DEV = 128
CAP = 17
ROWS = 2080
PAD = 2176
VEC = 64
LEAF = 256
NLEAF = 8
SPAN = 2048
GROUPS = 16
FRONT = 8
SHARE = 32
LEVELS = 5
PATH = 1280
S1 = 18
S2 = 10
S3 = 5
S4 = 10
MIB = 1024 * 1024


def nn(a, b):
    return lax.dot_general(a, b, (((1,), (0,)), ((), ())), preferred_element_type=F32)


def nt(a, b):
    return lax.dot_general(a, b, (((1,), (1,)), ((), ())), preferred_element_type=F32)


def tn(a, b):
    return lax.dot_general(a, b, (((0,), (0,)), ((), ())), preferred_element_type=F32)


def nn32(a, b):
    return lax.dot_general(
        a, b, (((1,), (0,)), ((), ())), preferred_element_type=F32, precision=HIGHEST
    )


def nt32(a, b):
    return lax.dot_general(
        a, b, (((1,), (1,)), ((), ())), preferred_element_type=F32, precision=HIGHEST
    )


def split(x):
    hi = x.astype(BF16)
    lo = (x - hi.astype(F32)).astype(BF16)
    return hi, lo


def iota(shape, dim):
    return lax.broadcasted_iota(jnp.int32, shape, dim)


I16 = jnp.int16


def onehot(mask):
    return jnp.where(mask, jnp.ones((), BF16), jnp.zeros((), BF16))


def onehot32(mask):
    return jnp.where(mask, 1.0, 0.0).astype(BF16)


def mark_row(row, height, start):
    width = row.shape[1]
    wide = jnp.broadcast_to(row, (16, width)).astype(I16)
    wide = jnp.concatenate([wide] * (height // 16), axis=0)
    return onehot(wide == (iota((height, width), 0) + start).astype(I16))


def mark_column(column, width):
    height = column.shape[0]
    wide = jnp.broadcast_to(column, (height, 128)).astype(I16)
    wide = jnp.concatenate([wide] * (width // 128), axis=1)
    return onehot(wide == iota((height, width), 1).astype(I16))


def stacked(x):
    hi, lo = split(x)
    return jnp.concatenate([hi, lo], axis=0)


def both(x):
    return x + pltpu.roll(x, 64, 1)


def folded(x):
    half = x.shape[0] // 2
    return x[0:half] + x[half:]


def fetch(source, target, sem):
    copy = pltpu.make_async_copy(source, target, sem)
    copy.start()
    return copy


def pack_kernel(
    vt_ref, now_hbm, before_hbm, out_ref, key_ref, dest, member, value, mark, now, before, sems
):
    loads = [fetch(now_hbm, now, sems.at[0]), fetch(before_hbm, before, sems.at[1])]
    dest[...] = jnp.full((8, PAD), -1, jnp.int32)
    dest[0:1, 0:ROWS] = vt_ref[...]
    target = dest[0:1, :]
    bucket = ((target.astype(F32) + 0.5) * (1.0 / ROWS)).astype(jnp.int32)
    bucket = jnp.where(target < 0, -1, bucket)
    place = target - bucket * ROWS
    member[...] = mark_row(bucket, DEV, 0)
    earlier = onehot32(
        (iota((128, 256), 0) < iota((128, 256), 1)) | (iota((128, 256), 1) >= 128)
    )
    carry = jnp.zeros((DEV, 128), F32)
    ranks = []
    for b in range(CAP):
        part = member[:, b * 128 : (b + 1) * 128]
        counts = nn(part, earlier)
        ranks.append(
            jnp.sum(part.astype(F32) * (counts[:, 0:128] + carry), axis=0, keepdims=True)
        )
        carry = carry + counts[:, 128:256]
    rank = jnp.concatenate(ranks, axis=1).astype(jnp.int32)
    key = jnp.where(target < 0, -1, rank * DEV + bucket)
    key_ref[...] = key
    for k in range(CAP):
        mark[k * DEV : (k + 1) * DEV, :] = mark_row(key, DEV, k * DEV)
    for load in loads:
        load.wait()
    value[:, SPAN:PAD] = jnp.zeros((4 * VEC, PAD - SPAN), BF16)
    now_hi, now_lo = split(now[...])
    bef_hi, bef_lo = split(before[...])
    value[0:64, 0:ROWS] = now_hi
    value[64:128, 0:ROWS] = bef_hi
    value[128:192, 0:ROWS] = now_lo
    value[192:256, 0:ROWS] = bef_lo
    block = nt(mark[...], value[...])
    block = block[:, 0:128] + block[:, 128:256]
    for k in range(CAP):
        out_ref[pl.ds(k, DEV, stride=S1), :] = block[k * DEV : (k + 1) * DEV]
    ranked = jnp.broadcast_to(rank, (32, PAD)) == iota((32, PAD), 0)
    high = place // 64
    marks = jnp.concatenate(
        [
            jnp.where(ranked, jnp.broadcast_to(high, (32, PAD)).astype(F32), 0.0),
            jnp.where(ranked, jnp.broadcast_to(place - high * 64, (32, PAD)).astype(F32), 0.0),
            jnp.zeros((64, PAD), F32),
        ],
        axis=0,
    ).astype(BF16)
    found = nt(member[...], marks)
    where = found * 64.0 + pltpu.roll(found, 96, 1)
    lane = iota((DEV, 128), 1)
    filled = (lane.astype(F32) < carry) & (lane < CAP)
    out_ref[pl.ds(CAP, DEV, stride=S1), :] = jnp.where(filled, where, -1.0)


def forward_kernel(
    home_ref,
    recv_ref,
    rows_ref,
    inv_hbm,
    below_hbm,
    ready_hbm,
    out_ref,
    solved_hbm,
    tree_hbm,
    mark,
    value,
    moved,
    update,
    inv_ref,
    below_ref,
    solved_ref,
    tree_ref,
    sems,
):
    inv_loads = [
        fetch(inv_hbm.at[q], inv_ref.at[q], sems.at[q]) for q in range(NLEAF)
    ]
    below_loads = [
        fetch(below_hbm.at[q], below_ref.at[q], sems.at[NLEAF + q]) for q in range(NLEAF)
    ]
    idx = recv_ref[pl.ds(CAP, DEV, stride=S1), :].astype(jnp.int32)
    for k in range(CAP):
        got = recv_ref[pl.ds(k, DEV, stride=S1), :].T
        value[:, k * DEV : (k + 1) * DEV] = stacked(got[0:64])
        mark[k * DEV : (k + 1) * DEV, :] = mark_column(idx[:, k : k + 1], PAD)
    tree_ref[...] = folded(nn(value[...], mark[...]))
    stores = [fetch(tree_ref, tree_hbm, sems.at[2 * NLEAF])]
    rows = rows_ref[...].astype(F32).T.astype(jnp.int32)
    for q in range(NLEAF):
        cols = slice(q * LEAF, (q + 1) * LEAF)
        inv_loads[q].wait()
        hi, lo = split(inv_ref[q])
        source = stacked(tree_ref[:, cols])
        solved = folded(nt(source, hi) + nt(source, lo))
        solved_ref[:, cols] = solved
        below_loads[q].wait()
        hi, lo = split(below_ref[q])
        solved = stacked(solved)
        update[:, cols] = stacked(folded(nt(solved, hi) + nt(solved, lo)))
        moved[cols, :] = mark_column(rows[:, q : q + 1], PATH)
    stores.append(fetch(solved_ref, solved_hbm, sems.at[2 * NLEAF + 1]))
    pushed = folded(nn(update[...], moved[...]))
    start = home_ref[0]
    own = pltpu.roll(tree_ref[:, SPAN:PAD], start % 128, 1)
    for j in range(S2):
        chunk = jnp.where(start // 128 == j, own, 0.0) - pushed[:, j * 128 : (j + 1) * 128]
        out_ref[pl.ds(j, DEV, stride=S2), :] = jnp.concatenate([chunk, chunk], axis=0)
    for store in stores:
        store.wait()


def side_kernel(
    recv_ref, tree_hbm, other_hbm, idx_ref, gram_ref, mark, value, tree_ref, other_ref, sems
):
    load = fetch(tree_hbm, tree_ref, sems.at[0])
    where = recv_ref[pl.ds(CAP, DEV, stride=S1), :]
    idx_ref[...] = where.T
    idx = where.astype(jnp.int32)
    for k in range(CAP):
        got = recv_ref[pl.ds(k, DEV, stride=S1), :].T
        value[:, k * DEV : (k + 1) * DEV] = stacked(got[64:128])
        mark[k * DEV : (k + 1) * DEV, :] = mark_column(idx[:, k : k + 1], PAD)
    before = folded(nn(value[...], mark[...]))
    load.wait()
    hi, lo = split(tree_ref[...])
    other_ref[0:64, :] = hi
    other_ref[128:192, :] = lo
    hi, lo = split(before)
    other_ref[64:128, :] = hi
    other_ref[192:256, :] = lo
    store = fetch(other_ref, other_hbm, sems.at[1])
    gram = folded(nt(other_ref[...], other_ref[...]))
    gram_ref[...] = gram[:, 0:128] + gram[:, 128:256]
    store.wait()


def prepare_kernel(
    inv_hbm, parent_hbm, square_hbm, link_hbm, inv_ref, parent_ref, square_ref, link_ref, sems
):
    inv_loads = []
    parent_loads = []
    stores = []
    for s in range(GROUPS):
        inv_loads.append(fetch(inv_hbm.at[s], inv_ref.at[s], sems.at[s]))
        if s > 0:
            at = s - 1
            parent_loads.append(
                fetch(parent_hbm.at[at], parent_ref.at[at], sems.at[GROUPS + at])
            )
    for s in range(GROUPS):
        inv_loads[s].wait()
        hi, lo = split(inv_ref[s])
        square_ref[s] = tn(hi, hi) + (tn(hi, lo) + tn(lo, hi))
        stores.append(fetch(square_ref.at[s], square_hbm.at[s], sems.at[2 * GROUPS + s]))
        if s > 0:
            at = s - 1
            parent_loads[at].wait()
            up, down = split(parent_ref[at])
            link_ref[at] = nn(up, hi) + (nn(up, lo) + nn(down, hi))
            stores.append(fetch(link_ref.at[at], link_hbm.at[at], sems.at[3 * GROUPS + at]))
    for store in stores:
        store.wait()


def to_row(column, eye):
    top = jnp.sum(jnp.where(eye, column[0:128], 0.0), axis=0, keepdims=True)
    bottom = jnp.sum(jnp.where(eye, column[128:256], 0.0), axis=0, keepdims=True)
    return jnp.concatenate([top, bottom], axis=1)


def to_column(row, eye):
    top = jnp.sum(jnp.where(eye, row[:, 0:128], 0.0), axis=1, keepdims=True)
    bottom = jnp.sum(jnp.where(eye, row[:, 128:256], 0.0), axis=1, keepdims=True)
    return jnp.concatenate([top, bottom], axis=0)


def apply(matrix, row, eye):
    product = matrix * row
    return to_row(jnp.sum(product[:, 0:128] + product[:, 128:256], axis=1, keepdims=True), eye)


def apply_t(matrix, row, eye):
    return jnp.sum(matrix * to_column(row, eye), axis=0, keepdims=True)


def separator_kernel(
    half_ref, recv_ref, square_hbm, link_hbm, out_ref, square_ref, link_ref, sems
):
    loads = {}
    for at in range(GROUPS - 2, -1, -1):
        loads[at] = fetch(link_hbm.at[at], link_ref.at[at], sems.at[at])
    square_loads = [
        fetch(square_hbm.at[s], square_ref.at[s], sems.at[GROUPS + s]) for s in range(GROUPS)
    ]
    eye = iota((128, 128), 0) == iota((128, 128), 1)
    source = {}
    for height in range(1, LEVELS + 1):
        count = max(GROUPS >> height, 1)
        first = count if height < LEVELS else 0
        span = DEV // count
        left = recv_ref[pl.ds(2 * height - 2, DEV, stride=S2), :]
        right = recv_ref[pl.ds(2 * height - 1, DEV, stride=S2), :]
        for c in range(count):
            at = slice(c * span, (c + 1) * span)
            source[first + c] = jnp.concatenate(
                [
                    jnp.sum(left[at], axis=0, keepdims=True),
                    jnp.sum(right[at], axis=0, keepdims=True),
                ],
                axis=1,
            )
    for height in range(2, LEVELS + 1):
        count = max(GROUPS >> height, 1)
        first = count if height < LEVELS else 0
        for s in range(first, first + count):
            for c in (1,) if s == 0 else (2 * s, 2 * s + 1):
                loads[c - 1].wait()
                source[s] = source[s] - apply(link_ref[c - 1], source[c], eye)
    back = {}
    for s in range(GROUPS):
        square_loads[s].wait()
        back[s] = apply_t(square_ref[s], source[s], eye)
        if s > 0:
            back[s] = back[s] - apply_t(link_ref[s - 1], back[s // 2], eye)
    upper = half_ref[0] == 1
    for jj in range(S3):
        lines = []
        for g in range(GROUPS):
            ends = []
            for j in (jj, S3 + jj):
                s = (GROUPS + g) >> (j // 2 + 1)
                ends.append(back[s][:, (j % 2) * 128 : (j % 2) * 128 + 128])
            line = jnp.where(upper, ends[1], ends[0])
            lines.append(jnp.broadcast_to(line, (FRONT, 128)))
        out_ref[pl.ds(jj, DEV, stride=S3), :] = jnp.concatenate(lines, axis=0)


def backward_kernel(
    home_ref,
    recv_ref,
    rows_ref,
    idx_ref,
    gram_ref,
    inv_hbm,
    below_hbm,
    solved_hbm,
    other_hbm,
    out_ref,
    known,
    parts,
    moved,
    mark,
    result,
    inv_ref,
    below_ref,
    solved_ref,
    other_ref,
    sems,
):
    loads = [fetch(solved_hbm, solved_ref, sems.at[2 * NLEAF])]
    below_loads = []
    inv_loads = []
    for q in range(NLEAF):
        below_loads.append(fetch(below_hbm.at[q], below_ref.at[q], sems.at[q]))
        inv_loads.append(fetch(inv_hbm.at[q], inv_ref.at[q], sems.at[NLEAF + q]))
    loads.append(fetch(other_hbm, other_ref, sems.at[2 * NLEAF + 1]))
    for q in range(NLEAF):
        moved[:, q * LEAF : (q + 1) * LEAF] = mark_row(rows_ref[q : q + 1, :], PATH, 0)
    for h in range(2):
        for jj in range(S3):
            j = h * S3 + jj
            chunk = recv_ref[pl.ds(h * 64 * S3 + jj, 64, stride=S3), :]
            known[:, j * 128 : (j + 1) * 128] = chunk
            parts[:, j * 128 : (j + 1) * 128] = stacked(chunk)
    picked = folded(nn(parts[...], moved[...]))
    start = home_ref[0]
    tile = pl.multiple_of((start // 128) * 128, 128)
    home = pltpu.roll(known[:, pl.ds(tile, 128)], (128 - start % 128) % 128, 1)
    home = jnp.where(iota((64, 128), 1) < SHARE, home, 0.0)
    result[:, SPAN:PAD] = stacked(home)
    for q in range(NLEAF):
        cols = slice(q * LEAF, (q + 1) * LEAF)
        if q == 0:
            loads[0].wait()
        below_loads[q].wait()
        hi, lo = split(below_ref[q])
        rows = stacked(picked[:, cols])
        source = stacked(solved_ref[:, cols] - folded(nn(rows, hi) + nn(rows, lo)))
        inv_loads[q].wait()
        hi, lo = split(inv_ref[q])
        result[:, cols] = stacked(folded(nn(source, hi) + nn(source, lo)))
    loads[1].wait()
    cross = folded(nt(result[...], other_ref[...]))
    cross = cross[:, 0:128] + cross[:, 128:256]
    square = both(folded(nt(result[...], result[...])))
    slots = idx_ref[...].astype(jnp.int32)
    for k in range(CAP):
        mark[:, k * DEV : (k + 1) * DEV] = mark_row(slots[k : k + 1, :], PAD, 0)
    packed = folded(nn(result[...], mark[...]))
    for j in range(8):
        pair = [packed[:, k * DEV : (k + 1) * DEV] for k in (2 * j, 2 * j + 1)]
        out_ref[pl.ds(j, DEV, stride=S4), :] = jnp.concatenate(pair, axis=0).T
    last = packed[:, 16 * DEV : 17 * DEV]
    last = jnp.concatenate([last, last], axis=0).T
    late = jnp.concatenate([square, gram_ref[64:128, :]], axis=0)
    out_ref[pl.ds(8, DEV, stride=S4), :] = jnp.where(iota((DEV, 128), 1) < 64, last, late)
    out_ref[pl.ds(9, DEV, stride=S4), :] = jnp.concatenate([cross, gram_ref[0:64, :]], axis=0)


def total_kernel(recv_ref, out_ref):
    first = jnp.sum(recv_ref[pl.ds(9, DEV, stride=S4), :], axis=0, keepdims=True)
    second = jnp.sum(recv_ref[pl.ds(8, DEV, stride=S4), :], axis=0, keepdims=True)
    out_ref[pl.ds(0, DEV, stride=2), :] = jnp.broadcast_to(first, (DEV, 128))
    out_ref[pl.ds(1, DEV, stride=2), :] = jnp.broadcast_to(second, (DEV, 128))


def unpack_kernel(key_ref, recv_ref, out_ref, mark, value):
    for k in range(CAP):
        mark[k * DEV : (k + 1) * DEV, :] = mark_row(key_ref[...], DEV, k * DEV)
    for j in range(9):
        got = recv_ref[pl.ds(j, DEV, stride=S4), :].T
        value[:, 2 * j * DEV : (2 * j + 1) * DEV] = stacked(got[0:64])
        if j < 8:
            value[:, (2 * j + 1) * DEV : (2 * j + 2) * DEV] = stacked(got[64:128])
    out_ref[...] = folded(nn(value[...], mark[...]))[:, 0:ROWS]


def finish_kernel(
    recv_ref,
    solved_ref,
    coupling_ref,
    now_hbm,
    before_hbm,
    proj_ref,
    factor_ref,
    next_ref,
    value,
    now_ref,
    before_ref,
    sems,
):
    loads = [fetch(now_hbm, now_ref, sems.at[0]), fetch(before_hbm, before_ref, sems.at[1])]
    first = recv_ref[pl.ds(0, DEV, stride=2), :]
    second = recv_ref[pl.ds(1, DEV, stride=2), :]
    count = 1.0 / (ROWS * DEV)
    s_b = first[0:64, 0:64] * count
    s_a = first[0:64, 64:128] * count
    b_b = first[64:128, 0:64] * count
    b_a = first[64:128, 64:128] * count
    s_s = second[0:64, 64:128] * count
    a_a = second[64:128, 64:128] * count
    coupling = coupling_ref[...]
    proj_ref[...] = s_b.T
    line_s = s_s - nt32(s_b, s_b) - nt32(coupling, s_a)
    line_b = s_b - nn32(s_b, b_b) - nt32(coupling, b_a)
    line_a = s_a - nn32(s_b, b_a) - nn32(coupling, a_a)
    gram = line_s - nt32(line_b, s_b) - nt32(line_a, coupling)
    eye = iota((64, 64), 0) == iota((64, 64), 1)
    work = jnp.concatenate([gram, jnp.where(eye, 1.0, 0.0)], axis=1)
    done = []
    for b in range(8):
        height = 64 - 8 * b
        at = 8 * b
        columns = [
            jnp.broadcast_to(work[:, at + c : at + c + 1], (height, 128)) for c in range(8)
        ]
        below = iota((height, 128), 0)
        for c in range(8):
            ratio = jnp.where(below > c, columns[c] * (1.0 / columns[c][c : c + 1, :]), 0.0)
            work = work - ratio * work[c : c + 1, :]
            for e in range(c + 1, 8):
                columns[e] = columns[e] - ratio * columns[e][c : c + 1, :]
        done.append(work[0:8])
        work = work[8:]
    work = jnp.concatenate(done, axis=0)
    scale = lax.rsqrt(jnp.sum(jnp.where(eye, work[:, 0:64], 0.0), axis=1, keepdims=True))
    work = work * scale
    factor_ref[...] = jnp.where(iota((64, 64), 0) <= iota((64, 64), 1), work[:, 0:64], 0.0)
    inverse = work[:, 64:128]
    weight = jnp.concatenate(
        [inverse, -nn32(inverse, s_b), -nn32(inverse, coupling)], axis=1
    )
    hi, lo = split(weight)
    weight = jnp.concatenate([hi, lo], axis=0)
    for load in loads:
        load.wait()
    for b, ref in enumerate((solved_ref, now_ref, before_ref)):
        hi, lo = split(ref[...])
        value[b * 64 : (b + 1) * 64, 0:ROWS] = hi
        value[b * 64 : (b + 1) * 64, PAD : PAD + ROWS] = lo
    high = nn(weight, value[:, 0:ROWS])
    low = nn(weight, value[:, PAD : PAD + ROWS])
    total = high + low
    next_ref[...] = total[0:64] + total[64:128]


def vmem(count):
    return [pl.BlockSpec(memory_space=pltpu.VMEM)] * count


def call(kernel, outs, operands, scratch=(), scalars=0, far=0, far_outs=(), limit=52, micros=4):
    kinds = [pltpu.SMEM] * scalars + [pltpu.VMEM] * (len(operands) - scalars - far)
    kinds += [pltpu.HBM] * far
    return pl.pallas_call(
        kernel,
        out_shape=[jax.ShapeDtypeStruct(shape, dtype) for shape, dtype in outs],
        in_specs=[pl.BlockSpec(memory_space=kind) for kind in kinds],
        out_specs=[
            pl.BlockSpec(memory_space=pltpu.HBM if i in far_outs else pltpu.VMEM)
            for i in range(len(outs))
        ],
        scratch_shapes=list(scratch),
        cost_estimate=pl.CostEstimate(
            flops=micros * 1000000000, bytes_accessed=micros * 3000000, transcendentals=0
        ),
        compiler_params=pltpu.CompilerParams(vmem_limit_bytes=limit * MIB),
    )(*operands)


def exchange(x, lines):
    return lax.all_to_all(
        x.reshape(DEV, 1, lines * 128), AXES, split_axis=0, concat_axis=0, tiled=True
    ).reshape(DEV * lines, 128)


def per_device(
    block_now,
    block_before,
    coupling,
    vertex_to_tree,
    tree_to_vertex,
    leaf_inverse,
    leaf_below,
    leaf_rows,
    sep_inverse,
    sep_parent,
):
    my_group = lax.axis_index("leaf")
    my_front = lax.axis_index("front")
    home_slot = jnp.zeros((), jnp.int32)
    for bit in range(LEVELS - 1):
        home_slot = home_slot + (my_group % (2 << bit) == 0).astype(jnp.int32)
    home_at = (home_slot * LEAF + my_front * SHARE).astype(jnp.int32).reshape(1)
    half = (my_group // 8).astype(jnp.int32).reshape(1)
    V = pltpu.VMEM
    S = pltpu.SemaphoreType.DMA
    packed, key = call(
        pack_kernel,
        [((DEV * S1, 128), F32), ((1, PAD), jnp.int32)],
        (vertex_to_tree.reshape(1, ROWS), block_now, block_before),
        [
            V((8, PAD), jnp.int32),
            V((DEV, PAD), BF16),
            V((256, PAD), BF16),
            V((PAD, PAD), BF16),
            V((64, ROWS), F32),
            V((64, ROWS), F32),
            S((2,)),
        ],
        far=2,
        limit=58,
    )
    arrived = exchange(packed, S1)
    square, link = call(
        prepare_kernel,
        [((GROUPS, LEAF, LEAF), F32), ((GROUPS - 1, LEAF, LEAF), F32)],
        (sep_inverse, sep_parent),
        [
            V((GROUPS, LEAF, LEAF), F32),
            V((GROUPS - 1, LEAF, LEAF), F32),
            V((GROUPS, LEAF, LEAF), F32),
            V((GROUPS - 1, LEAF, LEAF), F32),
            S((4 * GROUPS,)),
        ],
        far=2,
        far_outs=(0, 1),
    )
    pushed, leaf_solved, tree = call(
        forward_kernel,
        [((DEV * S2, 128), F32), ((64, SPAN), F32), ((64, PAD), F32)],
        (home_at, arrived, leaf_rows, leaf_inverse, leaf_below, link),
        [
            V((PAD, PAD), BF16),
            V((128, PAD), BF16),
            V((SPAN, PATH), BF16),
            V((128, SPAN), BF16),
            V((NLEAF, LEAF, LEAF), F32),
            V((NLEAF, LEAF, LEAF), F32),
            V((64, SPAN), F32),
            V((64, PAD), F32),
            S((2 * NLEAF + 2,)),
        ],
        1,
        far=3,
        limit=50,
        far_outs=(1, 2),
    )
    pushed = exchange(pushed, S2)
    other, idx, gram = call(
        side_kernel,
        [((256, PAD), BF16), ((128, 128), F32), ((128, 128), F32)],
        (arrived, tree),
        [
            V((PAD, PAD), BF16),
            V((128, PAD), BF16),
            V((64, PAD), F32),
            V((256, PAD), BF16),
            S((2,)),
        ],
        far=1,
        far_outs=(0,),
    )
    (paths,) = call(
        separator_kernel,
        [((DEV * S3, 128), F32)],
        (half, pushed, square, link),
        [
            V((GROUPS, LEAF, LEAF), F32),
            V((GROUPS - 1, LEAF, LEAF), F32),
            S((2 * GROUPS,)),
        ],
        1,
        far=2,
    )
    paths = exchange(paths, S3)
    (returning,) = call(
        backward_kernel,
        [((DEV * S4, 128), F32)],
        (
            home_at,
            paths,
            leaf_rows,
            idx,
            gram,
            leaf_inverse,
            leaf_below,
            leaf_solved,
            other,
        ),
        [
            V((64, PATH), F32),
            V((128, PATH), BF16),
            V((PATH, SPAN), BF16),
            V((PAD, PAD), BF16),
            V((128, PAD), BF16),
            V((NLEAF, LEAF, LEAF), F32),
            V((NLEAF, LEAF, LEAF), F32),
            V((64, SPAN), F32),
            V((256, PAD), BF16),
            S((2 * NLEAF + 2,)),
        ],
        1,
        far=4,
    )
    returned = exchange(returning, S4)
    (sums,) = call(total_kernel, [((DEV * 2, 128), F32)], (returned,), micros=1)
    sums = exchange(sums, 2)
    (solved,) = call(
        unpack_kernel,
        [((64, ROWS), F32)],
        (key, returned),
        [V((PAD, PAD), BF16), V((128, PAD), BF16)],
    )
    return tuple(
        call(
            finish_kernel,
            [((64, 64), F32), ((64, 64), F32), ((64, ROWS), F32)],
            (sums, solved, coupling, block_now, block_before),
            [V((192, 2 * PAD), BF16), V((64, ROWS), F32), V((64, ROWS), F32), S((2,))],
            far=2,
        )
    )


def solution(mesh):
    placed = (
        P(None, AXES),
        P(None, AXES),
        P(),
        P(AXES),
        P(AXES),
        P(AXES, None, None),
        P(AXES, None, None),
        P(AXES, None),
        P(),
        P(),
    )
    return jax.shard_map(
        per_device,
        mesh=mesh,
        in_specs=placed,
        out_specs=(P(), P(), P(None, AXES)),
        check_vma=False,
    )
```

```python
import jax
import jax.numpy as jnp
from jax import lax
from jax.experimental import pallas as pl
from jax.experimental.pallas import tpu as pltpu
from jax.sharding import PartitionSpec as P

F32 = jnp.float32
BF16 = jnp.bfloat16
HIGHEST = lax.Precision.HIGHEST
AXES = ("leaf", "front")
DEV = 128
CAP = 17
ROWS = 2080
PAD = 2176
VEC = 64
LEAF = 256
NLEAF = 8
SPAN = 2048
GROUPS = 16
FRONT = 8
SHARE = 32
LEVELS = 5
PATH = 1280
S1 = 18
S2 = 10
S3 = 5
S4 = 10
MIB = 1024 * 1024


def nn(a, b):
    return lax.dot_general(a, b, (((1,), (0,)), ((), ())), preferred_element_type=F32)


def nt(a, b):
    return lax.dot_general(a, b, (((1,), (1,)), ((), ())), preferred_element_type=F32)


def tn(a, b):
    return lax.dot_general(a, b, (((0,), (0,)), ((), ())), preferred_element_type=F32)


def nn32(a, b):
    return lax.dot_general(
        a, b, (((1,), (0,)), ((), ())), preferred_element_type=F32, precision=HIGHEST
    )


def nt32(a, b):
    return lax.dot_general(
        a, b, (((1,), (1,)), ((), ())), preferred_element_type=F32, precision=HIGHEST
    )


def split(x):
    hi = x.astype(BF16)
    lo = (x - hi.astype(F32)).astype(BF16)
    return hi, lo


def iota(shape, dim):
    return lax.broadcasted_iota(jnp.int32, shape, dim)


I16 = jnp.int16


def onehot(mask):
    return jnp.where(mask, jnp.ones((), BF16), jnp.zeros((), BF16))


def onehot32(mask):
    return jnp.where(mask, 1.0, 0.0).astype(BF16)


def mark_row(row, height, start):
    width = row.shape[1]
    wide = jnp.broadcast_to(row, (16, width)).astype(I16)
    wide = jnp.concatenate([wide] * (height // 16), axis=0)
    return onehot(wide == (iota((height, width), 0) + start).astype(I16))


def mark_column(column, width):
    height = column.shape[0]
    wide = jnp.broadcast_to(column, (height, 128)).astype(I16)
    wide = jnp.concatenate([wide] * (width // 128), axis=1)
    return onehot(wide == iota((height, width), 1).astype(I16))


def stacked(x):
    hi, lo = split(x)
    return jnp.concatenate([hi, lo], axis=0)


def both(x):
    return x + pltpu.roll(x, 64, 1)


def folded(x):
    half = x.shape[0] // 2
    return x[0:half] + x[half:]


def fetch(source, target, sem):
    copy = pltpu.make_async_copy(source, target, sem)
    copy.start()
    return copy


def pack_kernel(
    vt_ref, now_hbm, before_hbm, out_ref, key_ref, dest, member, value, mark, now, before, sems
):
    loads = [fetch(now_hbm, now, sems.at[0]), fetch(before_hbm, before, sems.at[1])]
    dest[...] = jnp.full((8, PAD), -1, jnp.int32)
    dest[0:1, 0:ROWS] = vt_ref[...].reshape(1, ROWS)
    target = dest[0:1, :]
    bucket = ((target.astype(F32) + 0.5) * (1.0 / ROWS)).astype(jnp.int32)
    bucket = jnp.where(target < 0, -1, bucket)
    place = target - bucket * ROWS
    member[...] = mark_row(bucket, DEV, 0)
    earlier = onehot32(
        (iota((128, 256), 0) < iota((128, 256), 1)) | (iota((128, 256), 1) >= 128)
    )
    carry = jnp.zeros((DEV, 128), F32)
    ranks = []
    for b in range(CAP):
        part = member[:, b * 128 : (b + 1) * 128]
        counts = nn(part, earlier)
        ranks.append(
            jnp.sum(part.astype(F32) * (counts[:, 0:128] + carry), axis=0, keepdims=True)
        )
        carry = carry + counts[:, 128:256]
    rank = jnp.concatenate(ranks, axis=1).astype(jnp.int32)
    key = jnp.where(target < 0, -1, rank * DEV + bucket)
    for load in loads:
        load.wait()
    value[:, SPAN:PAD] = jnp.zeros((4 * VEC, PAD - SPAN), BF16)
    now_hi, now_lo = split(now[...])
    bef_hi, bef_lo = split(before[...])
    value[0:64, 0:ROWS] = now_hi
    value[64:128, 0:ROWS] = bef_hi
    value[128:192, 0:ROWS] = now_lo
    value[192:256, 0:ROWS] = bef_lo
    key_ref[...] = key
    for k in range(CAP):
        mark[k * DEV : (k + 1) * DEV, :] = mark_row(key, DEV, k * DEV)
    block = nt(mark[...], value[...])
    block = block[:, 0:128] + block[:, 128:256]
    for k in range(CAP):
        out_ref[pl.ds(k, DEV, stride=S1), :] = block[k * DEV : (k + 1) * DEV]
    ranked = jnp.broadcast_to(rank, (32, PAD)) == iota((32, PAD), 0)
    high = place // 64
    marks = jnp.concatenate(
        [
            jnp.where(ranked, jnp.broadcast_to(high, (32, PAD)).astype(F32), 0.0),
            jnp.where(ranked, jnp.broadcast_to(place - high * 64, (32, PAD)).astype(F32), 0.0),
            jnp.zeros((64, PAD), F32),
        ],
        axis=0,
    ).astype(BF16)
    found = nt(member[...], marks)
    where = found * 64.0 + pltpu.roll(found, 96, 1)
    lane = iota((DEV, 128), 1)
    filled = (lane.astype(F32) < carry) & (lane < CAP)
    out_ref[pl.ds(CAP, DEV, stride=S1), :] = jnp.where(filled, where, -1.0)


def forward_kernel(
    home_ref,
    recv_ref,
    rows_ref,
    inv_hbm,
    below_hbm,
    ready_hbm,
    out_ref,
    solved_hbm,
    tree_hbm,
    mark,
    value,
    moved,
    update,
    inv_ref,
    below_ref,
    solved_ref,
    tree_ref,
    sems,
):
    inv_loads = [
        fetch(inv_hbm.at[q], inv_ref.at[q], sems.at[q]) for q in range(NLEAF)
    ]
    below_loads = [
        fetch(below_hbm.at[q], below_ref.at[q], sems.at[NLEAF + q]) for q in range(NLEAF)
    ]
    idx = recv_ref[pl.ds(CAP, DEV, stride=S1), :].astype(jnp.int32)
    for k in range(CAP):
        got = recv_ref[pl.ds(k, DEV, stride=S1), :].T
        value[:, k * DEV : (k + 1) * DEV] = stacked(got[0:64])
        mark[k * DEV : (k + 1) * DEV, :] = mark_column(idx[:, k : k + 1], PAD)
    tree_ref[...] = folded(nn(value[...], mark[...]))
    stores = [fetch(tree_ref, tree_hbm, sems.at[2 * NLEAF])]
    rows = rows_ref[...].astype(F32).T.astype(jnp.int32)
    for load in inv_loads + below_loads:
        load.wait()
    for q in range(NLEAF):
        cols = slice(q * LEAF, (q + 1) * LEAF)
        hi, lo = split(inv_ref[q])
        source = stacked(tree_ref[:, cols])
        solved = folded(nt(source, hi) + nt(source, lo))
        solved_ref[:, cols] = solved
        hi, lo = split(below_ref[q])
        solved = stacked(solved)
        update[:, cols] = stacked(folded(nt(solved, hi) + nt(solved, lo)))
        moved[cols, :] = mark_column(rows[:, q : q + 1], PATH)
    stores.append(fetch(solved_ref, solved_hbm, sems.at[2 * NLEAF + 1]))
    pushed = folded(nn(update[...], moved[...]))
    start = home_ref[0]
    own = pltpu.roll(tree_ref[:, SPAN:PAD], start % 128, 1)
    for j in range(S2):
        chunk = jnp.where(start // 128 == j, own, 0.0) - pushed[:, j * 128 : (j + 1) * 128]
        out_ref[pl.ds(j, DEV, stride=S2), :] = jnp.concatenate([chunk, chunk], axis=0)
    for store in stores:
        store.wait()


def side_kernel(
    recv_ref, tree_hbm, other_hbm, idx_ref, gram_ref, mark, value, tree_ref, other_ref, sems
):
    load = fetch(tree_hbm, tree_ref, sems.at[0])
    where = recv_ref[pl.ds(CAP, DEV, stride=S1), :]
    idx_ref[...] = where.T
    idx = where.astype(jnp.int32)
    for k in range(CAP):
        got = recv_ref[pl.ds(k, DEV, stride=S1), :].T
        value[:, k * DEV : (k + 1) * DEV] = stacked(got[64:128])
        mark[k * DEV : (k + 1) * DEV, :] = mark_column(idx[:, k : k + 1], PAD)
    before = folded(nn(value[...], mark[...]))
    load.wait()
    hi, lo = split(tree_ref[...])
    other_ref[0:64, :] = hi
    other_ref[128:192, :] = lo
    hi, lo = split(before)
    other_ref[64:128, :] = hi
    other_ref[192:256, :] = lo
    store = fetch(other_ref, other_hbm, sems.at[1])
    gram = folded(nt(other_ref[...], other_ref[...]))
    gram_ref[...] = gram[:, 0:128] + gram[:, 128:256]
    store.wait()


def prepare_kernel(
    inv_hbm, parent_hbm, square_hbm, link_hbm, inv_ref, parent_ref, square_ref, link_ref, sems
):
    inv_loads = []
    parent_loads = []
    stores = []
    for s in range(GROUPS):
        inv_loads.append(fetch(inv_hbm.at[s], inv_ref.at[s], sems.at[s]))
        if s > 0:
            at = s - 1
            parent_loads.append(
                fetch(parent_hbm.at[at], parent_ref.at[at], sems.at[GROUPS + at])
            )
    for first in (0, GROUPS // 2):
        for s in range(first, first + GROUPS // 2):
            inv_loads[s].wait()
            if s > 0:
                parent_loads[s - 1].wait()
        for s in range(first, first + GROUPS // 2):
            hi, lo = split(inv_ref[s])
            square_ref[s] = tn(hi, hi) + (tn(hi, lo) + tn(lo, hi))
            if s > 0:
                up, down = split(parent_ref[s - 1])
                link_ref[s - 1] = nn(up, hi) + (nn(up, lo) + nn(down, hi))
        for s in range(first, first + GROUPS // 2):
            stores.append(fetch(square_ref.at[s], square_hbm.at[s], sems.at[2 * GROUPS + s]))
            if s > 0:
                at = s - 1
                stores.append(fetch(link_ref.at[at], link_hbm.at[at], sems.at[3 * GROUPS + at]))
    for store in stores:
        store.wait()


def to_row(column, eye):
    top = jnp.sum(jnp.where(eye, column[0:128], 0.0), axis=0, keepdims=True)
    bottom = jnp.sum(jnp.where(eye, column[128:256], 0.0), axis=0, keepdims=True)
    return jnp.concatenate([top, bottom], axis=1)


def to_column(row, eye):
    top = jnp.sum(jnp.where(eye, row[:, 0:128], 0.0), axis=1, keepdims=True)
    bottom = jnp.sum(jnp.where(eye, row[:, 128:256], 0.0), axis=1, keepdims=True)
    return jnp.concatenate([top, bottom], axis=0)


def apply(matrix, row, eye):
    product = matrix * row
    return to_row(jnp.sum(product[:, 0:128] + product[:, 128:256], axis=1, keepdims=True), eye)


def apply_t(matrix, row, eye):
    return jnp.sum(matrix * to_column(row, eye), axis=0, keepdims=True)


def separator_kernel(
    half_ref, recv_ref, square_hbm, link_hbm, out_ref, square_ref, link_ref, sems
):
    loads = {}
    for at in range(GROUPS - 2, -1, -1):
        loads[at] = fetch(link_hbm.at[at], link_ref.at[at], sems.at[at])
    square_loads = [
        fetch(square_hbm.at[s], square_ref.at[s], sems.at[GROUPS + s]) for s in range(GROUPS)
    ]
    eye = iota((128, 128), 0) == iota((128, 128), 1)
    source = {}
    for height in range(1, LEVELS + 1):
        count = max(GROUPS >> height, 1)
        first = count if height < LEVELS else 0
        span = DEV // count
        left = recv_ref[pl.ds(2 * height - 2, DEV, stride=S2), :]
        right = recv_ref[pl.ds(2 * height - 1, DEV, stride=S2), :]
        for c in range(count):
            at = slice(c * span, (c + 1) * span)
            source[first + c] = jnp.concatenate(
                [
                    jnp.sum(left[at], axis=0, keepdims=True),
                    jnp.sum(right[at], axis=0, keepdims=True),
                ],
                axis=1,
            )
    for height in range(2, LEVELS + 1):
        count = max(GROUPS >> height, 1)
        first = count if height < LEVELS else 0
        if height == 2:
            for at in range(7, 15):
                loads[at].wait()
        if height == 3:
            for at in range(7):
                loads[at].wait()
        for s in range(first, first + count):
            for c in (1,) if s == 0 else (2 * s, 2 * s + 1):
                source[s] = source[s] - apply(link_ref[c - 1], source[c], eye)
    for load in square_loads:
        load.wait()
    back = {}
    for s in range(GROUPS):
        back[s] = apply_t(square_ref[s], source[s], eye)
        if s > 0:
            back[s] = back[s] - apply_t(link_ref[s - 1], back[s // 2], eye)
    upper = half_ref[0] == 1
    for jj in range(S3):
        lines = []
        for g in range(GROUPS):
            ends = []
            for j in (jj, S3 + jj):
                s = (GROUPS + g) >> (j // 2 + 1)
                ends.append(back[s][:, (j % 2) * 128 : (j % 2) * 128 + 128])
            line = jnp.where(upper, ends[1], ends[0])
            lines.append(jnp.broadcast_to(line, (FRONT, 128)))
        out_ref[pl.ds(jj, DEV, stride=S3), :] = jnp.concatenate(lines, axis=0)


def backward_kernel(
    home_ref,
    recv_ref,
    rows_ref,
    idx_ref,
    gram_ref,
    inv_hbm,
    below_hbm,
    solved_hbm,
    other_hbm,
    out_ref,
    known,
    parts,
    moved,
    mark,
    result,
    inv_ref,
    below_ref,
    solved_ref,
    other_ref,
    sems,
):
    loads = [fetch(solved_hbm, solved_ref, sems.at[2 * NLEAF])]
    below_loads = []
    inv_loads = []
    for q in range(NLEAF):
        below_loads.append(fetch(below_hbm.at[q], below_ref.at[q], sems.at[q]))
        inv_loads.append(fetch(inv_hbm.at[q], inv_ref.at[q], sems.at[NLEAF + q]))
    loads.append(fetch(other_hbm, other_ref, sems.at[2 * NLEAF + 1]))
    for q in range(NLEAF):
        moved[:, q * LEAF : (q + 1) * LEAF] = mark_row(rows_ref[q : q + 1, :], PATH, 0)
    for h in range(2):
        for jj in range(S3):
            j = h * S3 + jj
            chunk = recv_ref[pl.ds(h * 64 * S3 + jj, 64, stride=S3), :]
            known[:, j * 128 : (j + 1) * 128] = chunk
            parts[:, j * 128 : (j + 1) * 128] = stacked(chunk)
    picked = folded(nn(parts[...], moved[...]))
    for load in loads + below_loads + inv_loads:
        load.wait()
    start = home_ref[0]
    tile = pl.multiple_of((start // 128) * 128, 128)
    home = pltpu.roll(known[:, pl.ds(tile, 128)], (128 - start % 128) % 128, 1)
    home = jnp.where(iota((64, 128), 1) < SHARE, home, 0.0)
    result[:, SPAN:PAD] = stacked(home)
    for q in range(NLEAF):
        cols = slice(q * LEAF, (q + 1) * LEAF)
        hi, lo = split(below_ref[q])
        rows = stacked(picked[:, cols])
        source = stacked(solved_ref[:, cols] - folded(nn(rows, hi) + nn(rows, lo)))
        hi, lo = split(inv_ref[q])
        result[:, cols] = stacked(folded(nn(source, hi) + nn(source, lo)))
    cross = folded(nt(result[...], other_ref[...]))
    cross = cross[:, 0:128] + cross[:, 128:256]
    square = both(folded(nt(result[...], result[...])))
    slots = idx_ref[...].astype(jnp.int32)
    for k in range(CAP):
        mark[:, k * DEV : (k + 1) * DEV] = mark_row(slots[k : k + 1, :], PAD, 0)
    packed = folded(nn(result[...], mark[...]))
    for j in range(8):
        pair = [packed[:, k * DEV : (k + 1) * DEV] for k in (2 * j, 2 * j + 1)]
        out_ref[pl.ds(j, DEV, stride=S4), :] = jnp.concatenate(pair, axis=0).T
    last = packed[:, 16 * DEV : 17 * DEV]
    last = jnp.concatenate([last, last], axis=0).T
    late = jnp.concatenate([square, gram_ref[64:128, :]], axis=0)
    out_ref[pl.ds(8, DEV, stride=S4), :] = jnp.where(iota((DEV, 128), 1) < 64, last, late)
    out_ref[pl.ds(9, DEV, stride=S4), :] = jnp.concatenate([cross, gram_ref[0:64, :]], axis=0)


def total_kernel(recv_ref, out_ref):
    first = jnp.sum(recv_ref[pl.ds(9, DEV, stride=S4), :], axis=0, keepdims=True)
    second = jnp.sum(recv_ref[pl.ds(8, DEV, stride=S4), :], axis=0, keepdims=True)
    out_ref[pl.ds(0, DEV, stride=2), :] = jnp.broadcast_to(first, (DEV, 128))
    out_ref[pl.ds(1, DEV, stride=2), :] = jnp.broadcast_to(second, (DEV, 128))


def unpack_kernel(key_ref, recv_ref, out_ref, mark, value):
    for k in range(CAP):
        mark[k * DEV : (k + 1) * DEV, :] = mark_row(key_ref[...], DEV, k * DEV)
    for j in range(9):
        got = recv_ref[pl.ds(j, DEV, stride=S4), :].T
        value[:, 2 * j * DEV : (2 * j + 1) * DEV] = stacked(got[0:64])
        if j < 8:
            value[:, (2 * j + 1) * DEV : (2 * j + 2) * DEV] = stacked(got[64:128])
    out_ref[...] = folded(nn(value[...], mark[...]))[:, 0:ROWS]


def finish_kernel(
    recv_ref,
    solved_ref,
    coupling_ref,
    now_hbm,
    before_hbm,
    proj_ref,
    factor_ref,
    next_ref,
    value,
    now_ref,
    before_ref,
    sems,
):
    loads = [fetch(now_hbm, now_ref, sems.at[0]), fetch(before_hbm, before_ref, sems.at[1])]
    first = recv_ref[pl.ds(0, DEV, stride=2), :]
    second = recv_ref[pl.ds(1, DEV, stride=2), :]
    count = 1.0 / (ROWS * DEV)
    s_b = first[0:64, 0:64] * count
    s_a = first[0:64, 64:128] * count
    b_b = first[64:128, 0:64] * count
    b_a = first[64:128, 64:128] * count
    s_s = second[0:64, 64:128] * count
    a_a = second[64:128, 64:128] * count
    coupling = coupling_ref[...]
    proj_ref[...] = s_b.T
    line_s = s_s - nt32(s_b, s_b) - nt32(coupling, s_a)
    line_b = s_b - nn32(s_b, b_b) - nt32(coupling, b_a)
    line_a = s_a - nn32(s_b, b_a) - nn32(coupling, a_a)
    gram = line_s - nt32(line_b, s_b) - nt32(line_a, coupling)
    eye = iota((64, 64), 0) == iota((64, 64), 1)
    work = jnp.concatenate([gram, jnp.where(eye, 1.0, 0.0)], axis=1)
    done = []
    for b in range(8):
        height = 64 - 8 * b
        at = 8 * b
        columns = [
            jnp.broadcast_to(work[:, at + c : at + c + 1], (height, 128)) for c in range(8)
        ]
        below = iota((height, 128), 0)
        for c in range(8):
            ratio = jnp.where(below > c, columns[c] * (1.0 / columns[c][c : c + 1, :]), 0.0)
            work = work - ratio * work[c : c + 1, :]
            for e in range(c + 1, 8):
                columns[e] = columns[e] - ratio * columns[e][c : c + 1, :]
        done.append(work[0:8])
        work = work[8:]
    work = jnp.concatenate(done, axis=0)
    scale = lax.rsqrt(jnp.sum(jnp.where(eye, work[:, 0:64], 0.0), axis=1, keepdims=True))
    work = work * scale
    factor_ref[...] = jnp.where(iota((64, 64), 0) <= iota((64, 64), 1), work[:, 0:64], 0.0)
    inverse = work[:, 64:128]
    weight = jnp.concatenate(
        [inverse, -nn32(inverse, s_b), -nn32(inverse, coupling)], axis=1
    )
    hi, lo = split(weight)
    weight = jnp.concatenate([hi, lo], axis=0)
    for load in loads:
        load.wait()
    for b, ref in enumerate((solved_ref, now_ref, before_ref)):
        hi, lo = split(ref[...])
        value[b * 64 : (b + 1) * 64, 0:ROWS] = hi
        value[b * 64 : (b + 1) * 64, PAD : PAD + ROWS] = lo
    high = nn(weight, value[:, 0:ROWS])
    low = nn(weight, value[:, PAD : PAD + ROWS])
    total = high + low
    next_ref[...] = total[0:64] + total[64:128]


def vmem(count):
    return [pl.BlockSpec(memory_space=pltpu.VMEM)] * count


def call(kernel, outs, operands, scratch=(), scalars=0, far=0, far_outs=(), limit=52, micros=4):
    kinds = [pltpu.SMEM] * scalars + [pltpu.VMEM] * (len(operands) - scalars - far)
    kinds += [pltpu.HBM] * far
    return pl.pallas_call(
        kernel,
        out_shape=[jax.ShapeDtypeStruct(shape, dtype) for shape, dtype in outs],
        in_specs=[pl.BlockSpec(memory_space=kind) for kind in kinds],
        out_specs=[
            pl.BlockSpec(memory_space=pltpu.HBM if i in far_outs else pltpu.VMEM)
            for i in range(len(outs))
        ],
        scratch_shapes=list(scratch),
        cost_estimate=pl.CostEstimate(
            flops=micros * 1000000000, bytes_accessed=micros * 3000000, transcendentals=0
        ),
        compiler_params=pltpu.CompilerParams(vmem_limit_bytes=limit * MIB),
    )(*operands)


def exchange(x, lines):
    return lax.all_to_all(
        x.reshape(DEV, 1, lines * 128), AXES, split_axis=0, concat_axis=0, tiled=True
    ).reshape(DEV * lines, 128)


def per_device(
    block_now,
    block_before,
    coupling,
    vertex_to_tree,
    tree_to_vertex,
    leaf_inverse,
    leaf_below,
    leaf_rows,
    sep_inverse,
    sep_parent,
):
    my_group = lax.axis_index("leaf")
    my_front = lax.axis_index("front")
    home_slot = jnp.zeros((), jnp.int32)
    for bit in range(LEVELS - 1):
        home_slot = home_slot + (my_group % (2 << bit) == 0).astype(jnp.int32)
    home_at = (home_slot * LEAF + my_front * SHARE).astype(jnp.int32).reshape(1)
    half = (my_group // 8).astype(jnp.int32).reshape(1)
    V = pltpu.VMEM
    S = pltpu.SemaphoreType.DMA
    packed, key = call(
        pack_kernel,
        [((DEV * S1, 128), F32), ((1, PAD), jnp.int32)],
        (vertex_to_tree, block_now, block_before),
        [
            V((8, PAD), jnp.int32),
            V((DEV, PAD), BF16),
            V((256, PAD), BF16),
            V((PAD, PAD), BF16),
            V((64, ROWS), F32),
            V((64, ROWS), F32),
            S((2,)),
        ],
        far=2,
        limit=58,
    )
    arrived = exchange(packed, S1)
    square, link = call(
        prepare_kernel,
        [((GROUPS, LEAF, LEAF), F32), ((GROUPS - 1, LEAF, LEAF), F32)],
        (sep_inverse, sep_parent),
        [
            V((GROUPS, LEAF, LEAF), F32),
            V((GROUPS - 1, LEAF, LEAF), F32),
            V((GROUPS, LEAF, LEAF), F32),
            V((GROUPS - 1, LEAF, LEAF), F32),
            S((4 * GROUPS,)),
        ],
        far=2,
        far_outs=(0, 1),
    )
    pushed, leaf_solved, tree = call(
        forward_kernel,
        [((DEV * S2, 128), F32), ((64, SPAN), F32), ((64, PAD), F32)],
        (home_at, arrived, leaf_rows, leaf_inverse, leaf_below, link),
        [
            V((PAD, PAD), BF16),
            V((128, PAD), BF16),
            V((SPAN, PATH), BF16),
            V((128, SPAN), BF16),
            V((NLEAF, LEAF, LEAF), F32),
            V((NLEAF, LEAF, LEAF), F32),
            V((64, SPAN), F32),
            V((64, PAD), F32),
            S((2 * NLEAF + 2,)),
        ],
        1,
        far=3,
        limit=50,
        far_outs=(1, 2),
    )
    pushed = exchange(pushed, S2)
    other, idx, gram = call(
        side_kernel,
        [((256, PAD), BF16), ((128, 128), F32), ((128, 128), F32)],
        (arrived, tree),
        [
            V((PAD, PAD), BF16),
            V((128, PAD), BF16),
            V((64, PAD), F32),
            V((256, PAD), BF16),
            S((2,)),
        ],
        far=1,
        far_outs=(0,),
    )
    (paths,) = call(
        separator_kernel,
        [((DEV * S3, 128), F32)],
        (half, pushed, square, link),
        [
            V((GROUPS, LEAF, LEAF), F32),
            V((GROUPS - 1, LEAF, LEAF), F32),
            S((2 * GROUPS,)),
        ],
        1,
        far=2,
    )
    paths = exchange(paths, S3)
    (returning,) = call(
        backward_kernel,
        [((DEV * S4, 128), F32)],
        (
            home_at,
            paths,
            leaf_rows,
            idx,
            gram,
            leaf_inverse,
            leaf_below,
            leaf_solved,
            other,
        ),
        [
            V((64, PATH), F32),
            V((128, PATH), BF16),
            V((PATH, SPAN), BF16),
            V((PAD, PAD), BF16),
            V((128, PAD), BF16),
            V((NLEAF, LEAF, LEAF), F32),
            V((NLEAF, LEAF, LEAF), F32),
            V((64, SPAN), F32),
            V((256, PAD), BF16),
            S((2 * NLEAF + 2,)),
        ],
        1,
        far=4,
    )
    returned = exchange(returning, S4)
    (sums,) = call(total_kernel, [((DEV * 2, 128), F32)], (returned,), micros=1)
    sums = exchange(sums, 2)
    (solved,) = call(
        unpack_kernel,
        [((64, ROWS), F32)],
        (key, returned),
        [V((PAD, PAD), BF16), V((128, PAD), BF16)],
    )
    return tuple(
        call(
            finish_kernel,
            [((64, 64), F32), ((64, 64), F32), ((64, ROWS), F32)],
            (sums, solved, coupling, block_now, block_before),
            [V((192, 2 * PAD), BF16), V((64, ROWS), F32), V((64, ROWS), F32), S((2,))],
            far=2,
        )
    )


def solution(mesh):
    placed = (
        P(None, AXES),
        P(None, AXES),
        P(),
        P(AXES),
        P(AXES),
        P(AXES, None, None),
        P(AXES, None, None),
        P(AXES, None),
        P(),
        P(),
    )
    return jax.shard_map(
        per_device,
        mesh=mesh,
        in_specs=placed,
        out_specs=(P(), P(), P(None, AXES)),
        check_vma=False,
    )
```

```python
import jax
import jax.numpy as jnp
from jax import lax
from jax.experimental import pallas as pl
from jax.experimental.pallas import tpu as pltpu
from jax.sharding import Mesh
from jax.sharding import PartitionSpec as P

F32 = jnp.float32
BF16 = jnp.bfloat16
HIGHEST = lax.Precision.HIGHEST
AXES = ("half", "group", "front")
NEAR = ("group", "front")
HALF = 64
DEV = 128
CAP = 17
ROWS = 2080
PAD = 2176
VEC = 64
LEAF = 256
NLEAF = 8
SPAN = 2048
GROUPS = 16
FRONT = 8
SHARE = 32
LEVELS = 5
PATH = 1280
S1 = 18
S2 = 10
S3 = 10
S4 = 10
MIB = 1024 * 1024


def nn(a, b):
    return lax.dot_general(a, b, (((1,), (0,)), ((), ())), preferred_element_type=F32)


def nt(a, b):
    return lax.dot_general(a, b, (((1,), (1,)), ((), ())), preferred_element_type=F32)


def tn(a, b):
    return lax.dot_general(a, b, (((0,), (0,)), ((), ())), preferred_element_type=F32)


def nn32(a, b):
    return lax.dot_general(
        a, b, (((1,), (0,)), ((), ())), preferred_element_type=F32, precision=HIGHEST
    )


def nt32(a, b):
    return lax.dot_general(
        a, b, (((1,), (1,)), ((), ())), preferred_element_type=F32, precision=HIGHEST
    )


def split(x):
    hi = x.astype(BF16)
    lo = (x - hi.astype(F32)).astype(BF16)
    return hi, lo


def iota(shape, dim):
    return lax.broadcasted_iota(jnp.int32, shape, dim)


I16 = jnp.int16


def onehot(mask):
    return jnp.where(mask, jnp.ones((), BF16), jnp.zeros((), BF16))


def onehot32(mask):
    return jnp.where(mask, 1.0, 0.0).astype(BF16)


def mark_row(row, height, start):
    width = row.shape[1]
    wide = jnp.broadcast_to(row, (16, width)).astype(I16)
    wide = jnp.concatenate([wide] * (height // 16), axis=0)
    return onehot(wide == (iota((height, width), 0) + start).astype(I16))


def mark_column(column, width):
    height = column.shape[0]
    wide = jnp.broadcast_to(column, (height, 128)).astype(I16)
    wide = jnp.concatenate([wide] * (width // 128), axis=1)
    return onehot(wide == iota((height, width), 1).astype(I16))


def stacked(x):
    hi, lo = split(x)
    return jnp.concatenate([hi, lo], axis=0)


def both(x):
    return x + pltpu.roll(x, 64, 1)


def folded(x):
    half = x.shape[0] // 2
    return x[0:half] + x[half:]


def fetch(source, target, sem):
    copy = pltpu.make_async_copy(source, target, sem)
    copy.start()
    return copy


def pack_kernel(
    vt_ref, now_hbm, before_hbm, out_ref, key_ref, dest, member, value, mark, now, before, sems
):
    loads = [fetch(now_hbm, now, sems.at[0]), fetch(before_hbm, before, sems.at[1])]
    dest[...] = jnp.full((8, PAD), -1, jnp.int32)
    dest[0:1, 0:ROWS] = vt_ref[...].reshape(1, ROWS)
    target = dest[0:1, :]
    bucket = ((target.astype(F32) + 0.5) * (1.0 / ROWS)).astype(jnp.int32)
    bucket = jnp.where(target < 0, -1, bucket)
    place = target - bucket * ROWS
    member[...] = mark_row(bucket, DEV, 0)
    earlier = onehot32(
        (iota((128, 256), 0) < iota((128, 256), 1)) | (iota((128, 256), 1) >= 128)
    )
    carry = jnp.zeros((DEV, 128), F32)
    ranks = []
    for b in range(CAP):
        part = member[:, b * 128 : (b + 1) * 128]
        counts = nn(part, earlier)
        ranks.append(
            jnp.sum(part.astype(F32) * (counts[:, 0:128] + carry), axis=0, keepdims=True)
        )
        carry = carry + counts[:, 128:256]
    rank = jnp.concatenate(ranks, axis=1).astype(jnp.int32)
    key = jnp.where(target < 0, -1, rank * DEV + bucket)
    for load in loads:
        load.wait()
    value[:, SPAN:PAD] = jnp.zeros((4 * VEC, PAD - SPAN), BF16)
    now_hi, now_lo = split(now[...])
    bef_hi, bef_lo = split(before[...])
    value[0:64, 0:ROWS] = now_hi
    value[64:128, 0:ROWS] = bef_hi
    value[128:192, 0:ROWS] = now_lo
    value[192:256, 0:ROWS] = bef_lo
    key_ref[...] = key
    for k in range(CAP):
        mark[k * DEV : (k + 1) * DEV, :] = mark_row(key, DEV, k * DEV)
    block = nt(mark[...], value[...])
    block = block[:, 0:128] + block[:, 128:256]
    for k in range(CAP):
        out_ref[pl.ds(k, DEV, stride=S1), :] = block[k * DEV : (k + 1) * DEV]
    ranked = jnp.broadcast_to(rank, (32, PAD)) == iota((32, PAD), 0)
    high = place // 64
    marks = jnp.concatenate(
        [
            jnp.where(ranked, jnp.broadcast_to(high, (32, PAD)).astype(F32), 0.0),
            jnp.where(ranked, jnp.broadcast_to(place - high * 64, (32, PAD)).astype(F32), 0.0),
            jnp.zeros((64, PAD), F32),
        ],
        axis=0,
    ).astype(BF16)
    found = nt(member[...], marks)
    where = found * 64.0 + pltpu.roll(found, 96, 1)
    lane = iota((DEV, 128), 1)
    filled = (lane.astype(F32) < carry) & (lane < CAP)
    out_ref[pl.ds(CAP, DEV, stride=S1), :] = jnp.where(filled, where, -1.0)


def forward_kernel(
    home_ref,
    recv_ref,
    rows_ref,
    inv_hbm,
    below_hbm,
    ready_hbm,
    out_ref,
    solved_hbm,
    tree_hbm,
    mark,
    value,
    moved,
    update,
    inv_ref,
    below_ref,
    solved_ref,
    tree_ref,
    sems,
):
    inv_loads = [
        fetch(inv_hbm.at[q], inv_ref.at[q], sems.at[q]) for q in range(NLEAF)
    ]
    below_loads = [
        fetch(below_hbm.at[q], below_ref.at[q], sems.at[NLEAF + q]) for q in range(NLEAF)
    ]
    idx = recv_ref[pl.ds(CAP, DEV, stride=S1), :].astype(jnp.int32)
    for k in range(CAP):
        got = recv_ref[pl.ds(k, DEV, stride=S1), :].T
        value[:, k * DEV : (k + 1) * DEV] = stacked(got[0:64])
        mark[k * DEV : (k + 1) * DEV, :] = mark_column(idx[:, k : k + 1], PAD)
    tree_ref[...] = folded(nn(value[...], mark[...]))
    stores = [fetch(tree_ref, tree_hbm, sems.at[2 * NLEAF])]
    rows = rows_ref[...].astype(F32).T.astype(jnp.int32)
    for q in range(NLEAF):
        moved[q * LEAF : (q + 1) * LEAF, :] = mark_column(rows[:, q : q + 1], PATH)
    for load in inv_loads + below_loads:
        load.wait()
    for q in range(NLEAF):
        cols = slice(q * LEAF, (q + 1) * LEAF)
        hi, lo = split(inv_ref[q])
        source = stacked(tree_ref[:, cols])
        solved = folded(nt(source, hi) + nt(source, lo))
        solved_ref[:, cols] = solved
        hi, lo = split(below_ref[q])
        solved = stacked(solved)
        update[:, cols] = stacked(folded(nt(solved, hi) + nt(solved, lo)))
    stores.append(fetch(solved_ref, solved_hbm, sems.at[2 * NLEAF + 1]))
    pushed = folded(nn(update[...], moved[...]))
    start = home_ref[0]
    own = pltpu.roll(tree_ref[:, SPAN:PAD], start % 128, 1)
    for j in range(S2):
        chunk = jnp.where(start // 128 == j, own, 0.0) - pushed[:, j * 128 : (j + 1) * 128]
        out_ref[pl.ds(j, HALF, stride=S2), :] = chunk
    for store in stores:
        store.wait()


def side_kernel(
    recv_ref, tree_hbm, other_hbm, idx_ref, gram_ref, mark, value, tree_ref, other_ref, sems
):
    load = fetch(tree_hbm, tree_ref, sems.at[0])
    where = recv_ref[pl.ds(CAP, DEV, stride=S1), :]
    idx_ref[...] = where.T
    idx = where.astype(jnp.int32)
    for k in range(CAP):
        got = recv_ref[pl.ds(k, DEV, stride=S1), :].T
        value[:, k * DEV : (k + 1) * DEV] = stacked(got[64:128])
        mark[k * DEV : (k + 1) * DEV, :] = mark_column(idx[:, k : k + 1], PAD)
    before = folded(nn(value[...], mark[...]))
    load.wait()
    hi, lo = split(tree_ref[...])
    other_ref[0:64, :] = hi
    other_ref[128:192, :] = lo
    hi, lo = split(before)
    other_ref[64:128, :] = hi
    other_ref[192:256, :] = lo
    store = fetch(other_ref, other_hbm, sems.at[1])
    gram = folded(nt(other_ref[...], other_ref[...]))
    gram_ref[...] = gram[:, 0:128] + gram[:, 128:256]
    store.wait()


def prepare_kernel(
    inv_hbm, parent_hbm, square_hbm, link_hbm, inv_ref, parent_ref, square_ref, link_ref, sems
):
    inv_loads = []
    parent_loads = []
    stores = []
    for s in range(GROUPS):
        inv_loads.append(fetch(inv_hbm.at[s], inv_ref.at[s], sems.at[s]))
        if s > 0:
            at = s - 1
            parent_loads.append(
                fetch(parent_hbm.at[at], parent_ref.at[at], sems.at[GROUPS + at])
            )
    for first in (0, GROUPS // 2):
        for s in range(first, first + GROUPS // 2):
            inv_loads[s].wait()
            if s > 0:
                parent_loads[s - 1].wait()
        for s in range(first, first + GROUPS // 2):
            hi, lo = split(inv_ref[s])
            square_ref[s] = tn(hi, hi) + (tn(hi, lo) + tn(lo, hi))
            if s > 0:
                up, down = split(parent_ref[s - 1])
                link_ref[s - 1] = nn(up, hi) + (nn(up, lo) + nn(down, hi))
        for s in range(first, first + GROUPS // 2):
            stores.append(fetch(square_ref.at[s], square_hbm.at[s], sems.at[2 * GROUPS + s]))
            if s > 0:
                at = s - 1
                stores.append(fetch(link_ref.at[at], link_hbm.at[at], sems.at[3 * GROUPS + at]))
    for store in stores:
        store.wait()


def to_row(column, eye):
    top = jnp.sum(jnp.where(eye, column[0:128], 0.0), axis=0, keepdims=True)
    bottom = jnp.sum(jnp.where(eye, column[128:256], 0.0), axis=0, keepdims=True)
    return jnp.concatenate([top, bottom], axis=1)


def to_column(row, eye):
    top = jnp.sum(jnp.where(eye, row[:, 0:128], 0.0), axis=1, keepdims=True)
    bottom = jnp.sum(jnp.where(eye, row[:, 128:256], 0.0), axis=1, keepdims=True)
    return jnp.concatenate([top, bottom], axis=0)


def apply(matrix, row, eye):
    product = matrix * row
    return to_row(jnp.sum(product[:, 0:128] + product[:, 128:256], axis=1, keepdims=True), eye)


def apply_t(matrix, row, eye):
    return jnp.sum(matrix * to_column(row, eye), axis=0, keepdims=True)


def local_links(half):
    return [7 + 4 * half + c for c in range(4)] + [3 + 2 * half + c for c in range(2)] + [1 + half]


def up_kernel(half_ref, recv_ref, link_hbm, ready_hbm, top_ref, source_ref, link_ref, sems):
    half = half_ref[0]
    loads = [
        fetch(link_hbm.at[at], link_ref.at[i], sems.at[i])
        for i, at in enumerate(local_links(half))
    ]
    eye = iota((128, 128), 0) == iota((128, 128), 1)
    sums = []
    for height in range(1, LEVELS + 1):
        count = max(8 >> height, 1)
        span = HALF // count
        left = recv_ref[pl.ds(2 * height - 2, HALF, stride=S2), :]
        right = recv_ref[pl.ds(2 * height - 1, HALF, stride=S2), :]
        for c in range(count):
            at = slice(c * span, (c + 1) * span)
            ends = [jnp.sum(part[at], axis=0, keepdims=True) for part in (left, right)]
            sums.append(jnp.concatenate(ends, axis=1))
    for load in loads:
        load.wait()
    for i in range(7):
        to = 4 + i // 2 if i < 4 else (6 if i < 6 else 7)
        sums[to] = sums[to] - apply(link_ref[i], sums[i], eye)
    top_ref[...] = jnp.concatenate(sums[7:9] + [jnp.zeros((6, LEAF), F32)], axis=0)
    source_ref[...] = jnp.concatenate(sums[0:7] + [jnp.zeros((1, LEAF), F32)], axis=0)


def square_kernel(half_ref, source_ref, square_hbm, out_ref, square_ref, sems):
    half = half_ref[0]
    loads = [
        fetch(square_hbm.at[at + 1], square_ref.at[i], sems.at[i])
        for i, at in enumerate(local_links(half))
    ]
    eye = iota((128, 128), 0) == iota((128, 128), 1)
    for load in loads:
        load.wait()
    lines = [apply_t(square_ref[i], source_ref[i : i + 1, :], eye) for i in range(7)]
    out_ref[...] = jnp.concatenate(lines + [jnp.zeros((1, LEAF), F32)], axis=0)


def down_kernel(
    half_ref,
    top_ref,
    other_ref,
    line_ref,
    square_hbm,
    link_hbm,
    out_ref,
    square_ref,
    link_ref,
    sems,
):
    half = half_ref[0]
    first = [
        fetch(link_hbm.at[0], link_ref.at[7], sems.at[7]),
        fetch(square_hbm.at[0], square_ref.at[0], sems.at[8]),
        fetch(square_hbm.at[1], square_ref.at[1], sems.at[9]),
    ]
    links = local_links(half)
    loads = [fetch(link_hbm.at[links[i]], link_ref.at[i], sems.at[i]) for i in range(6, -1, -1)]
    eye = iota((128, 128), 0) == iota((128, 128), 1)
    total = top_ref[...] + other_ref[...]
    below = total[0:1]
    for load in first:
        load.wait()
    root = total[1:2] - apply(link_ref[7], below, eye)
    root = apply_t(square_ref[0], root, eye)
    below = apply_t(square_ref[1], below, eye) - apply_t(link_ref[7], root, eye)
    for load in loads:
        load.wait()
    line = line_ref[...]
    third = line[6:7] - apply_t(link_ref[6], below, eye)
    second = [line[4 + c : 5 + c] - apply_t(link_ref[4 + c], third, eye) for c in range(2)]
    lowest = [line[c : c + 1] - apply_t(link_ref[c], second[c // 2], eye) for c in range(4)]
    for j in range(S3):
        lines = []
        for g in range(8):
            value = (lowest[g // 2], second[g // 4], third, below, root)[j // 2]
            value = value[:, (j % 2) * 128 : (j % 2) * 128 + 128]
            lines.append(jnp.broadcast_to(value, (FRONT, 128)))
        out_ref[pl.ds(j, HALF, stride=S3), :] = jnp.concatenate(lines, axis=0)


def backward_kernel(
    home_ref,
    recv_ref,
    rows_ref,
    idx_ref,
    gram_ref,
    inv_hbm,
    below_hbm,
    solved_hbm,
    other_hbm,
    out_ref,
    known,
    parts,
    moved,
    mark,
    result,
    inv_ref,
    below_ref,
    solved_ref,
    other_ref,
    sems,
):
    loads = [fetch(solved_hbm, solved_ref, sems.at[2 * NLEAF])]
    below_loads = []
    inv_loads = []
    for q in range(NLEAF):
        below_loads.append(fetch(below_hbm.at[q], below_ref.at[q], sems.at[q]))
        inv_loads.append(fetch(inv_hbm.at[q], inv_ref.at[q], sems.at[NLEAF + q]))
    loads.append(fetch(other_hbm, other_ref, sems.at[2 * NLEAF + 1]))
    for q in range(NLEAF):
        moved[:, q * LEAF : (q + 1) * LEAF] = mark_row(rows_ref[q : q + 1, :], PATH, 0)
    for j in range(S3):
        chunk = recv_ref[pl.ds(j, HALF, stride=S3), :]
        known[:, j * 128 : (j + 1) * 128] = chunk
        parts[:, j * 128 : (j + 1) * 128] = stacked(chunk)
    picked = folded(nn(parts[...], moved[...]))
    slots = idx_ref[...].astype(jnp.int32)
    for k in range(CAP):
        mark[:, k * DEV : (k + 1) * DEV] = mark_row(slots[k : k + 1, :], PAD, 0)
    for load in loads + below_loads + inv_loads:
        load.wait()
    start = home_ref[0]
    tile = pl.multiple_of((start // 128) * 128, 128)
    home = pltpu.roll(known[:, pl.ds(tile, 128)], (128 - start % 128) % 128, 1)
    home = jnp.where(iota((64, 128), 1) < SHARE, home, 0.0)
    result[:, SPAN:PAD] = stacked(home)
    for q in range(NLEAF):
        cols = slice(q * LEAF, (q + 1) * LEAF)
        hi, lo = split(below_ref[q])
        rows = stacked(picked[:, cols])
        source = stacked(solved_ref[:, cols] - folded(nn(rows, hi) + nn(rows, lo)))
        hi, lo = split(inv_ref[q])
        result[:, cols] = stacked(folded(nn(source, hi) + nn(source, lo)))
    cross = folded(nt(result[...], other_ref[...]))
    cross = cross[:, 0:128] + cross[:, 128:256]
    square = both(folded(nt(result[...], result[...])))
    packed = folded(nn(result[...], mark[...]))
    for j in range(8):
        pair = [packed[:, k * DEV : (k + 1) * DEV] for k in (2 * j, 2 * j + 1)]
        out_ref[pl.ds(j, DEV, stride=S4), :] = jnp.concatenate(pair, axis=0).T
    last = packed[:, 16 * DEV : 17 * DEV]
    last = jnp.concatenate([last, last], axis=0).T
    late = jnp.concatenate([square, gram_ref[64:128, :]], axis=0)
    out_ref[pl.ds(8, DEV, stride=S4), :] = jnp.where(iota((DEV, 128), 1) < 64, last, late)
    out_ref[pl.ds(9, DEV, stride=S4), :] = jnp.concatenate([cross, gram_ref[0:64, :]], axis=0)


def total_kernel(recv_ref, out_ref):
    first = jnp.sum(recv_ref[pl.ds(9, DEV, stride=S4), :], axis=0, keepdims=True)
    second = jnp.sum(recv_ref[pl.ds(8, DEV, stride=S4), :], axis=0, keepdims=True)
    out_ref[pl.ds(0, DEV, stride=2), :] = jnp.broadcast_to(first, (DEV, 128))
    out_ref[pl.ds(1, DEV, stride=2), :] = jnp.broadcast_to(second, (DEV, 128))


def unpack_kernel(key_ref, recv_ref, out_ref, mark, value):
    for k in range(CAP):
        mark[k * DEV : (k + 1) * DEV, :] = mark_row(key_ref[...], DEV, k * DEV)
    for j in range(9):
        got = recv_ref[pl.ds(j, DEV, stride=S4), :].T
        value[:, 2 * j * DEV : (2 * j + 1) * DEV] = stacked(got[0:64])
        if j < 8:
            value[:, (2 * j + 1) * DEV : (2 * j + 2) * DEV] = stacked(got[64:128])
    out_ref[...] = folded(nn(value[...], mark[...]))[:, 0:ROWS]


def finish_kernel(
    recv_ref,
    solved_ref,
    coupling_ref,
    now_hbm,
    before_hbm,
    proj_ref,
    factor_ref,
    next_ref,
    value,
    now_ref,
    before_ref,
    sems,
):
    loads = [fetch(now_hbm, now_ref, sems.at[0]), fetch(before_hbm, before_ref, sems.at[1])]
    first = recv_ref[pl.ds(0, DEV, stride=2), :]
    second = recv_ref[pl.ds(1, DEV, stride=2), :]
    count = 1.0 / (ROWS * DEV)
    s_b = first[0:64, 0:64] * count
    s_a = first[0:64, 64:128] * count
    b_b = first[64:128, 0:64] * count
    b_a = first[64:128, 64:128] * count
    s_s = second[0:64, 64:128] * count
    a_a = second[64:128, 64:128] * count
    coupling = coupling_ref[...]
    proj_ref[...] = s_b.T
    line_s = s_s - nt32(s_b, s_b) - nt32(coupling, s_a)
    line_b = s_b - nn32(s_b, b_b) - nt32(coupling, b_a)
    line_a = s_a - nn32(s_b, b_a) - nn32(coupling, a_a)
    gram = line_s - nt32(line_b, s_b) - nt32(line_a, coupling)
    eye = iota((64, 64), 0) == iota((64, 64), 1)
    work = jnp.concatenate([gram, jnp.where(eye, 1.0, 0.0)], axis=1)
    done = []
    for b in range(8):
        height = 64 - 8 * b
        at = 8 * b
        columns = [
            jnp.broadcast_to(work[:, at + c : at + c + 1], (height, 128)) for c in range(8)
        ]
        below = iota((height, 128), 0)
        for c in range(8):
            ratio = jnp.where(below > c, columns[c] * (1.0 / columns[c][c : c + 1, :]), 0.0)
            work = work - ratio * work[c : c + 1, :]
            for e in range(c + 1, 8):
                columns[e] = columns[e] - ratio * columns[e][c : c + 1, :]
        done.append(work[0:8])
        work = work[8:]
    work = jnp.concatenate(done, axis=0)
    scale = lax.rsqrt(jnp.sum(jnp.where(eye, work[:, 0:64], 0.0), axis=1, keepdims=True))
    work = work * scale
    factor_ref[...] = jnp.where(iota((64, 64), 0) <= iota((64, 64), 1), work[:, 0:64], 0.0)
    inverse = work[:, 64:128]
    weight = jnp.concatenate(
        [inverse, -nn32(inverse, s_b), -nn32(inverse, coupling)], axis=1
    )
    hi, lo = split(weight)
    weight = jnp.concatenate([hi, lo], axis=0)
    for load in loads:
        load.wait()
    for b, ref in enumerate((solved_ref, now_ref, before_ref)):
        hi, lo = split(ref[...])
        value[b * 64 : (b + 1) * 64, 0:ROWS] = hi
        value[b * 64 : (b + 1) * 64, PAD : PAD + ROWS] = lo
    high = nn(weight, value[:, 0:ROWS])
    low = nn(weight, value[:, PAD : PAD + ROWS])
    total = high + low
    next_ref[...] = total[0:64] + total[64:128]


def vmem(count):
    return [pl.BlockSpec(memory_space=pltpu.VMEM)] * count


def call(kernel, outs, operands, scratch=(), scalars=0, far=0, far_outs=(), limit=52, micros=4):
    kinds = [pltpu.SMEM] * scalars + [pltpu.VMEM] * (len(operands) - scalars - far)
    kinds += [pltpu.HBM] * far
    return pl.pallas_call(
        kernel,
        out_shape=[jax.ShapeDtypeStruct(shape, dtype) for shape, dtype in outs],
        in_specs=[pl.BlockSpec(memory_space=kind) for kind in kinds],
        out_specs=[
            pl.BlockSpec(memory_space=pltpu.HBM if i in far_outs else pltpu.VMEM)
            for i in range(len(outs))
        ],
        scratch_shapes=list(scratch),
        cost_estimate=pl.CostEstimate(
            flops=micros * 1000000000, bytes_accessed=micros * 3000000, transcendentals=0
        ),
        compiler_params=pltpu.CompilerParams(vmem_limit_bytes=limit * MIB),
    )(*operands)


def exchange(x, lines, axes=AXES):
    peers = x.shape[0] // lines
    return lax.all_to_all(
        x.reshape(peers, 1, lines * 128), axes, split_axis=0, concat_axis=0, tiled=True
    ).reshape(peers * lines, 128)


def per_device(
    block_now,
    block_before,
    coupling,
    vertex_to_tree,
    tree_to_vertex,
    leaf_inverse,
    leaf_below,
    leaf_rows,
    sep_inverse,
    sep_parent,
):
    my_half = lax.axis_index("half")
    my_group = my_half * 8 + lax.axis_index("group")
    my_front = lax.axis_index("front")
    home_slot = jnp.zeros((), jnp.int32)
    for bit in range(LEVELS - 1):
        home_slot = home_slot + (my_group % (2 << bit) == 0).astype(jnp.int32)
    home_at = (home_slot * LEAF + my_front * SHARE).astype(jnp.int32).reshape(1)
    half = my_half.astype(jnp.int32).reshape(1)
    V = pltpu.VMEM
    S = pltpu.SemaphoreType.DMA
    packed, key = call(
        pack_kernel,
        [((DEV * S1, 128), F32), ((1, PAD), jnp.int32)],
        (vertex_to_tree, block_now, block_before),
        [
            V((8, PAD), jnp.int32),
            V((DEV, PAD), BF16),
            V((256, PAD), BF16),
            V((PAD, PAD), BF16),
            V((64, ROWS), F32),
            V((64, ROWS), F32),
            S((2,)),
        ],
        far=2,
        limit=58,
    )
    arrived = exchange(packed, S1)
    square, link = call(
        prepare_kernel,
        [((GROUPS, LEAF, LEAF), F32), ((GROUPS - 1, LEAF, LEAF), F32)],
        (sep_inverse, sep_parent),
        [
            V((GROUPS, LEAF, LEAF), F32),
            V((GROUPS - 1, LEAF, LEAF), F32),
            V((GROUPS, LEAF, LEAF), F32),
            V((GROUPS - 1, LEAF, LEAF), F32),
            S((4 * GROUPS,)),
        ],
        far=2,
        far_outs=(0, 1),
    )
    pushed, leaf_solved, tree = call(
        forward_kernel,
        [((HALF * S2, 128), F32), ((64, SPAN), F32), ((64, PAD), F32)],
        (home_at, arrived, leaf_rows, leaf_inverse, leaf_below, link),
        [
            V((PAD, PAD), BF16),
            V((128, PAD), BF16),
            V((SPAN, PATH), BF16),
            V((128, SPAN), BF16),
            V((NLEAF, LEAF, LEAF), F32),
            V((NLEAF, LEAF, LEAF), F32),
            V((64, SPAN), F32),
            V((64, PAD), F32),
            S((2 * NLEAF + 2,)),
        ],
        1,
        far=3,
        limit=50,
        far_outs=(1, 2),
    )
    pushed = exchange(pushed, S2, NEAR)
    other, idx, gram = call(
        side_kernel,
        [((256, PAD), BF16), ((128, 128), F32), ((128, 128), F32)],
        (arrived, tree),
        [
            V((PAD, PAD), BF16),
            V((128, PAD), BF16),
            V((64, PAD), F32),
            V((256, PAD), BF16),
            S((2,)),
        ],
        far=1,
        far_outs=(0,),
    )
    small = ((8, LEAF), F32)
    top, source = call(
        up_kernel,
        [small, small],
        (half, pushed, link, other),
        [V((7, LEAF, LEAF), F32), S((7,))],
        1,
        far=2,
    )
    other_top = lax.ppermute(top, "half", [(0, 1), (1, 0)])
    (line,) = call(
        square_kernel,
        [small],
        (half, source, square),
        [V((7, LEAF, LEAF), F32), S((7,))],
        1,
        far=1,
        micros=2,
    )
    (paths,) = call(
        down_kernel,
        [((HALF * S3, 128), F32)],
        (half, top, other_top, line, square, link),
        [V((2, LEAF, LEAF), F32), V((8, LEAF, LEAF), F32), S((10,))],
        1,
        far=2,
    )
    paths = exchange(paths, S3, NEAR)
    (returning,) = call(
        backward_kernel,
        [((DEV * S4, 128), F32)],
        (
            home_at,
            paths,
            leaf_rows,
            idx,
            gram,
            leaf_inverse,
            leaf_below,
            leaf_solved,
            other,
        ),
        [
            V((64, PATH), F32),
            V((128, PATH), BF16),
            V((PATH, SPAN), BF16),
            V((PAD, PAD), BF16),
            V((128, PAD), BF16),
            V((NLEAF, LEAF, LEAF), F32),
            V((NLEAF, LEAF, LEAF), F32),
            V((64, SPAN), F32),
            V((256, PAD), BF16),
            S((2 * NLEAF + 2,)),
        ],
        1,
        far=4,
    )
    returned = exchange(returning, S4)
    (sums,) = call(total_kernel, [((DEV * 2, 128), F32)], (returned,), micros=1)
    sums = exchange(sums, 2)
    (solved,) = call(
        unpack_kernel,
        [((64, ROWS), F32)],
        (key, returned),
        [V((PAD, PAD), BF16), V((128, PAD), BF16)],
    )
    return tuple(
        call(
            finish_kernel,
            [((64, 64), F32), ((64, 64), F32), ((64, ROWS), F32)],
            (sums, solved, coupling, block_now, block_before),
            [V((192, 2 * PAD), BF16), V((64, ROWS), F32), V((64, ROWS), F32), S((2,))],
            far=2,
        )
    )


def solution(mesh):
    placed = (
        P(None, AXES),
        P(None, AXES),
        P(),
        P(AXES),
        P(AXES),
        P(AXES, None, None),
        P(AXES, None, None),
        P(AXES, None),
        P(),
        P(),
    )
    split_mesh = Mesh(mesh.devices.reshape(2, 8, 8), AXES)
    return jax.shard_map(
        per_device,
        mesh=split_mesh,
        in_specs=placed,
        out_specs=(P(), P(), P(None, AXES)),
        check_vma=False,
    )
```

```python
import jax
import jax.numpy as jnp
from jax import lax
from jax.experimental import pallas as pl
from jax.experimental.pallas import tpu as pltpu
from jax.sharding import Mesh
from jax.sharding import PartitionSpec as P

F32 = jnp.float32
BF16 = jnp.bfloat16
HIGHEST = lax.Precision.HIGHEST
AXES = ("half", "group", "front")
NEAR = ("group", "front")
HALF = 64
DEV = 128
CAP = 17
ROWS = 2080
PAD = 2176
VEC = 64
LEAF = 256
NLEAF = 8
SPAN = 2048
GROUPS = 16
FRONT = 8
SHARE = 32
LEVELS = 5
PATH = 1280
S1 = 18
S2 = 10
S3 = 10
S4 = 10
MIB = 1024 * 1024


def nn(a, b):
    return lax.dot_general(a, b, (((1,), (0,)), ((), ())), preferred_element_type=F32)


def nt(a, b):
    return lax.dot_general(a, b, (((1,), (1,)), ((), ())), preferred_element_type=F32)


def tn(a, b):
    return lax.dot_general(a, b, (((0,), (0,)), ((), ())), preferred_element_type=F32)


def nn32(a, b):
    return lax.dot_general(
        a, b, (((1,), (0,)), ((), ())), preferred_element_type=F32, precision=HIGHEST
    )


def nt32(a, b):
    return lax.dot_general(
        a, b, (((1,), (1,)), ((), ())), preferred_element_type=F32, precision=HIGHEST
    )


def split(x):
    hi = x.astype(BF16)
    lo = (x - hi.astype(F32)).astype(BF16)
    return hi, lo


def iota(shape, dim):
    return lax.broadcasted_iota(jnp.int32, shape, dim)


I16 = jnp.int16


def onehot(mask):
    return jnp.where(mask, jnp.ones((), BF16), jnp.zeros((), BF16))


def onehot32(mask):
    return jnp.where(mask, 1.0, 0.0).astype(BF16)


def mark_row(row, height, start):
    width = row.shape[1]
    wide = jnp.broadcast_to(row, (16, width)).astype(I16)
    wide = jnp.concatenate([wide] * (height // 16), axis=0)
    return onehot(wide == (iota((height, width), 0) + start).astype(I16))


def mark_column(column, width):
    height = column.shape[0]
    wide = jnp.broadcast_to(column, (height, 128)).astype(I16)
    wide = jnp.concatenate([wide] * (width // 128), axis=1)
    return onehot(wide == iota((height, width), 1).astype(I16))


def stacked(x):
    hi, lo = split(x)
    return jnp.concatenate([hi, lo], axis=0)


def both(x):
    return x + pltpu.roll(x, 64, 1)


def crossed(x, half):
    return jnp.where(half == 1, jnp.concatenate([x[32:64], x[0:32]], axis=0), x)


def folded(x):
    half = x.shape[0] // 2
    return x[0:half] + x[half:]


def fetch(source, target, sem):
    copy = pltpu.make_async_copy(source, target, sem)
    copy.start()
    return copy


def pack_kernel(
    vt_ref, now_hbm, before_hbm, out_ref, key_ref, dest, member, value, mark, now, before, sems
):
    loads = [fetch(now_hbm, now, sems.at[0]), fetch(before_hbm, before, sems.at[1])]
    dest[...] = jnp.full((8, PAD), -1, jnp.int32)
    dest[0:1, 0:ROWS] = vt_ref[...].reshape(1, ROWS)
    target = dest[0:1, :]
    bucket = ((target.astype(F32) + 0.5) * (1.0 / ROWS)).astype(jnp.int32)
    bucket = jnp.where(target < 0, -1, bucket)
    place = target - bucket * ROWS
    member[...] = mark_row(bucket, DEV, 0)
    earlier = onehot32(
        (iota((128, 256), 0) < iota((128, 256), 1)) | (iota((128, 256), 1) >= 128)
    )
    carry = jnp.zeros((DEV, 128), F32)
    ranks = []
    for b in range(CAP):
        part = member[:, b * 128 : (b + 1) * 128]
        counts = nn(part, earlier)
        ranks.append(
            jnp.sum(part.astype(F32) * (counts[:, 0:128] + carry), axis=0, keepdims=True)
        )
        carry = carry + counts[:, 128:256]
    rank = jnp.concatenate(ranks, axis=1).astype(jnp.int32)
    key = jnp.where(target < 0, -1, rank * DEV + bucket)
    for k in range(8):
        mark[k * DEV : (k + 1) * DEV, :] = mark_row(key, DEV, k * DEV)
    for load in loads:
        load.wait()
    value[:, SPAN:PAD] = jnp.zeros((4 * VEC, PAD - SPAN), BF16)
    now_hi, now_lo = split(now[...])
    bef_hi, bef_lo = split(before[...])
    value[0:64, 0:ROWS] = now_hi
    value[64:128, 0:ROWS] = bef_hi
    value[128:192, 0:ROWS] = now_lo
    value[192:256, 0:ROWS] = bef_lo
    key_ref[...] = key
    for k in range(8, CAP):
        mark[k * DEV : (k + 1) * DEV, :] = mark_row(key, DEV, k * DEV)
    block = nt(mark[...], value[...])
    block = block[:, 0:128] + block[:, 128:256]
    for k in range(CAP):
        out_ref[pl.ds(k, DEV, stride=S1), :] = block[k * DEV : (k + 1) * DEV]
    ranked = jnp.broadcast_to(rank, (32, PAD)) == iota((32, PAD), 0)
    high = place // 64
    marks = jnp.concatenate(
        [
            jnp.where(ranked, jnp.broadcast_to(high, (32, PAD)).astype(F32), 0.0),
            jnp.where(ranked, jnp.broadcast_to(place - high * 64, (32, PAD)).astype(F32), 0.0),
            jnp.zeros((64, PAD), F32),
        ],
        axis=0,
    ).astype(BF16)
    found = nt(member[...], marks)
    where = found * 64.0 + pltpu.roll(found, 96, 1)
    lane = iota((DEV, 128), 1)
    filled = (lane.astype(F32) < carry) & (lane < CAP)
    out_ref[pl.ds(CAP, DEV, stride=S1), :] = jnp.where(filled, where, -1.0)


def forward_kernel(
    home_ref,
    recv_ref,
    rows_ref,
    inv_hbm,
    below_hbm,
    ready_hbm,
    out_ref,
    solved_hbm,
    tree_hbm,
    mark,
    value,
    moved,
    update,
    inv_ref,
    below_ref,
    solved_ref,
    tree_ref,
    sems,
):
    loads = [fetch(inv_hbm, inv_ref, sems.at[0]), fetch(below_hbm, below_ref, sems.at[1])]
    idx = recv_ref[pl.ds(CAP, DEV, stride=S1), :].astype(jnp.int32)
    for k in range(CAP):
        got = recv_ref[pl.ds(k, DEV, stride=S1), :].T
        value[:, k * DEV : (k + 1) * DEV] = stacked(got[0:64])
        mark[k * DEV : (k + 1) * DEV, :] = mark_column(idx[:, k : k + 1], PAD)
    tree_ref[...] = folded(nn(value[...], mark[...]))
    stores = [fetch(tree_ref, tree_hbm, sems.at[2])]
    rows = rows_ref[...].astype(F32).T.astype(jnp.int32)
    for q in range(NLEAF):
        moved[q * LEAF : (q + 1) * LEAF, :] = mark_column(rows[:, q : q + 1], PATH)
    for load in loads:
        load.wait()
    for q in range(NLEAF):
        cols = slice(q * LEAF, (q + 1) * LEAF)
        hi, lo = split(inv_ref[q])
        source = stacked(tree_ref[:, cols])
        solved = folded(nt(source, hi) + nt(source, lo))
        solved_ref[:, cols] = solved
        hi, lo = split(below_ref[q])
        solved = stacked(solved)
        update[:, cols] = stacked(folded(nt(solved, hi) + nt(solved, lo)))
    stores.append(fetch(solved_ref, solved_hbm, sems.at[3]))
    pushed = folded(nn(update[...], moved[...]))
    start = home_ref[0]
    own = pltpu.roll(tree_ref[:, SPAN:PAD], start % 128, 1)
    for j in range(S2):
        chunk = jnp.where(start // 128 == j, own, 0.0) - pushed[:, j * 128 : (j + 1) * 128]
        out_ref[pl.ds(j, HALF, stride=S2), :] = crossed(chunk, home_ref[1])
    for store in stores:
        store.wait()


def side_kernel(
    recv_ref, tree_hbm, other_hbm, idx_ref, gram_ref, mark, value, tree_ref, other_ref, sems
):
    load = fetch(tree_hbm, tree_ref, sems.at[0])
    where = recv_ref[pl.ds(CAP, DEV, stride=S1), :]
    idx_ref[...] = where.T
    idx = where.astype(jnp.int32)
    for k in range(CAP):
        got = recv_ref[pl.ds(k, DEV, stride=S1), :].T
        value[:, k * DEV : (k + 1) * DEV] = stacked(got[64:128])
        mark[k * DEV : (k + 1) * DEV, :] = mark_column(idx[:, k : k + 1], PAD)
    before = folded(nn(value[...], mark[...]))
    load.wait()
    hi, lo = split(tree_ref[...])
    other_ref[0:64, :] = hi
    other_ref[128:192, :] = lo
    hi, lo = split(before)
    other_ref[64:128, :] = hi
    other_ref[192:256, :] = lo
    store = fetch(other_ref, other_hbm, sems.at[1])
    gram = folded(nt(other_ref[...], other_ref[...]))
    gram_ref[...] = gram[:, 0:128] + gram[:, 128:256]
    store.wait()


def prepare_kernel(
    inv_hbm, parent_hbm, square_hbm, link_hbm, inv_ref, parent_ref, square_ref, link_ref, sems
):
    inv_loads = []
    parent_loads = []
    stores = []
    for s in range(GROUPS):
        inv_loads.append(fetch(inv_hbm.at[s], inv_ref.at[s], sems.at[s]))
        if s > 0:
            at = s - 1
            parent_loads.append(
                fetch(parent_hbm.at[at], parent_ref.at[at], sems.at[GROUPS + at])
            )
    for first in (0, GROUPS // 2):
        for s in range(first, first + GROUPS // 2):
            inv_loads[s].wait()
            if s > 0:
                parent_loads[s - 1].wait()
        for s in range(first, first + GROUPS // 2):
            hi, lo = split(inv_ref[s])
            square_ref[s] = tn(hi, hi) + (tn(hi, lo) + tn(lo, hi))
            if s > 0:
                up, down = split(parent_ref[s - 1])
                link_ref[s - 1] = nn(up, hi) + (nn(up, lo) + nn(down, hi))
        for s in range(first, first + GROUPS // 2):
            stores.append(fetch(square_ref.at[s], square_hbm.at[s], sems.at[2 * GROUPS + s]))
            if s > 0:
                at = s - 1
                stores.append(fetch(link_ref.at[at], link_hbm.at[at], sems.at[3 * GROUPS + at]))
    for store in stores:
        store.wait()


def to_row(column, eye):
    top = jnp.sum(jnp.where(eye, column[0:128], 0.0), axis=0, keepdims=True)
    bottom = jnp.sum(jnp.where(eye, column[128:256], 0.0), axis=0, keepdims=True)
    return jnp.concatenate([top, bottom], axis=1)


def to_column(row, eye):
    top = jnp.sum(jnp.where(eye, row[:, 0:128], 0.0), axis=1, keepdims=True)
    bottom = jnp.sum(jnp.where(eye, row[:, 128:256], 0.0), axis=1, keepdims=True)
    return jnp.concatenate([top, bottom], axis=0)


def apply(matrix, row, eye):
    product = matrix * row
    return to_row(jnp.sum(product[:, 0:128] + product[:, 128:256], axis=1, keepdims=True), eye)


def apply_t(matrix, row, eye):
    return jnp.sum(matrix * to_column(row, eye), axis=0, keepdims=True)


def local_links(half):
    return [7 + 4 * half + c for c in range(4)] + [3 + 2 * half + c for c in range(2)] + [1 + half]


def up_kernel(half_ref, recv_ref, link_hbm, ready_hbm, top_ref, source_ref, link_ref, sems):
    half = half_ref[0]
    loads = [
        fetch(link_hbm.at[at], link_ref.at[i], sems.at[i])
        for i, at in enumerate(local_links(half))
    ]
    eye = iota((128, 128), 0) == iota((128, 128), 1)
    sums = []
    for height in range(1, LEVELS + 1):
        count = max(8 >> height, 1)
        span = HALF // count
        left = recv_ref[pl.ds(2 * height - 2, HALF, stride=S2), :]
        right = recv_ref[pl.ds(2 * height - 1, HALF, stride=S2), :]
        for c in range(count):
            at = slice(c * span, (c + 1) * span)
            ends = [jnp.sum(part[at], axis=0, keepdims=True) for part in (left, right)]
            sums.append(jnp.concatenate(ends, axis=1))
    for load in loads:
        load.wait()
    for i in range(7):
        to = 4 + i // 2 if i < 4 else (6 if i < 6 else 7)
        sums[to] = sums[to] - apply(link_ref[i], sums[i], eye)
    top_ref[...] = jnp.concatenate(sums[7:9] + [jnp.zeros((6, LEAF), F32)], axis=0)
    source_ref[...] = jnp.concatenate(sums[0:7] + [jnp.zeros((1, LEAF), F32)], axis=0)


def square_kernel(
    half_ref, source_ref, square_hbm, link_hbm, out_ref, high_ref, square_ref, sems
):
    half = half_ref[0]
    loads = [
        fetch(square_hbm.at[at + 1], square_ref.at[i], sems.at[i])
        for i, at in enumerate(local_links(half))
    ]
    high = [
        fetch(square_hbm.at[0:2], high_ref.at[0:2], sems.at[7]),
        fetch(link_hbm.at[0], high_ref.at[2], sems.at[8]),
    ]
    eye = iota((128, 128), 0) == iota((128, 128), 1)
    for load in loads:
        load.wait()
    lines = [apply_t(square_ref[i], source_ref[i : i + 1, :], eye) for i in range(7)]
    out_ref[...] = jnp.concatenate(lines + [jnp.zeros((1, LEAF), F32)], axis=0)
    for load in high:
        load.wait()


def down_kernel(top_ref, other_ref, line_ref, link_ref, high_ref, out_ref):
    eye = iota((128, 128), 0) == iota((128, 128), 1)
    total = top_ref[...] + other_ref[...]
    below = total[0:1]
    root = total[1:2] - apply(high_ref[2], below, eye)
    root = apply_t(high_ref[0], root, eye)
    below = apply_t(high_ref[1], below, eye) - apply_t(high_ref[2], root, eye)
    line = line_ref[...]
    third = line[6:7] - apply_t(link_ref[6], below, eye)
    second = [line[4 + c : 5 + c] - apply_t(link_ref[4 + c], third, eye) for c in range(2)]
    lowest = [line[c : c + 1] - apply_t(link_ref[c], second[c // 2], eye) for c in range(4)]
    for j in range(S3):
        lines = []
        for g in range(8):
            value = (lowest[g // 2], second[g // 4], third, below, root)[j // 2]
            value = value[:, (j % 2) * 128 : (j % 2) * 128 + 128]
            lines.append(jnp.broadcast_to(value, (FRONT, 128)))
        out_ref[pl.ds(j, HALF, stride=S3), :] = jnp.concatenate(lines, axis=0)


def backward_kernel(
    home_ref,
    recv_ref,
    rows_ref,
    idx_ref,
    gram_ref,
    inv_ref,
    below_ref,
    solved_hbm,
    other_hbm,
    out_ref,
    known,
    parts,
    moved,
    mark,
    result,
    solved_ref,
    other_ref,
    sems,
):
    loads = [fetch(solved_hbm, solved_ref, sems.at[0]), fetch(other_hbm, other_ref, sems.at[1])]
    for q in range(NLEAF):
        moved[:, q * LEAF : (q + 1) * LEAF] = mark_row(rows_ref[q : q + 1, :], PATH, 0)
    for j in range(S3):
        chunk = crossed(recv_ref[pl.ds(j, HALF, stride=S3), :], home_ref[1])
        known[:, j * 128 : (j + 1) * 128] = chunk
        parts[:, j * 128 : (j + 1) * 128] = stacked(chunk)
    picked = folded(nn(parts[...], moved[...]))
    for load in loads:
        load.wait()
    start = home_ref[0]
    tile = pl.multiple_of((start // 128) * 128, 128)
    home = pltpu.roll(known[:, pl.ds(tile, 128)], (128 - start % 128) % 128, 1)
    home = jnp.where(iota((64, 128), 1) < SHARE, home, 0.0)
    result[:, SPAN:PAD] = stacked(home)
    for q in range(NLEAF):
        cols = slice(q * LEAF, (q + 1) * LEAF)
        hi, lo = split(below_ref[q])
        rows = stacked(picked[:, cols])
        source = stacked(solved_ref[:, cols] - folded(nn(rows, hi) + nn(rows, lo)))
        hi, lo = split(inv_ref[q])
        result[:, cols] = stacked(folded(nn(source, hi) + nn(source, lo)))
    cross = folded(nt(result[...], other_ref[...]))
    cross = cross[:, 0:128] + cross[:, 128:256]
    square = both(folded(nt(result[...], result[...])))
    slots = idx_ref[...].astype(jnp.int32)
    for k in range(CAP):
        mark[:, k * DEV : (k + 1) * DEV] = mark_row(slots[k : k + 1, :], PAD, 0)
    packed = folded(nn(result[...], mark[...]))
    for j in range(8):
        pair = [packed[:, k * DEV : (k + 1) * DEV] for k in (2 * j, 2 * j + 1)]
        out_ref[pl.ds(j, DEV, stride=S4), :] = jnp.concatenate(pair, axis=0).T
    last = packed[:, 16 * DEV : 17 * DEV]
    last = jnp.concatenate([last, last], axis=0).T
    late = jnp.concatenate([square, gram_ref[64:128, :]], axis=0)
    out_ref[pl.ds(8, DEV, stride=S4), :] = jnp.where(iota((DEV, 128), 1) < 64, last, late)
    out_ref[pl.ds(9, DEV, stride=S4), :] = jnp.concatenate([cross, gram_ref[0:64, :]], axis=0)


def total_kernel(recv_ref, out_ref):
    first = jnp.sum(recv_ref[pl.ds(9, DEV, stride=S4), :], axis=0, keepdims=True)
    second = jnp.sum(recv_ref[pl.ds(8, DEV, stride=S4), :], axis=0, keepdims=True)
    out_ref[pl.ds(0, DEV, stride=2), :] = jnp.broadcast_to(first, (DEV, 128))
    out_ref[pl.ds(1, DEV, stride=2), :] = jnp.broadcast_to(second, (DEV, 128))


def unpack_kernel(key_ref, recv_ref, out_ref, mark, value):
    for k in range(CAP):
        mark[k * DEV : (k + 1) * DEV, :] = mark_row(key_ref[...], DEV, k * DEV)
    for j in range(9):
        got = recv_ref[pl.ds(j, DEV, stride=S4), :].T
        value[:, 2 * j * DEV : (2 * j + 1) * DEV] = stacked(got[0:64])
        if j < 8:
            value[:, (2 * j + 1) * DEV : (2 * j + 2) * DEV] = stacked(got[64:128])
    out_ref[...] = folded(nn(value[...], mark[...]))[:, 0:ROWS]


def finish_kernel(
    recv_ref, solved_ref, now_ref, before_ref, coupling_ref, proj_ref, factor_ref, next_ref, value
):
    first = recv_ref[pl.ds(0, DEV, stride=2), :]
    second = recv_ref[pl.ds(1, DEV, stride=2), :]
    count = 1.0 / (ROWS * DEV)
    s_b = first[0:64, 0:64] * count
    s_a = first[0:64, 64:128] * count
    b_b = first[64:128, 0:64] * count
    b_a = first[64:128, 64:128] * count
    s_s = second[0:64, 64:128] * count
    a_a = second[64:128, 64:128] * count
    coupling = coupling_ref[...]
    proj_ref[...] = s_b.T
    line_s = s_s - nt32(s_b, s_b) - nt32(coupling, s_a)
    line_b = s_b - nn32(s_b, b_b) - nt32(coupling, b_a)
    line_a = s_a - nn32(s_b, b_a) - nn32(coupling, a_a)
    gram = line_s - nt32(line_b, s_b) - nt32(line_a, coupling)
    eye = iota((64, 64), 0) == iota((64, 64), 1)
    work = jnp.concatenate([gram, jnp.where(eye, 1.0, 0.0)], axis=1)
    done = []
    for b in range(8):
        height = 64 - 8 * b
        at = 8 * b
        columns = [
            jnp.broadcast_to(work[:, at + c : at + c + 1], (height, 128)) for c in range(8)
        ]
        below = iota((height, 128), 0)
        for c in range(8):
            ratio = jnp.where(below > c, columns[c] * (1.0 / columns[c][c : c + 1, :]), 0.0)
            work = work - ratio * work[c : c + 1, :]
            for e in range(c + 1, 8):
                columns[e] = columns[e] - ratio * columns[e][c : c + 1, :]
        done.append(work[0:8])
        work = work[8:]
    work = jnp.concatenate(done, axis=0)
    scale = lax.rsqrt(jnp.sum(jnp.where(eye, work[:, 0:64], 0.0), axis=1, keepdims=True))
    work = work * scale
    factor_ref[...] = jnp.where(iota((64, 64), 0) <= iota((64, 64), 1), work[:, 0:64], 0.0)
    inverse = work[:, 64:128]
    weight = jnp.concatenate(
        [inverse, -nn32(inverse, s_b), -nn32(inverse, coupling)], axis=1
    )
    hi, lo = split(weight)
    weight = jnp.concatenate([hi, lo], axis=0)
    for b, ref in enumerate((solved_ref, now_ref, before_ref)):
        hi, lo = split(ref[...])
        value[b * 64 : (b + 1) * 64, 0:ROWS] = hi
        value[b * 64 : (b + 1) * 64, PAD : PAD + ROWS] = lo
    total = nn(weight, value[:, 0:ROWS]) + nn(weight, value[:, PAD : PAD + ROWS])
    next_ref[...] = folded(total)


def call(kernel, outs, operands, scratch=(), scalars=0, far=0, far_outs=(), limit=52, micros=4):
    kinds = [pltpu.SMEM] * scalars + [pltpu.VMEM] * (len(operands) - scalars - far)
    kinds += [pltpu.HBM] * far
    return pl.pallas_call(
        kernel,
        out_shape=[jax.ShapeDtypeStruct(shape, dtype) for shape, dtype in outs],
        in_specs=[pl.BlockSpec(memory_space=kind) for kind in kinds],
        out_specs=[
            pl.BlockSpec(memory_space=pltpu.HBM if i in far_outs else pltpu.VMEM)
            for i in range(len(outs))
        ],
        scratch_shapes=list(scratch),
        cost_estimate=pl.CostEstimate(
            flops=micros * 1000000000, bytes_accessed=micros * 3000000, transcendentals=0
        ),
        compiler_params=pltpu.CompilerParams(vmem_limit_bytes=limit * MIB),
    )(*operands)


def exchange(x, lines, axes=AXES):
    peers = x.shape[0] // lines
    return lax.all_to_all(
        x.reshape(peers, 1, lines * 128), axes, split_axis=0, concat_axis=0, tiled=True
    ).reshape(peers * lines, 128)


def per_device(
    block_now,
    block_before,
    coupling,
    vertex_to_tree,
    tree_to_vertex,
    leaf_inverse,
    leaf_below,
    leaf_rows,
    sep_inverse,
    sep_parent,
):
    my_half = lax.axis_index("half")
    my_group = my_half * 8 + lax.axis_index("group")
    my_front = lax.axis_index("front")
    home_slot = jnp.zeros((), jnp.int32)
    for bit in range(LEVELS - 1):
        home_slot = home_slot + (my_group % (2 << bit) == 0).astype(jnp.int32)
    home_at = jnp.stack([home_slot * LEAF + my_front * SHARE, my_half]).astype(jnp.int32)
    half = my_half.astype(jnp.int32).reshape(1)
    V = pltpu.VMEM
    S = pltpu.SemaphoreType.DMA
    packed, key = call(
        pack_kernel,
        [((DEV * S1, 128), F32), ((1, PAD), jnp.int32)],
        (vertex_to_tree, block_now, block_before),
        [
            V((8, PAD), jnp.int32),
            V((DEV, PAD), BF16),
            V((256, PAD), BF16),
            V((PAD, PAD), BF16),
            V((64, ROWS), F32),
            V((64, ROWS), F32),
            S((2,)),
        ],
        far=2,
        limit=58,
    )
    arrived = exchange(packed, S1)
    square, link = call(
        prepare_kernel,
        [((GROUPS, LEAF, LEAF), F32), ((GROUPS - 1, LEAF, LEAF), F32)],
        (sep_inverse, sep_parent),
        [
            V((GROUPS, LEAF, LEAF), F32),
            V((GROUPS - 1, LEAF, LEAF), F32),
            V((GROUPS, LEAF, LEAF), F32),
            V((GROUPS - 1, LEAF, LEAF), F32),
            S((4 * GROUPS,)),
        ],
        far=2,
        far_outs=(0, 1),
    )
    pushed, leaf_solved, tree = call(
        forward_kernel,
        [((HALF * S2, 128), F32), ((64, SPAN), F32), ((64, PAD), F32)],
        (home_at, arrived, leaf_rows, leaf_inverse, leaf_below, link),
        [
            V((PAD, PAD), BF16),
            V((128, PAD), BF16),
            V((SPAN, PATH), BF16),
            V((128, SPAN), BF16),
            V((NLEAF, LEAF, LEAF), F32),
            V((NLEAF, LEAF, LEAF), F32),
            V((64, SPAN), F32),
            V((64, PAD), F32),
            S((4,)),
        ],
        1,
        far=3,
        limit=50,
        far_outs=(1, 2),
    )
    pushed = exchange(pushed, S2, NEAR)
    other, idx, gram = call(
        side_kernel,
        [((256, PAD), BF16), ((128, 128), F32), ((128, 128), F32)],
        (arrived, tree),
        [
            V((PAD, PAD), BF16),
            V((128, PAD), BF16),
            V((64, PAD), F32),
            V((256, PAD), BF16),
            S((2,)),
        ],
        far=1,
        far_outs=(0,),
    )
    small = ((8, LEAF), F32)
    top, source, links = call(
        up_kernel,
        [small, small, ((7, LEAF, LEAF), F32)],
        (half, pushed, link, other),
        [S((7,))],
        1,
        far=2,
    )
    across = [(i, i ^ 12) for i in range(GROUPS)]
    other_top = lax.ppermute(top, ("half", "group"), across)
    line, high = call(
        square_kernel,
        [small, ((3, LEAF, LEAF), F32)],
        (half, source, square, link),
        [V((7, LEAF, LEAF), F32), S((9,))],
        1,
        far=2,
        micros=2,
    )
    (paths,) = call(
        down_kernel,
        [((HALF * S3, 128), F32)],
        (top, other_top, line, links, high),
    )
    paths = exchange(paths, S3, NEAR)
    (returning,) = call(
        backward_kernel,
        [((DEV * S4, 128), F32)],
        (
            home_at,
            paths,
            leaf_rows,
            idx,
            gram,
            leaf_inverse,
            leaf_below,
            leaf_solved,
            other,
        ),
        [
            V((64, PATH), F32),
            V((128, PATH), BF16),
            V((PATH, SPAN), BF16),
            V((PAD, PAD), BF16),
            V((128, PAD), BF16),
            V((64, SPAN), F32),
            V((256, PAD), BF16),
            S((2,)),
        ],
        1,
        far=2,
        limit=46,
    )
    returned = exchange(returning, S4)
    (sums,) = call(total_kernel, [((DEV * 2, 128), F32)], (returned,), micros=1)
    sums = exchange(sums, 2)
    (solved,) = call(
        unpack_kernel,
        [((64, ROWS), F32)],
        (key, returned),
        [V((PAD, PAD), BF16), V((128, PAD), BF16)],
    )
    return tuple(
        call(
            finish_kernel,
            [((64, 64), F32), ((64, 64), F32), ((64, ROWS), F32)],
            (sums, solved, block_now, block_before, coupling),
            [V((192, 2 * PAD), BF16)],
        )
    )


def solution(mesh):
    placed = (
        P(None, AXES),
        P(None, AXES),
        P(),
        P(AXES),
        P(AXES),
        P(AXES, None, None),
        P(AXES, None, None),
        P(AXES, None),
        P(),
        P(),
    )
    split_mesh = Mesh(mesh.devices.reshape(2, 8, 8), AXES)
    return jax.shard_map(
        per_device,
        mesh=split_mesh,
        in_specs=placed,
        out_specs=(P(), P(), P(None, AXES)),
        check_vma=False,
    )
```

```python
import jax
import jax.numpy as jnp
from jax import lax
from jax.experimental import pallas as pl
from jax.experimental.pallas import tpu as pltpu
from jax.sharding import Mesh
from jax.sharding import PartitionSpec as P

F32 = jnp.float32
BF16 = jnp.bfloat16
HIGHEST = lax.Precision.HIGHEST
AXES = ("half", "group", "front")
NEAR = ("group", "front")
HALF = 64
DEV = 128
CAP = 17
ROWS = 2080
PAD = 2176
VEC = 64
LEAF = 256
NLEAF = 8
SPAN = 2048
GROUPS = 16
FRONT = 8
SHARE = 32
LEVELS = 5
PATH = 1280
S1 = 18
S2 = 10
S3 = 10
S4 = 10
MIB = 1024 * 1024


def nn(a, b):
    return lax.dot_general(a, b, (((1,), (0,)), ((), ())), preferred_element_type=F32)


def nt(a, b):
    return lax.dot_general(a, b, (((1,), (1,)), ((), ())), preferred_element_type=F32)


def tn(a, b):
    return lax.dot_general(a, b, (((0,), (0,)), ((), ())), preferred_element_type=F32)


def nn32(a, b):
    return lax.dot_general(
        a, b, (((1,), (0,)), ((), ())), preferred_element_type=F32, precision=HIGHEST
    )


def nt32(a, b):
    return lax.dot_general(
        a, b, (((1,), (1,)), ((), ())), preferred_element_type=F32, precision=HIGHEST
    )


def split(x):
    hi = x.astype(BF16)
    lo = (x - hi.astype(F32)).astype(BF16)
    return hi, lo


def iota(shape, dim):
    return lax.broadcasted_iota(jnp.int32, shape, dim)


I16 = jnp.int16


def onehot(mask):
    return jnp.where(mask, jnp.ones((), BF16), jnp.zeros((), BF16))


def onehot32(mask):
    return jnp.where(mask, 1.0, 0.0).astype(BF16)


def mark_row(row, height, start):
    width = row.shape[1]
    wide = jnp.broadcast_to(row, (16, width)).astype(I16)
    wide = jnp.concatenate([wide] * (height // 16), axis=0)
    return onehot(wide == (iota((height, width), 0) + start).astype(I16))


def mark_column(column, width):
    height = column.shape[0]
    wide = jnp.broadcast_to(column, (height, 128)).astype(I16)
    wide = jnp.concatenate([wide] * (width // 128), axis=1)
    return onehot(wide == iota((height, width), 1).astype(I16))


def stacked(x):
    hi, lo = split(x)
    return jnp.concatenate([hi, lo], axis=0)


def both(x):
    return x + pltpu.roll(x, 64, 1)


def crossed(x, half):
    return jnp.where(half == 1, jnp.concatenate([x[32:64], x[0:32]], axis=0), x)


def folded(x):
    half = x.shape[0] // 2
    return x[0:half] + x[half:]


def fetch(source, target, sem):
    copy = pltpu.make_async_copy(source, target, sem)
    copy.start()
    return copy


def pack_kernel(
    vt_ref, now_hbm, before_hbm, out_ref, key_ref, dest, member, value, mark, now, before, sems
):
    loads = [fetch(now_hbm, now, sems.at[0]), fetch(before_hbm, before, sems.at[1])]
    dest[...] = jnp.full((8, PAD), -1, jnp.int32)
    dest[0:1, 0:ROWS] = vt_ref[...].reshape(1, ROWS)
    target = dest[0:1, :]
    bucket = ((target.astype(F32) + 0.5) * (1.0 / ROWS)).astype(jnp.int32)
    bucket = jnp.where(target < 0, -1, bucket)
    place = target - bucket * ROWS
    member[...] = mark_row(bucket, DEV, 0)
    earlier = onehot32(
        (iota((128, 256), 0) < iota((128, 256), 1)) | (iota((128, 256), 1) >= 128)
    )
    carry = jnp.zeros((DEV, 128), F32)
    ranks = []
    for b in range(CAP):
        part = member[:, b * 128 : (b + 1) * 128]
        counts = nn(part, earlier)
        ranks.append(
            jnp.sum(part.astype(F32) * (counts[:, 0:128] + carry), axis=0, keepdims=True)
        )
        carry = carry + counts[:, 128:256]
    rank = jnp.concatenate(ranks, axis=1).astype(jnp.int32)
    key = jnp.where(target < 0, -1, rank * DEV + bucket)
    for k in range(8):
        mark[k * DEV : (k + 1) * DEV, :] = mark_row(key, DEV, k * DEV)
    for load in loads:
        load.wait()
    value[:, SPAN:PAD] = jnp.zeros((4 * VEC, PAD - SPAN), BF16)
    now_hi, now_lo = split(now[...])
    bef_hi, bef_lo = split(before[...])
    value[0:64, 0:ROWS] = now_hi
    value[64:128, 0:ROWS] = bef_hi
    value[128:192, 0:ROWS] = now_lo
    value[192:256, 0:ROWS] = bef_lo
    key_ref[...] = key
    for k in range(8, CAP):
        mark[k * DEV : (k + 1) * DEV, :] = mark_row(key, DEV, k * DEV)
    block = nt(mark[...], value[...])
    block = block[:, 0:128] + block[:, 128:256]
    for k in range(CAP):
        out_ref[pl.ds(k, DEV, stride=S1), :] = block[k * DEV : (k + 1) * DEV]
    ranked = jnp.broadcast_to(rank, (32, PAD)) == iota((32, PAD), 0)
    high = place // 64
    marks = jnp.concatenate(
        [
            jnp.where(ranked, jnp.broadcast_to(high, (32, PAD)).astype(F32), 0.0),
            jnp.where(ranked, jnp.broadcast_to(place - high * 64, (32, PAD)).astype(F32), 0.0),
            jnp.zeros((64, PAD), F32),
        ],
        axis=0,
    ).astype(BF16)
    found = nt(member[...], marks)
    where = found * 64.0 + pltpu.roll(found, 96, 1)
    lane = iota((DEV, 128), 1)
    filled = (lane.astype(F32) < carry) & (lane < CAP)
    out_ref[pl.ds(CAP, DEV, stride=S1), :] = jnp.where(filled, where, -1.0)


def forward_kernel(
    home_ref,
    half_ref,
    recv_ref,
    rows_ref,
    inv_hbm,
    below_hbm,
    ready_hbm,
    out_ref,
    solved_hbm,
    tree_hbm,
    mark,
    value,
    moved,
    update,
    inv_ref,
    below_ref,
    solved_ref,
    tree_ref,
    sems,
):
    loads = []
    for q in range(NLEAF):
        loads.append(fetch(inv_hbm.at[q], inv_ref.at[q], sems.at[4 + q]))
        loads.append(fetch(below_hbm.at[q], below_ref.at[q], sems.at[12 + q]))
    idx = recv_ref[pl.ds(CAP, DEV, stride=S1), :].astype(jnp.int32)
    for k in range(CAP):
        got = recv_ref[pl.ds(k, DEV, stride=S1), :].T
        value[:, k * DEV : (k + 1) * DEV] = stacked(got[0:64])
        mark[k * DEV : (k + 1) * DEV, :] = mark_column(idx[:, k : k + 1], PAD)
    tree_ref[...] = folded(nn(value[...], mark[...]))
    stores = [fetch(tree_ref, tree_hbm, sems.at[2])]
    rows = rows_ref[...].astype(F32).T.astype(jnp.int32)
    for q in range(NLEAF):
        moved[q * LEAF : (q + 1) * LEAF, :] = mark_column(rows[:, q : q + 1], PATH)
    for load in loads:
        load.wait()
    for q in range(NLEAF):
        cols = slice(q * LEAF, (q + 1) * LEAF)
        hi, lo = split(inv_ref[q])
        source = stacked(tree_ref[:, cols])
        solved = folded(nt(source, hi) + nt(source, lo))
        solved_ref[:, cols] = solved
        hi, lo = split(below_ref[q])
        solved = stacked(solved)
        update[:, cols] = stacked(folded(nt(solved, hi) + nt(solved, lo)))
    stores.append(fetch(solved_ref, solved_hbm, sems.at[3]))
    pushed = folded(nn(update[...], moved[...]))
    start = home_ref[0]
    own = pltpu.roll(tree_ref[:, SPAN:PAD], start % 128, 1)
    for j in range(S2):
        chunk = jnp.where(start // 128 == j, own, 0.0) - pushed[:, j * 128 : (j + 1) * 128]
        out_ref[pl.ds(j, HALF, stride=S2), :] = crossed(chunk, half_ref[0])
    for store in stores:
        store.wait()


def side_kernel(
    recv_ref, tree_hbm, other_hbm, idx_ref, gram_ref, mark, value, tree_ref, other_ref, sems
):
    load = fetch(tree_hbm, tree_ref, sems.at[0])
    where = recv_ref[pl.ds(CAP, DEV, stride=S1), :]
    idx_ref[...] = where.T
    idx = where.astype(jnp.int32)
    for k in range(CAP):
        got = recv_ref[pl.ds(k, DEV, stride=S1), :].T
        value[:, k * DEV : (k + 1) * DEV] = stacked(got[64:128])
        mark[k * DEV : (k + 1) * DEV, :] = mark_column(idx[:, k : k + 1], PAD)
    before = folded(nn(value[...], mark[...]))
    load.wait()
    hi, lo = split(tree_ref[...])
    other_ref[0:64, :] = hi
    other_ref[128:192, :] = lo
    hi, lo = split(before)
    other_ref[64:128, :] = hi
    other_ref[192:256, :] = lo
    store = fetch(other_ref, other_hbm, sems.at[1])
    gram = folded(nt(other_ref[...], other_ref[...]))
    gram_ref[...] = gram[:, 0:128] + gram[:, 128:256]
    store.wait()


def prepare_kernel(
    inv_hbm, parent_hbm, square_hbm, link_hbm, inv_ref, parent_ref, square_ref, link_ref, sems
):
    inv_loads = []
    parent_loads = []
    stores = []
    for s in range(GROUPS):
        inv_loads.append(fetch(inv_hbm.at[s], inv_ref.at[s], sems.at[s]))
        if s > 0:
            at = s - 1
            parent_loads.append(
                fetch(parent_hbm.at[at], parent_ref.at[at], sems.at[GROUPS + at])
            )
    for first in (0, GROUPS // 2):
        for s in range(first, first + GROUPS // 2):
            inv_loads[s].wait()
            if s > 0:
                parent_loads[s - 1].wait()
        for s in range(first, first + GROUPS // 2):
            hi, lo = split(inv_ref[s])
            square_ref[s] = tn(hi, hi) + (tn(hi, lo) + tn(lo, hi))
            if s > 0:
                up, down = split(parent_ref[s - 1])
                link_ref[s - 1] = nn(up, hi) + (nn(up, lo) + nn(down, hi))
        for s in range(first, first + GROUPS // 2):
            stores.append(fetch(square_ref.at[s], square_hbm.at[s], sems.at[2 * GROUPS + s]))
            if s > 0:
                at = s - 1
                stores.append(fetch(link_ref.at[at], link_hbm.at[at], sems.at[3 * GROUPS + at]))
    for store in stores:
        store.wait()


def to_row(column, eye):
    top = jnp.sum(jnp.where(eye, column[0:128], 0.0), axis=0, keepdims=True)
    bottom = jnp.sum(jnp.where(eye, column[128:256], 0.0), axis=0, keepdims=True)
    return jnp.concatenate([top, bottom], axis=1)


def to_column(row, eye):
    top = jnp.sum(jnp.where(eye, row[:, 0:128], 0.0), axis=1, keepdims=True)
    bottom = jnp.sum(jnp.where(eye, row[:, 128:256], 0.0), axis=1, keepdims=True)
    return jnp.concatenate([top, bottom], axis=0)


def apply(matrix, row, eye):
    product = matrix * row
    return to_row(jnp.sum(product[:, 0:128] + product[:, 128:256], axis=1, keepdims=True), eye)


def apply_t(matrix, row, eye):
    return jnp.sum(matrix * to_column(row, eye), axis=0, keepdims=True)


def local_links(half):
    return [7 + 4 * half + c for c in range(4)] + [3 + 2 * half + c for c in range(2)] + [1 + half]


def up_kernel(half_ref, recv_ref, link_hbm, ready_hbm, top_ref, source_ref, link_ref, sems):
    half = half_ref[0]
    loads = [
        fetch(link_hbm.at[at], link_ref.at[i], sems.at[i])
        for i, at in enumerate(local_links(half))
    ]
    eye = iota((128, 128), 0) == iota((128, 128), 1)
    sums = []
    for height in range(1, LEVELS + 1):
        count = max(8 >> height, 1)
        span = HALF // count
        left = recv_ref[pl.ds(2 * height - 2, HALF, stride=S2), :]
        right = recv_ref[pl.ds(2 * height - 1, HALF, stride=S2), :]
        for c in range(count):
            at = slice(c * span, (c + 1) * span)
            ends = [jnp.sum(part[at], axis=0, keepdims=True) for part in (left, right)]
            sums.append(jnp.concatenate(ends, axis=1))
    for load in loads:
        load.wait()
    for i in range(7):
        to = 4 + i // 2 if i < 4 else (6 if i < 6 else 7)
        sums[to] = sums[to] - apply(link_ref[i], sums[i], eye)
    top_ref[...] = jnp.concatenate(sums[7:9] + [jnp.zeros((6, LEAF), F32)], axis=0)
    source_ref[...] = jnp.concatenate(sums[0:7] + [jnp.zeros((1, LEAF), F32)], axis=0)


def square_kernel(
    half_ref, source_ref, square_hbm, link_hbm, out_ref, high_ref, square_ref, sems
):
    half = half_ref[0]
    loads = [
        fetch(square_hbm.at[at + 1], square_ref.at[i], sems.at[i])
        for i, at in enumerate(local_links(half))
    ]
    high = [
        fetch(square_hbm.at[0:2], high_ref.at[0:2], sems.at[7]),
        fetch(link_hbm.at[0], high_ref.at[2], sems.at[8]),
    ]
    eye = iota((128, 128), 0) == iota((128, 128), 1)
    for load in loads:
        load.wait()
    lines = [apply_t(square_ref[i], source_ref[i : i + 1, :], eye) for i in range(7)]
    out_ref[...] = jnp.concatenate(lines + [jnp.zeros((1, LEAF), F32)], axis=0)
    for load in high:
        load.wait()


def down_kernel(top_ref, other_ref, line_ref, link_ref, high_ref, out_ref):
    eye = iota((128, 128), 0) == iota((128, 128), 1)
    total = top_ref[...] + other_ref[...]
    below = total[0:1]
    root = total[1:2] - apply(high_ref[2], below, eye)
    root = apply_t(high_ref[0], root, eye)
    below = apply_t(high_ref[1], below, eye) - apply_t(high_ref[2], root, eye)
    line = line_ref[...]
    third = line[6:7] - apply_t(link_ref[6], below, eye)
    second = [line[4 + c : 5 + c] - apply_t(link_ref[4 + c], third, eye) for c in range(2)]
    lowest = [line[c : c + 1] - apply_t(link_ref[c], second[c // 2], eye) for c in range(4)]
    for j in range(S3):
        lines = []
        for g in range(8):
            value = (lowest[g // 2], second[g // 4], third, below, root)[j // 2]
            value = value[:, (j % 2) * 128 : (j % 2) * 128 + 128]
            lines.append(jnp.broadcast_to(value, (FRONT, 128)))
        out_ref[pl.ds(j, HALF, stride=S3), :] = jnp.concatenate(lines, axis=0)


def backward_kernel(
    home_ref,
    half_ref,
    recv_ref,
    rows_ref,
    idx_ref,
    gram_ref,
    inv_ref,
    below_ref,
    solved_hbm,
    other_hbm,
    out_ref,
    known,
    parts,
    moved,
    mark,
    result,
    solved_ref,
    other_ref,
    sems,
):
    loads = [fetch(solved_hbm, solved_ref, sems.at[0]), fetch(other_hbm, other_ref, sems.at[1])]
    for q in range(NLEAF):
        moved[:, q * LEAF : (q + 1) * LEAF] = mark_row(rows_ref[q : q + 1, :], PATH, 0)
    for j in range(S3):
        chunk = crossed(recv_ref[pl.ds(j, HALF, stride=S3), :], half_ref[0])
        known[:, j * 128 : (j + 1) * 128] = chunk
        parts[:, j * 128 : (j + 1) * 128] = stacked(chunk)
    picked = folded(nn(parts[...], moved[...]))
    for load in loads:
        load.wait()
    start = home_ref[0]
    tile = pl.multiple_of((start // 128) * 128, 128)
    home = pltpu.roll(known[:, pl.ds(tile, 128)], (128 - start % 128) % 128, 1)
    home = jnp.where(iota((64, 128), 1) < SHARE, home, 0.0)
    result[:, SPAN:PAD] = stacked(home)
    for q in range(NLEAF):
        cols = slice(q * LEAF, (q + 1) * LEAF)
        hi, lo = split(below_ref[q])
        rows = stacked(picked[:, cols])
        source = stacked(solved_ref[:, cols] - folded(nn(rows, hi) + nn(rows, lo)))
        hi, lo = split(inv_ref[q])
        result[:, cols] = stacked(folded(nn(source, hi) + nn(source, lo)))
    cross = folded(nt(result[...], other_ref[...]))
    cross = cross[:, 0:128] + cross[:, 128:256]
    square = both(folded(nt(result[...], result[...])))
    slots = idx_ref[...].astype(jnp.int32)
    for k in range(CAP):
        mark[:, k * DEV : (k + 1) * DEV] = mark_row(slots[k : k + 1, :], PAD, 0)
    packed = folded(nn(result[...], mark[...]))
    for j in range(8):
        pair = [packed[:, k * DEV : (k + 1) * DEV] for k in (2 * j, 2 * j + 1)]
        out_ref[pl.ds(j, DEV, stride=S4), :] = jnp.concatenate(pair, axis=0).T
    last = packed[:, 16 * DEV : 17 * DEV]
    last = jnp.concatenate([last, last], axis=0).T
    late = jnp.concatenate([square, gram_ref[64:128, :]], axis=0)
    out_ref[pl.ds(8, DEV, stride=S4), :] = jnp.where(iota((DEV, 128), 1) < 64, last, late)
    out_ref[pl.ds(9, DEV, stride=S4), :] = jnp.concatenate([cross, gram_ref[0:64, :]], axis=0)


def total_kernel(recv_ref, out_ref):
    first = jnp.sum(recv_ref[pl.ds(9, DEV, stride=S4), :], axis=0, keepdims=True)
    second = jnp.sum(recv_ref[pl.ds(8, DEV, stride=S4), :], axis=0, keepdims=True)
    out_ref[pl.ds(0, DEV, stride=2), :] = jnp.broadcast_to(first, (DEV, 128))
    out_ref[pl.ds(1, DEV, stride=2), :] = jnp.broadcast_to(second, (DEV, 128))


def unpack_kernel(key_ref, recv_ref, out_ref, mark, value):
    for k in range(CAP):
        mark[k * DEV : (k + 1) * DEV, :] = mark_row(key_ref[...], DEV, k * DEV)
    for j in range(9):
        got = recv_ref[pl.ds(j, DEV, stride=S4), :].T
        value[:, 2 * j * DEV : (2 * j + 1) * DEV] = stacked(got[0:64])
        if j < 8:
            value[:, (2 * j + 1) * DEV : (2 * j + 2) * DEV] = stacked(got[64:128])
    out_ref[...] = folded(nn(value[...], mark[...]))[:, 0:ROWS]


def finish_kernel(
    recv_ref, solved_ref, now_ref, before_ref, coupling_ref, proj_ref, factor_ref, next_ref, value
):
    first = recv_ref[pl.ds(0, DEV, stride=2), :]
    second = recv_ref[pl.ds(1, DEV, stride=2), :]
    count = 1.0 / (ROWS * DEV)
    s_b = first[0:64, 0:64] * count
    s_a = first[0:64, 64:128] * count
    b_b = first[64:128, 0:64] * count
    b_a = first[64:128, 64:128] * count
    s_s = second[0:64, 64:128] * count
    a_a = second[64:128, 64:128] * count
    coupling = coupling_ref[...]
    proj_ref[...] = s_b.T
    line_s = s_s - nt32(s_b, s_b) - nt32(coupling, s_a)
    line_b = s_b - nn32(s_b, b_b) - nt32(coupling, b_a)
    line_a = s_a - nn32(s_b, b_a) - nn32(coupling, a_a)
    gram = line_s - nt32(line_b, s_b) - nt32(line_a, coupling)
    eye = iota((64, 64), 0) == iota((64, 64), 1)
    work = jnp.concatenate([gram, jnp.where(eye, 1.0, 0.0)], axis=1)
    done = []
    for b in range(4):
        height = 64 - 16 * b
        at = 16 * b
        columns = [
            jnp.broadcast_to(work[:, at + c : at + c + 1], (height, 128)) for c in range(16)
        ]
        below = iota((height, 128), 0)
        for c in range(16):
            ratio = jnp.where(below > c, columns[c] * (1.0 / columns[c][c : c + 1, :]), 0.0)
            work = work - ratio * work[c : c + 1, :]
            for e in range(c + 1, 16):
                columns[e] = columns[e] - ratio * columns[e][c : c + 1, :]
        done.append(work[0:16])
        work = work[16:]
    work = jnp.concatenate(done, axis=0)
    scale = lax.rsqrt(jnp.sum(jnp.where(eye, work[:, 0:64], 0.0), axis=1, keepdims=True))
    work = work * scale
    factor_ref[...] = jnp.where(iota((64, 64), 0) <= iota((64, 64), 1), work[:, 0:64], 0.0)
    inverse = work[:, 64:128]
    weight = jnp.concatenate(
        [inverse, -nn32(inverse, s_b), -nn32(inverse, coupling)], axis=1
    )
    hi, lo = split(weight)
    weight = jnp.concatenate([hi, lo], axis=0)
    for b, ref in enumerate((solved_ref, now_ref, before_ref)):
        hi, lo = split(ref[...])
        value[b * 64 : (b + 1) * 64, 0:ROWS] = hi
        value[b * 64 : (b + 1) * 64, PAD : PAD + ROWS] = lo
    total = nn(weight, value[:, 0:ROWS]) + nn(weight, value[:, PAD : PAD + ROWS])
    next_ref[...] = folded(total)


def call(kernel, outs, operands, scratch=(), scalars=0, far=0, far_outs=(), limit=52, micros=4):
    kinds = [pltpu.SMEM] * scalars + [pltpu.VMEM] * (len(operands) - scalars - far)
    kinds += [pltpu.HBM] * far
    return pl.pallas_call(
        kernel,
        out_shape=[jax.ShapeDtypeStruct(shape, dtype) for shape, dtype in outs],
        in_specs=[pl.BlockSpec(memory_space=kind) for kind in kinds],
        out_specs=[
            pl.BlockSpec(memory_space=pltpu.HBM if i in far_outs else pltpu.VMEM)
            for i in range(len(outs))
        ],
        scratch_shapes=list(scratch),
        cost_estimate=pl.CostEstimate(
            flops=micros * 1000000000, bytes_accessed=micros * 3000000, transcendentals=0
        ),
        compiler_params=pltpu.CompilerParams(vmem_limit_bytes=limit * MIB),
    )(*operands)


def exchange(x, lines, axes=AXES):
    peers = x.shape[0] // lines
    return lax.all_to_all(
        x.reshape(peers, 1, lines * 128), axes, split_axis=0, concat_axis=0, tiled=True
    ).reshape(peers * lines, 128)


def per_device(
    block_now,
    block_before,
    coupling,
    vertex_to_tree,
    tree_to_vertex,
    leaf_inverse,
    leaf_below,
    leaf_rows,
    sep_inverse,
    sep_parent,
):
    my_half = lax.axis_index("half")
    my_group = my_half * 8 + lax.axis_index("group")
    my_front = lax.axis_index("front")
    home_slot = jnp.zeros((), jnp.int32)
    for bit in range(LEVELS - 1):
        home_slot = home_slot + (my_group % (2 << bit) == 0).astype(jnp.int32)
    home_at = (home_slot * LEAF + my_front * SHARE).astype(jnp.int32).reshape(1)
    half = my_half.astype(jnp.int32).reshape(1)
    V = pltpu.VMEM
    S = pltpu.SemaphoreType.DMA
    packed, key = call(
        pack_kernel,
        [((DEV * S1, 128), F32), ((1, PAD), jnp.int32)],
        (vertex_to_tree, block_now, block_before),
        [
            V((8, PAD), jnp.int32),
            V((DEV, PAD), BF16),
            V((256, PAD), BF16),
            V((PAD, PAD), BF16),
            V((64, ROWS), F32),
            V((64, ROWS), F32),
            S((2,)),
        ],
        far=2,
        limit=58,
    )
    arrived = exchange(packed, S1)
    square, link = call(
        prepare_kernel,
        [((GROUPS, LEAF, LEAF), F32), ((GROUPS - 1, LEAF, LEAF), F32)],
        (sep_inverse, sep_parent),
        [
            V((GROUPS, LEAF, LEAF), F32),
            V((GROUPS - 1, LEAF, LEAF), F32),
            V((GROUPS, LEAF, LEAF), F32),
            V((GROUPS - 1, LEAF, LEAF), F32),
            S((4 * GROUPS,)),
        ],
        far=2,
        far_outs=(0, 1),
    )
    pushed, leaf_solved, tree = call(
        forward_kernel,
        [((HALF * S2, 128), F32), ((64, SPAN), F32), ((64, PAD), F32)],
        (home_at, half, arrived, leaf_rows, leaf_inverse, leaf_below, link),
        [
            V((PAD, PAD), BF16),
            V((128, PAD), BF16),
            V((SPAN, PATH), BF16),
            V((128, SPAN), BF16),
            V((NLEAF, LEAF, LEAF), F32),
            V((NLEAF, LEAF, LEAF), F32),
            V((64, SPAN), F32),
            V((64, PAD), F32),
            S((20,)),
        ],
        2,
        far=3,
        limit=50,
        far_outs=(1, 2),
    )
    pushed = exchange(pushed, S2, NEAR)
    other, idx, gram = call(
        side_kernel,
        [((256, PAD), BF16), ((128, 128), F32), ((128, 128), F32)],
        (arrived, tree),
        [
            V((PAD, PAD), BF16),
            V((128, PAD), BF16),
            V((64, PAD), F32),
            V((256, PAD), BF16),
            S((2,)),
        ],
        far=1,
        far_outs=(0,),
    )
    small = ((8, LEAF), F32)
    top, source, links = call(
        up_kernel,
        [small, small, ((7, LEAF, LEAF), F32)],
        (half, pushed, link, other),
        [S((7,))],
        1,
        far=2,
        limit=50,
    )
    across = [(i, i ^ 12) for i in range(GROUPS)]
    other_top = lax.ppermute(top, ("half", "group"), across)
    line, high = call(
        square_kernel,
        [small, ((3, LEAF, LEAF), F32)],
        (half, source, square, link),
        [V((7, LEAF, LEAF), F32), S((9,))],
        1,
        far=2,
        limit=50,
        micros=2,
    )
    (paths,) = call(
        down_kernel,
        [((HALF * S3, 128), F32)],
        (top, other_top, line, links, high),
        limit=50,
    )
    paths = exchange(paths, S3, NEAR)
    (returning,) = call(
        backward_kernel,
        [((DEV * S4, 128), F32)],
        (
            home_at,
            half,
            paths,
            leaf_rows,
            idx,
            gram,
            leaf_inverse,
            leaf_below,
            leaf_solved,
            other,
        ),
        [
            V((64, PATH), F32),
            V((128, PATH), BF16),
            V((PATH, SPAN), BF16),
            V((PAD, PAD), BF16),
            V((128, PAD), BF16),
            V((64, SPAN), F32),
            V((256, PAD), BF16),
            S((2,)),
        ],
        2,
        far=2,
        limit=46,
    )
    returned = exchange(returning, S4)
    (sums,) = call(total_kernel, [((DEV * 2, 128), F32)], (returned,), micros=1)
    sums = exchange(sums, 2)
    (solved,) = call(
        unpack_kernel,
        [((64, ROWS), F32)],
        (key, returned),
        [V((PAD, PAD), BF16), V((128, PAD), BF16)],
    )
    return tuple(
        call(
            finish_kernel,
            [((64, 64), F32), ((64, 64), F32), ((64, ROWS), F32)],
            (sums, solved, block_now, block_before, coupling),
            [V((192, 2 * PAD), BF16)],
        )
    )


def solution(mesh):
    placed = (
        P(None, AXES),
        P(None, AXES),
        P(),
        P(AXES),
        P(AXES),
        P(AXES, None, None),
        P(AXES, None, None),
        P(AXES, None),
        P(),
        P(),
    )
    split_mesh = Mesh(mesh.devices.reshape(2, 8, 8), AXES)
    return jax.shard_map(
        per_device,
        mesh=split_mesh,
        in_specs=placed,
        out_specs=(P(), P(), P(None, AXES)),
        check_vma=False,
    )
```

```python
import jax
import jax.numpy as jnp
from jax import lax
from jax.experimental import pallas as pl
from jax.experimental.pallas import tpu as pltpu
from jax.sharding import Mesh
from jax.sharding import PartitionSpec as P

F32 = jnp.float32
BF16 = jnp.bfloat16
HIGHEST = lax.Precision.HIGHEST
AXES = ("half", "group", "front")
NEAR = ("group", "front")
HALF = 64
DEV = 128
CAP = 17
ROWS = 2080
PAD = 2176
VEC = 64
LEAF = 256
NLEAF = 8
SPAN = 2048
GROUPS = 16
FRONT = 8
SHARE = 32
LEVELS = 5
PATH = 1280
S1 = 18
S2 = 10
S3 = 10
S4 = 12
S5 = 3
MIB = 1024 * 1024


def nn(a, b):
    return lax.dot_general(a, b, (((1,), (0,)), ((), ())), preferred_element_type=F32)


def nt(a, b):
    return lax.dot_general(a, b, (((1,), (1,)), ((), ())), preferred_element_type=F32)


def tn(a, b):
    return lax.dot_general(a, b, (((0,), (0,)), ((), ())), preferred_element_type=F32)


def nn32(a, b):
    return lax.dot_general(
        a, b, (((1,), (0,)), ((), ())), preferred_element_type=F32, precision=HIGHEST
    )


def nt32(a, b):
    return lax.dot_general(
        a, b, (((1,), (1,)), ((), ())), preferred_element_type=F32, precision=HIGHEST
    )


def split(x):
    hi = x.astype(BF16)
    lo = (x - hi.astype(F32)).astype(BF16)
    return hi, lo


def iota(shape, dim):
    return lax.broadcasted_iota(jnp.int32, shape, dim)


I16 = jnp.int16


def onehot(mask):
    return jnp.where(mask, jnp.ones((), BF16), jnp.zeros((), BF16))


def onehot32(mask):
    return jnp.where(mask, 1.0, 0.0).astype(BF16)


def mark_row(row, height, start):
    width = row.shape[1]
    wide = jnp.broadcast_to(row, (16, width)).astype(I16)
    wide = jnp.concatenate([wide] * (height // 16), axis=0)
    return onehot(wide == (iota((height, width), 0) + start).astype(I16))


def mark_column(column, width):
    height = column.shape[0]
    wide = jnp.broadcast_to(column, (height, 128)).astype(I16)
    wide = jnp.concatenate([wide] * (width // 128), axis=1)
    return onehot(wide == iota((height, width), 1).astype(I16))


def stacked(x):
    hi, lo = split(x)
    return jnp.concatenate([hi, lo], axis=0)


def both(x):
    return x + pltpu.roll(x, 64, 1)


def crossed(x, half):
    return jnp.where(half == 1, jnp.concatenate([x[32:64], x[0:32]], axis=0), x)


def folded(x):
    half = x.shape[0] // 2
    return x[0:half] + x[half:]


def fetch(source, target, sem):
    copy = pltpu.make_async_copy(source, target, sem)
    copy.start()
    return copy


def pack_kernel(
    vt_ref, now_hbm, before_hbm, out_ref, key_ref, dest, member, value, mark, now, before, sems
):
    loads = [fetch(now_hbm, now, sems.at[0]), fetch(before_hbm, before, sems.at[1])]
    dest[...] = jnp.full((8, PAD), -1, jnp.int32)
    dest[0:1, 0:ROWS] = vt_ref[...].reshape(1, ROWS)
    target = dest[0:1, :]
    bucket = ((target.astype(F32) + 0.5) * (1.0 / ROWS)).astype(jnp.int32)
    bucket = jnp.where(target < 0, -1, bucket)
    place = target - bucket * ROWS
    member[...] = mark_row(bucket, DEV, 0)
    earlier = onehot32(
        (iota((128, 256), 0) < iota((128, 256), 1)) | (iota((128, 256), 1) >= 128)
    )
    carry = jnp.zeros((DEV, 128), F32)
    ranks = []
    for b in range(CAP):
        part = member[:, b * 128 : (b + 1) * 128]
        counts = nn(part, earlier)
        ranks.append(
            jnp.sum(part.astype(F32) * (counts[:, 0:128] + carry), axis=0, keepdims=True)
        )
        carry = carry + counts[:, 128:256]
    rank = jnp.concatenate(ranks, axis=1).astype(jnp.int32)
    key = jnp.where(target < 0, -1, rank * DEV + bucket)
    ranked = jnp.broadcast_to(rank, (32, PAD)) == iota((32, PAD), 0)
    high = place // 64
    marks = jnp.concatenate(
        [
            jnp.where(ranked, jnp.broadcast_to(high, (32, PAD)).astype(F32), 0.0),
            jnp.where(ranked, jnp.broadcast_to(place - high * 64, (32, PAD)).astype(F32), 0.0),
            jnp.zeros((64, PAD), F32),
        ],
        axis=0,
    ).astype(BF16)
    found = nt(member[...], marks)
    where = found * 64.0 + pltpu.roll(found, 96, 1)
    lane = iota((DEV, 128), 1)
    filled = (lane.astype(F32) < carry) & (lane < CAP)
    out_ref[pl.ds(CAP, DEV, stride=S1), :] = jnp.where(filled, where, -1.0)
    for k in range(8):
        mark[k * DEV : (k + 1) * DEV, :] = mark_row(key, DEV, k * DEV)
    for load in loads:
        load.wait()
    value[:, SPAN:PAD] = jnp.zeros((4 * VEC, PAD - SPAN), BF16)
    now_hi, now_lo = split(now[...])
    bef_hi, bef_lo = split(before[...])
    value[0:64, 0:ROWS] = now_hi
    value[64:128, 0:ROWS] = bef_hi
    value[128:192, 0:ROWS] = now_lo
    value[192:256, 0:ROWS] = bef_lo
    key_ref[...] = key
    for k in range(8, CAP):
        mark[k * DEV : (k + 1) * DEV, :] = mark_row(key, DEV, k * DEV)
    block = nt(mark[...], value[...])
    block = block[:, 0:128] + block[:, 128:256]
    for k in range(CAP):
        out_ref[pl.ds(k, DEV, stride=S1), :] = block[k * DEV : (k + 1) * DEV]


def forward_kernel(
    home_ref,
    half_ref,
    recv_ref,
    rows_ref,
    inv_hbm,
    below_hbm,
    ready_hbm,
    out_ref,
    solved_hbm,
    tree_hbm,
    mark,
    value,
    moved,
    update,
    inv_ref,
    below_ref,
    solved_ref,
    tree_ref,
    sems,
):
    loads = []
    for q in range(NLEAF):
        loads.append(fetch(inv_hbm.at[q], inv_ref.at[q], sems.at[4 + q]))
        loads.append(fetch(below_hbm.at[q], below_ref.at[q], sems.at[12 + q]))
    idx = recv_ref[pl.ds(CAP, DEV, stride=S1), :].astype(jnp.int32)
    for k in range(CAP):
        got = recv_ref[pl.ds(k, DEV, stride=S1), :].T
        value[:, k * DEV : (k + 1) * DEV] = stacked(got[0:64])
        mark[k * DEV : (k + 1) * DEV, :] = mark_column(idx[:, k : k + 1], PAD)
    tree_ref[...] = folded(nn(value[...], mark[...]))
    stores = [fetch(tree_ref, tree_hbm, sems.at[2])]
    rows = rows_ref[...].astype(F32).T.astype(jnp.int32)
    for q in range(NLEAF):
        moved[q * LEAF : (q + 1) * LEAF, :] = mark_column(rows[:, q : q + 1], PATH)
    for load in loads:
        load.wait()
    for q in range(NLEAF):
        cols = slice(q * LEAF, (q + 1) * LEAF)
        hi, lo = split(inv_ref[q])
        source = stacked(tree_ref[:, cols])
        solved = folded(nt(source, hi) + nt(source, lo))
        solved_ref[:, cols] = solved
        hi, lo = split(below_ref[q])
        solved = stacked(solved)
        update[:, cols] = stacked(folded(nt(solved, hi) + nt(solved, lo)))
    stores.append(fetch(solved_ref, solved_hbm, sems.at[3]))
    pushed = folded(nn(update[...], moved[...]))
    start = home_ref[0]
    own = pltpu.roll(tree_ref[:, SPAN:PAD], start % 128, 1)
    for j in range(S2):
        chunk = jnp.where(start // 128 == j, own, 0.0) - pushed[:, j * 128 : (j + 1) * 128]
        out_ref[pl.ds(j, HALF, stride=S2), :] = crossed(chunk, half_ref[0])
    for store in stores:
        store.wait()


def side_kernel(
    recv_ref, tree_hbm, other_hbm, idx_ref, gram_ref, mark, value, tree_ref, other_ref, sems
):
    load = fetch(tree_hbm, tree_ref, sems.at[0])
    where = recv_ref[pl.ds(CAP, DEV, stride=S1), :]
    idx_ref[...] = where.T
    idx = where.astype(jnp.int32)
    for k in range(CAP):
        got = recv_ref[pl.ds(k, DEV, stride=S1), :].T
        value[:, k * DEV : (k + 1) * DEV] = stacked(got[64:128])
        mark[k * DEV : (k + 1) * DEV, :] = mark_column(idx[:, k : k + 1], PAD)
    before = folded(nn(value[...], mark[...]))
    load.wait()
    hi, lo = split(tree_ref[...])
    other_ref[0:64, :] = hi
    other_ref[128:192, :] = lo
    hi, lo = split(before)
    other_ref[64:128, :] = hi
    other_ref[192:256, :] = lo
    store = fetch(other_ref, other_hbm, sems.at[1])
    gram = folded(nt(other_ref[...], other_ref[...]))
    gram_ref[...] = gram[:, 0:128] + gram[:, 128:256]
    store.wait()


def prepare_kernel(
    inv_hbm, parent_hbm, square_hbm, link_hbm, inv_ref, parent_ref, square_ref, link_ref, sems
):
    inv_loads = []
    parent_loads = []
    stores = []
    for s in range(GROUPS):
        inv_loads.append(fetch(inv_hbm.at[s], inv_ref.at[s], sems.at[s]))
        if s > 0:
            at = s - 1
            parent_loads.append(
                fetch(parent_hbm.at[at], parent_ref.at[at], sems.at[GROUPS + at])
            )
    for first in (0, GROUPS // 2):
        for s in range(first, first + GROUPS // 2):
            inv_loads[s].wait()
            if s > 0:
                parent_loads[s - 1].wait()
        for s in range(first, first + GROUPS // 2):
            hi, lo = split(inv_ref[s])
            square_ref[s] = tn(hi, hi) + (tn(hi, lo) + tn(lo, hi))
            if s > 0:
                up, down = split(parent_ref[s - 1])
                link_ref[s - 1] = nn(up, hi) + (nn(up, lo) + nn(down, hi))
        for s in range(first, first + GROUPS // 2):
            stores.append(fetch(square_ref.at[s], square_hbm.at[s], sems.at[2 * GROUPS + s]))
            if s > 0:
                at = s - 1
                stores.append(fetch(link_ref.at[at], link_hbm.at[at], sems.at[3 * GROUPS + at]))
    for store in stores:
        store.wait()


def to_row(column, eye):
    top = jnp.sum(jnp.where(eye, column[0:128], 0.0), axis=0, keepdims=True)
    bottom = jnp.sum(jnp.where(eye, column[128:256], 0.0), axis=0, keepdims=True)
    return jnp.concatenate([top, bottom], axis=1)


def to_column(row, eye):
    top = jnp.sum(jnp.where(eye, row[:, 0:128], 0.0), axis=1, keepdims=True)
    bottom = jnp.sum(jnp.where(eye, row[:, 128:256], 0.0), axis=1, keepdims=True)
    return jnp.concatenate([top, bottom], axis=0)


def apply(matrix, row, eye):
    product = matrix * row
    return to_row(jnp.sum(product[:, 0:128] + product[:, 128:256], axis=1, keepdims=True), eye)


def apply_t(matrix, row, eye):
    return jnp.sum(matrix * to_column(row, eye), axis=0, keepdims=True)


def local_links(half):
    return [7 + 4 * half + c for c in range(4)] + [3 + 2 * half + c for c in range(2)] + [1 + half]


def up_kernel(half_ref, recv_ref, link_hbm, ready_hbm, top_ref, source_ref, link_ref, sems):
    half = half_ref[0]
    loads = [
        fetch(link_hbm.at[at], link_ref.at[i], sems.at[i])
        for i, at in enumerate(local_links(half))
    ]
    eye = iota((128, 128), 0) == iota((128, 128), 1)
    sums = []
    for height in range(1, LEVELS + 1):
        count = max(8 >> height, 1)
        span = HALF // count
        left = recv_ref[pl.ds(2 * height - 2, HALF, stride=S2), :]
        right = recv_ref[pl.ds(2 * height - 1, HALF, stride=S2), :]
        for c in range(count):
            at = slice(c * span, (c + 1) * span)
            ends = [jnp.sum(part[at], axis=0, keepdims=True) for part in (left, right)]
            sums.append(jnp.concatenate(ends, axis=1))
    for load in loads:
        load.wait()
    for i in range(7):
        to = 4 + i // 2 if i < 4 else (6 if i < 6 else 7)
        sums[to] = sums[to] - apply(link_ref[i], sums[i], eye)
    top_ref[...] = jnp.concatenate(sums[7:9] + [jnp.zeros((6, LEAF), F32)], axis=0)
    source_ref[...] = jnp.concatenate(sums[0:7] + [jnp.zeros((1, LEAF), F32)], axis=0)


def square_kernel(
    half_ref, source_ref, square_hbm, link_hbm, out_ref, high_ref, square_ref, sems
):
    half = half_ref[0]
    loads = [
        fetch(square_hbm.at[at + 1], square_ref.at[i], sems.at[i])
        for i, at in enumerate(local_links(half))
    ]
    high = [
        fetch(square_hbm.at[0:2], high_ref.at[0:2], sems.at[7]),
        fetch(link_hbm.at[0], high_ref.at[2], sems.at[8]),
    ]
    eye = iota((128, 128), 0) == iota((128, 128), 1)
    for load in loads:
        load.wait()
    lines = [apply_t(square_ref[i], source_ref[i : i + 1, :], eye) for i in range(7)]
    out_ref[...] = jnp.concatenate(lines + [jnp.zeros((1, LEAF), F32)], axis=0)
    for load in high:
        load.wait()


def down_kernel(top_ref, other_ref, line_ref, link_ref, high_ref, out_ref):
    eye = iota((128, 128), 0) == iota((128, 128), 1)
    total = top_ref[...] + other_ref[...]
    below = total[0:1]
    root = total[1:2] - apply(high_ref[2], below, eye)
    root = apply_t(high_ref[0], root, eye)
    below = apply_t(high_ref[1], below, eye) - apply_t(high_ref[2], root, eye)
    line = line_ref[...]
    third = line[6:7] - apply_t(link_ref[6], below, eye)
    second = [line[4 + c : 5 + c] - apply_t(link_ref[4 + c], third, eye) for c in range(2)]
    lowest = [line[c : c + 1] - apply_t(link_ref[c], second[c // 2], eye) for c in range(4)]
    for j in range(S3):
        lines = []
        for g in range(8):
            value = (lowest[g // 2], second[g // 4], third, below, root)[j // 2]
            value = value[:, (j % 2) * 128 : (j % 2) * 128 + 128]
            lines.append(jnp.broadcast_to(value, (FRONT, 128)))
        out_ref[pl.ds(j, HALF, stride=S3), :] = jnp.concatenate(lines, axis=0)


def backward_kernel(
    home_ref,
    half_ref,
    recv_ref,
    rows_ref,
    idx_ref,
    gram_ref,
    inv_ref,
    below_ref,
    solved_hbm,
    other_hbm,
    out_ref,
    known,
    parts,
    moved,
    mark,
    result,
    solved_ref,
    other_ref,
    sems,
):
    loads = [fetch(solved_hbm, solved_ref, sems.at[0]), fetch(other_hbm, other_ref, sems.at[1])]
    for q in range(NLEAF):
        moved[:, q * LEAF : (q + 1) * LEAF] = mark_row(rows_ref[q : q + 1, :], PATH, 0)
    for j in range(S3):
        chunk = crossed(recv_ref[pl.ds(j, HALF, stride=S3), :], half_ref[0])
        known[:, j * 128 : (j + 1) * 128] = chunk
        parts[:, j * 128 : (j + 1) * 128] = stacked(chunk)
    picked = folded(nn(parts[...], moved[...]))
    for load in loads:
        load.wait()
    start = home_ref[0]
    tile = pl.multiple_of((start // 128) * 128, 128)
    home = pltpu.roll(known[:, pl.ds(tile, 128)], (128 - start % 128) % 128, 1)
    home = jnp.where(iota((64, 128), 1) < SHARE, home, 0.0)
    result[:, SPAN:PAD] = stacked(home)
    for q in range(NLEAF):
        cols = slice(q * LEAF, (q + 1) * LEAF)
        hi, lo = split(below_ref[q])
        rows = stacked(picked[:, cols])
        source = stacked(solved_ref[:, cols] - folded(nn(rows, hi) + nn(rows, lo)))
        hi, lo = split(inv_ref[q])
        result[:, cols] = stacked(folded(nn(source, hi) + nn(source, lo)))
    cross = folded(nt(result[...], other_ref[...]))
    cross = cross[:, 0:128] + cross[:, 128:256]
    square = both(folded(nt(result[...], result[...])))
    slots = idx_ref[...].astype(jnp.int32)
    for k in range(CAP):
        mark[:, k * DEV : (k + 1) * DEV] = mark_row(slots[k : k + 1, :], PAD, 0)
    packed = folded(nn(result[...], mark[...]))
    for j in range(8):
        pair = [packed[:, k * DEV : (k + 1) * DEV] for k in (2 * j, 2 * j + 1)]
        out_ref[pl.ds(j, DEV, stride=S4), :] = jnp.concatenate(pair, axis=0).T
    last = packed[:, 16 * DEV : 17 * DEV]
    last = jnp.concatenate([last, last], axis=0).T
    low = iota((DEV, 128), 1) < 64
    out_ref[pl.ds(8, DEV, stride=S4), :] = jnp.where(low, last, 0.0)
    late = jnp.where(low[0:64], square, gram_ref[64:128, :])
    for i, block in enumerate((cross, gram_ref[0:64, :], late)):
        out_ref[pl.ds(9 + i, DEV, stride=S4), :] = jnp.concatenate([block, block], axis=0)


def total_kernel(recv_ref, out_ref):
    for i in range(S5):
        line = jnp.sum(recv_ref[pl.ds(9 + i, DEV, stride=S4), :], axis=0, keepdims=True)
        out_ref[pl.ds(i, HALF, stride=S5), :] = jnp.broadcast_to(line, (HALF, 128))


def unpack_kernel(key_ref, recv_ref, out_ref, mark, value):
    for k in range(CAP):
        mark[k * DEV : (k + 1) * DEV, :] = mark_row(key_ref[...], DEV, k * DEV)
    for j in range(9):
        got = recv_ref[pl.ds(j, DEV, stride=S4), :].T
        value[:, 2 * j * DEV : (2 * j + 1) * DEV] = stacked(got[0:64])
        if j < 8:
            value[:, (2 * j + 1) * DEV : (2 * j + 2) * DEV] = stacked(got[64:128])
    out_ref[...] = folded(nn(value[...], mark[...]))[:, 0:ROWS]


def finish_kernel(
    recv_ref, solved_ref, now_ref, before_ref, coupling_ref, proj_ref, factor_ref, next_ref, value
):
    count = 1.0 / (ROWS * DEV)
    cross, own, late = [recv_ref[pl.ds(i, HALF, stride=S5), :] * count for i in range(S5)]
    s_b, s_a = cross[:, 0:64], cross[:, 64:128]
    b_b, b_a = own[:, 0:64], own[:, 64:128]
    s_s, a_a = late[:, 0:64], late[:, 64:128]
    coupling = coupling_ref[...]
    proj_ref[...] = s_b.T
    line_s = s_s - nt32(s_b, s_b) - nt32(coupling, s_a)
    line_b = s_b - nn32(s_b, b_b) - nt32(coupling, b_a)
    line_a = s_a - nn32(s_b, b_a) - nn32(coupling, a_a)
    gram = line_s - nt32(line_b, s_b) - nt32(line_a, coupling)
    eye = iota((64, 64), 0) == iota((64, 64), 1)
    work = jnp.concatenate([gram, jnp.where(eye, 1.0, 0.0)], axis=1)
    done = []
    for b in range(4):
        height = 64 - 16 * b
        at = 16 * b
        columns = [
            jnp.broadcast_to(work[:, at + c : at + c + 1], (height, 128)) for c in range(16)
        ]
        below = iota((height, 128), 0)
        for c in range(16):
            ratio = jnp.where(below > c, columns[c] * (1.0 / columns[c][c : c + 1, :]), 0.0)
            work = work - ratio * work[c : c + 1, :]
            for e in range(c + 1, 16):
                columns[e] = columns[e] - ratio * columns[e][c : c + 1, :]
        done.append(work[0:16])
        work = work[16:]
    work = jnp.concatenate(done, axis=0)
    scale = lax.rsqrt(jnp.sum(jnp.where(eye, work[:, 0:64], 0.0), axis=1, keepdims=True))
    work = work * scale
    factor_ref[...] = jnp.where(iota((64, 64), 0) <= iota((64, 64), 1), work[:, 0:64], 0.0)
    inverse = work[:, 64:128]
    weight = jnp.concatenate(
        [inverse, -nn32(inverse, s_b), -nn32(inverse, coupling)], axis=1
    )
    hi, lo = split(weight)
    weight = jnp.concatenate([hi, lo], axis=0)
    for b, ref in enumerate((solved_ref, now_ref, before_ref)):
        hi, lo = split(ref[...])
        value[b * 64 : (b + 1) * 64, 0:ROWS] = hi
        value[b * 64 : (b + 1) * 64, PAD : PAD + ROWS] = lo
    total = nn(weight, value[:, 0:ROWS]) + nn(weight, value[:, PAD : PAD + ROWS])
    next_ref[...] = folded(total)


def call(kernel, outs, operands, scratch=(), scalars=0, far=0, far_outs=(), limit=52, micros=4):
    kinds = [pltpu.SMEM] * scalars + [pltpu.VMEM] * (len(operands) - scalars - far)
    kinds += [pltpu.HBM] * far
    return pl.pallas_call(
        kernel,
        out_shape=[jax.ShapeDtypeStruct(shape, dtype) for shape, dtype in outs],
        in_specs=[pl.BlockSpec(memory_space=kind) for kind in kinds],
        out_specs=[
            pl.BlockSpec(memory_space=pltpu.HBM if i in far_outs else pltpu.VMEM)
            for i in range(len(outs))
        ],
        scratch_shapes=list(scratch),
        cost_estimate=pl.CostEstimate(
            flops=micros * 1000000000, bytes_accessed=micros * 3000000, transcendentals=0
        ),
        compiler_params=pltpu.CompilerParams(vmem_limit_bytes=limit * MIB),
    )(*operands)


def exchange(x, lines, axes=AXES):
    peers = x.shape[0] // lines
    return lax.all_to_all(
        x.reshape(peers, 1, lines * 128), axes, split_axis=0, concat_axis=0, tiled=True
    ).reshape(peers * lines, 128)


def per_device(
    block_now,
    block_before,
    coupling,
    vertex_to_tree,
    tree_to_vertex,
    leaf_inverse,
    leaf_below,
    leaf_rows,
    sep_inverse,
    sep_parent,
):
    my_half = lax.axis_index("half")
    my_group = my_half * 8 + lax.axis_index("group")
    my_front = lax.axis_index("front")
    home_slot = jnp.zeros((), jnp.int32)
    for bit in range(LEVELS - 1):
        home_slot = home_slot + (my_group % (2 << bit) == 0).astype(jnp.int32)
    home_at = (home_slot * LEAF + my_front * SHARE).astype(jnp.int32).reshape(1)
    half = my_half.astype(jnp.int32).reshape(1)
    V = pltpu.VMEM
    S = pltpu.SemaphoreType.DMA
    packed, key = call(
        pack_kernel,
        [((DEV * S1, 128), F32), ((1, PAD), jnp.int32)],
        (vertex_to_tree, block_now, block_before),
        [
            V((8, PAD), jnp.int32),
            V((DEV, PAD), BF16),
            V((256, PAD), BF16),
            V((PAD, PAD), BF16),
            V((64, ROWS), F32),
            V((64, ROWS), F32),
            S((2,)),
        ],
        far=2,
        limit=58,
    )
    arrived = exchange(packed, S1)
    square, link = call(
        prepare_kernel,
        [((GROUPS, LEAF, LEAF), F32), ((GROUPS - 1, LEAF, LEAF), F32)],
        (sep_inverse, sep_parent),
        [
            V((GROUPS, LEAF, LEAF), F32),
            V((GROUPS - 1, LEAF, LEAF), F32),
            V((GROUPS, LEAF, LEAF), F32),
            V((GROUPS - 1, LEAF, LEAF), F32),
            S((4 * GROUPS,)),
        ],
        far=2,
        far_outs=(0, 1),
    )
    pushed, leaf_solved, tree = call(
        forward_kernel,
        [((HALF * S2, 128), F32), ((64, SPAN), F32), ((64, PAD), F32)],
        (home_at, half, arrived, leaf_rows, leaf_inverse, leaf_below, link),
        [
            V((PAD, PAD), BF16),
            V((128, PAD), BF16),
            V((SPAN, PATH), BF16),
            V((128, SPAN), BF16),
            V((NLEAF, LEAF, LEAF), F32),
            V((NLEAF, LEAF, LEAF), F32),
            V((64, SPAN), F32),
            V((64, PAD), F32),
            S((20,)),
        ],
        2,
        far=3,
        limit=50,
        far_outs=(1, 2),
    )
    pushed = exchange(pushed, S2, NEAR)
    other, idx, gram = call(
        side_kernel,
        [((256, PAD), BF16), ((128, 128), F32), ((128, 128), F32)],
        (arrived, tree),
        [
            V((PAD, PAD), BF16),
            V((128, PAD), BF16),
            V((64, PAD), F32),
            V((256, PAD), BF16),
            S((2,)),
        ],
        far=1,
        far_outs=(0,),
    )
    small = ((8, LEAF), F32)
    top, source, links = call(
        up_kernel,
        [small, small, ((7, LEAF, LEAF), F32)],
        (half, pushed, link, other),
        [S((7,))],
        1,
        far=2,
        limit=50,
    )
    across = [(i, i ^ 12) for i in range(GROUPS)]
    other_top = lax.ppermute(top, ("half", "group"), across)
    line, high = call(
        square_kernel,
        [small, ((3, LEAF, LEAF), F32)],
        (half, source, square, link),
        [V((7, LEAF, LEAF), F32), S((9,))],
        1,
        far=2,
        limit=50,
        micros=2,
    )
    (paths,) = call(
        down_kernel,
        [((HALF * S3, 128), F32)],
        (top, other_top, line, links, high),
        limit=50,
    )
    paths = exchange(paths, S3, NEAR)
    (returning,) = call(
        backward_kernel,
        [((DEV * S4, 128), F32)],
        (
            home_at,
            half,
            paths,
            leaf_rows,
            idx,
            gram,
            leaf_inverse,
            leaf_below,
            leaf_solved,
            other,
        ),
        [
            V((64, PATH), F32),
            V((128, PATH), BF16),
            V((PATH, SPAN), BF16),
            V((PAD, PAD), BF16),
            V((128, PAD), BF16),
            V((64, SPAN), F32),
            V((256, PAD), BF16),
            S((2,)),
        ],
        2,
        far=2,
        limit=46,
    )
    returned = exchange(returning, S4)
    (sums,) = call(total_kernel, [((HALF * S5, 128), F32)], (returned,), micros=1)
    sums = exchange(sums, S5, NEAR)
    (solved,) = call(
        unpack_kernel,
        [((64, ROWS), F32)],
        (key, returned),
        [V((PAD, PAD), BF16), V((128, PAD), BF16)],
    )
    return tuple(
        call(
            finish_kernel,
            [((64, 64), F32), ((64, 64), F32), ((64, ROWS), F32)],
            (sums, solved, block_now, block_before, coupling),
            [V((192, 2 * PAD), BF16)],
        )
    )


def solution(mesh):
    placed = (
        P(None, AXES),
        P(None, AXES),
        P(),
        P(AXES),
        P(AXES),
        P(AXES, None, None),
        P(AXES, None, None),
        P(AXES, None),
        P(),
        P(),
    )
    split_mesh = Mesh(mesh.devices.reshape(2, 8, 8), AXES)
    return jax.shard_map(
        per_device,
        mesh=split_mesh,
        in_specs=placed,
        out_specs=(P(), P(), P(None, AXES)),
        check_vma=False,
    )
```

```python
import jax
import jax.numpy as jnp
from jax import lax
from jax.experimental import pallas as pl
from jax.experimental.pallas import tpu as pltpu
from jax.sharding import Mesh
from jax.sharding import PartitionSpec as P

F32 = jnp.float32
BF16 = jnp.bfloat16
HIGHEST = lax.Precision.HIGHEST
AXES = ("half", "group", "front")
NEAR = ("group", "front")
HALF = 64
DEV = 128
CAP = 17
ROWS = 2080
PAD = 2176
VEC = 64
LEAF = 256
NLEAF = 8
SPAN = 2048
GROUPS = 16
FRONT = 8
SHARE = 32
LEVELS = 5
PATH = 1280
S1 = 18
S2 = 10
S3 = 10
S4 = 10
MIB = 1024 * 1024


def nn(a, b):
    return lax.dot_general(a, b, (((1,), (0,)), ((), ())), preferred_element_type=F32)


def nt(a, b):
    return lax.dot_general(a, b, (((1,), (1,)), ((), ())), preferred_element_type=F32)


def tn(a, b):
    return lax.dot_general(a, b, (((0,), (0,)), ((), ())), preferred_element_type=F32)


def nn32(a, b):
    return lax.dot_general(
        a, b, (((1,), (0,)), ((), ())), preferred_element_type=F32, precision=HIGHEST
    )


def nt32(a, b):
    return lax.dot_general(
        a, b, (((1,), (1,)), ((), ())), preferred_element_type=F32, precision=HIGHEST
    )


def split(x):
    hi = x.astype(BF16)
    lo = (x - hi.astype(F32)).astype(BF16)
    return hi, lo


def iota(shape, dim):
    return lax.broadcasted_iota(jnp.int32, shape, dim)


I16 = jnp.int16


def onehot(mask):
    return jnp.where(mask, jnp.ones((), BF16), jnp.zeros((), BF16))


def onehot32(mask):
    return jnp.where(mask, 1.0, 0.0).astype(BF16)


def mark_row(row, height, start):
    width = row.shape[1]
    wide = jnp.broadcast_to(row, (16, width)).astype(I16)
    wide = jnp.concatenate([wide] * (height // 16), axis=0)
    return onehot(wide == (iota((height, width), 0) + start).astype(I16))


def mark_column(column, width):
    height = column.shape[0]
    wide = jnp.broadcast_to(column, (height, 128)).astype(I16)
    wide = jnp.concatenate([wide] * (width // 128), axis=1)
    return onehot(wide == iota((height, width), 1).astype(I16))


def stacked(x):
    hi, lo = split(x)
    return jnp.concatenate([hi, lo], axis=0)


def both(x):
    return x + pltpu.roll(x, 64, 1)


def crossed(x, half):
    return jnp.where(half == 1, jnp.concatenate([x[32:64], x[0:32]], axis=0), x)


def folded(x):
    half = x.shape[0] // 2
    return x[0:half] + x[half:]


def fetch(source, target, sem):
    copy = pltpu.make_async_copy(source, target, sem)
    copy.start()
    return copy


def pack_kernel(
    vt_ref, now_hbm, before_hbm, out_ref, key_ref, dest, member, value, mark, now, before, sems
):
    loads = [fetch(now_hbm, now, sems.at[0]), fetch(before_hbm, before, sems.at[1])]
    dest[...] = jnp.full((8, PAD), -1, jnp.int32)
    dest[0:1, 0:ROWS] = vt_ref[...].reshape(1, ROWS)
    target = dest[0:1, :]
    bucket = ((target.astype(F32) + 0.5) * (1.0 / ROWS)).astype(jnp.int32)
    bucket = jnp.where(target < 0, -1, bucket)
    place = target - bucket * ROWS
    member[...] = mark_row(bucket, DEV, 0)
    earlier = onehot32(
        (iota((128, 256), 0) < iota((128, 256), 1)) | (iota((128, 256), 1) >= 128)
    )
    carry = jnp.zeros((DEV, 128), F32)
    ranks = []
    for b in range(CAP):
        part = member[:, b * 128 : (b + 1) * 128]
        counts = nn(part, earlier)
        ranks.append(
            jnp.sum(part.astype(F32) * (counts[:, 0:128] + carry), axis=0, keepdims=True)
        )
        carry = carry + counts[:, 128:256]
    rank = jnp.concatenate(ranks, axis=1).astype(jnp.int32)
    key = jnp.where(target < 0, -1, rank * DEV + bucket)
    for k in range(8):
        mark[k * DEV : (k + 1) * DEV, :] = mark_row(key, DEV, k * DEV)
    for load in loads:
        load.wait()
    value[:, SPAN:PAD] = jnp.zeros((4 * VEC, PAD - SPAN), BF16)
    now_hi, now_lo = split(now[...])
    bef_hi, bef_lo = split(before[...])
    value[0:64, 0:ROWS] = now_hi
    value[64:128, 0:ROWS] = bef_hi
    value[128:192, 0:ROWS] = now_lo
    value[192:256, 0:ROWS] = bef_lo
    key_ref[...] = key
    for k in range(8, CAP):
        mark[k * DEV : (k + 1) * DEV, :] = mark_row(key, DEV, k * DEV)
    block = nt(mark[...], value[...])
    block = block[:, 0:128] + block[:, 128:256]
    for k in range(CAP):
        out_ref[pl.ds(k, DEV, stride=S1), :] = block[k * DEV : (k + 1) * DEV]
    ranked = jnp.broadcast_to(rank, (32, PAD)) == iota((32, PAD), 0)
    high = place // 64
    marks = jnp.concatenate(
        [
            jnp.where(ranked, jnp.broadcast_to(high, (32, PAD)).astype(F32), 0.0),
            jnp.where(ranked, jnp.broadcast_to(place - high * 64, (32, PAD)).astype(F32), 0.0),
            jnp.zeros((64, PAD), F32),
        ],
        axis=0,
    ).astype(BF16)
    found = nt(member[...], marks)
    where = found * 64.0 + pltpu.roll(found, 96, 1)
    lane = iota((DEV, 128), 1)
    filled = (lane.astype(F32) < carry) & (lane < CAP)
    out_ref[pl.ds(CAP, DEV, stride=S1), :] = jnp.where(filled, where, -1.0)


def forward_kernel(
    home_ref,
    half_ref,
    recv_ref,
    rows_ref,
    inv_hbm,
    below_hbm,
    ready_hbm,
    out_ref,
    solved_hbm,
    tree_hbm,
    mark,
    value,
    moved,
    update,
    inv_ref,
    below_ref,
    solved_ref,
    tree_ref,
    sems,
):
    loads = []
    for q in range(NLEAF):
        loads.append(fetch(inv_hbm.at[q], inv_ref.at[q], sems.at[4 + q]))
        loads.append(fetch(below_hbm.at[q], below_ref.at[q], sems.at[12 + q]))
    idx = recv_ref[pl.ds(CAP, DEV, stride=S1), :].astype(jnp.int32)
    for k in range(CAP):
        got = recv_ref[pl.ds(k, DEV, stride=S1), :].T
        value[:, k * DEV : (k + 1) * DEV] = stacked(got[0:64])
        mark[k * DEV : (k + 1) * DEV, :] = mark_column(idx[:, k : k + 1], PAD)
    tree_ref[...] = folded(nn(value[...], mark[...]))
    stores = [fetch(tree_ref, tree_hbm, sems.at[2])]
    rows = rows_ref[...].astype(F32).T.astype(jnp.int32)
    for q in range(NLEAF):
        moved[q * LEAF : (q + 1) * LEAF, :] = mark_column(rows[:, q : q + 1], PATH)
    for load in loads:
        load.wait()
    for q in range(NLEAF):
        cols = slice(q * LEAF, (q + 1) * LEAF)
        hi, lo = split(inv_ref[q])
        source = stacked(tree_ref[:, cols])
        solved = folded(nt(source, hi) + nt(source, lo))
        solved_ref[:, cols] = solved
        hi, lo = split(below_ref[q])
        solved = stacked(solved)
        update[:, cols] = stacked(folded(nt(solved, hi) + nt(solved, lo)))
    stores.append(fetch(solved_ref, solved_hbm, sems.at[3]))
    pushed = folded(nn(update[...], moved[...]))
    start = home_ref[0]
    own = pltpu.roll(tree_ref[:, SPAN:PAD], start % 128, 1)
    for j in range(S2):
        chunk = jnp.where(start // 128 == j, own, 0.0) - pushed[:, j * 128 : (j + 1) * 128]
        out_ref[pl.ds(j, HALF, stride=S2), :] = crossed(chunk, half_ref[0])
    for store in stores:
        store.wait()


def side_kernel(
    recv_ref, tree_hbm, other_hbm, idx_ref, gram_ref, mark, value, tree_ref, other_ref, sems
):
    load = fetch(tree_hbm, tree_ref, sems.at[0])
    where = recv_ref[pl.ds(CAP, DEV, stride=S1), :]
    idx_ref[...] = where.T
    idx = where.astype(jnp.int32)
    for k in range(CAP):
        got = recv_ref[pl.ds(k, DEV, stride=S1), :].T
        value[:, k * DEV : (k + 1) * DEV] = stacked(got[64:128])
        mark[k * DEV : (k + 1) * DEV, :] = mark_column(idx[:, k : k + 1], PAD)
    before = folded(nn(value[...], mark[...]))
    load.wait()
    hi, lo = split(tree_ref[...])
    other_ref[0:64, :] = hi
    other_ref[128:192, :] = lo
    hi, lo = split(before)
    other_ref[64:128, :] = hi
    other_ref[192:256, :] = lo
    store = fetch(other_ref, other_hbm, sems.at[1])
    gram = folded(nt(other_ref[...], other_ref[...]))
    gram_ref[...] = gram[:, 0:128] + gram[:, 128:256]
    store.wait()


def prepare_kernel(
    inv_hbm, parent_hbm, square_hbm, link_hbm, inv_ref, parent_ref, square_ref, link_ref, sems
):
    inv_loads = []
    parent_loads = []
    stores = []
    for s in range(GROUPS):
        inv_loads.append(fetch(inv_hbm.at[s], inv_ref.at[s], sems.at[s]))
        if s > 0:
            at = s - 1
            parent_loads.append(
                fetch(parent_hbm.at[at], parent_ref.at[at], sems.at[GROUPS + at])
            )
    for first in (0, GROUPS // 2):
        for s in range(first, first + GROUPS // 2):
            inv_loads[s].wait()
            if s > 0:
                parent_loads[s - 1].wait()
        for s in range(first, first + GROUPS // 2):
            hi, lo = split(inv_ref[s])
            square_ref[s] = tn(hi, hi) + (tn(hi, lo) + tn(lo, hi))
            if s > 0:
                up, down = split(parent_ref[s - 1])
                link_ref[s - 1] = nn(up, hi) + (nn(up, lo) + nn(down, hi))
        for s in range(first, first + GROUPS // 2):
            stores.append(fetch(square_ref.at[s], square_hbm.at[s], sems.at[2 * GROUPS + s]))
            if s > 0:
                at = s - 1
                stores.append(fetch(link_ref.at[at], link_hbm.at[at], sems.at[3 * GROUPS + at]))
    for store in stores:
        store.wait()


def to_row(column, eye):
    top = jnp.sum(jnp.where(eye, column[0:128], 0.0), axis=0, keepdims=True)
    bottom = jnp.sum(jnp.where(eye, column[128:256], 0.0), axis=0, keepdims=True)
    return jnp.concatenate([top, bottom], axis=1)


def to_column(row, eye):
    top = jnp.sum(jnp.where(eye, row[:, 0:128], 0.0), axis=1, keepdims=True)
    bottom = jnp.sum(jnp.where(eye, row[:, 128:256], 0.0), axis=1, keepdims=True)
    return jnp.concatenate([top, bottom], axis=0)


def apply(matrix, row, eye):
    product = matrix * row
    return to_row(jnp.sum(product[:, 0:128] + product[:, 128:256], axis=1, keepdims=True), eye)


def apply_t(matrix, row, eye):
    return jnp.sum(matrix * to_column(row, eye), axis=0, keepdims=True)


def local_links(half):
    return [7 + 4 * half + c for c in range(4)] + [3 + 2 * half + c for c in range(2)] + [1 + half]


def up_kernel(half_ref, recv_ref, link_hbm, ready_hbm, top_ref, source_ref, link_ref, sems):
    half = half_ref[0]
    loads = [
        fetch(link_hbm.at[at], link_ref.at[i], sems.at[i])
        for i, at in enumerate(local_links(half))
    ]
    eye = iota((128, 128), 0) == iota((128, 128), 1)
    sums = []
    for height in range(1, LEVELS + 1):
        count = max(8 >> height, 1)
        span = HALF // count
        left = recv_ref[pl.ds(2 * height - 2, HALF, stride=S2), :]
        right = recv_ref[pl.ds(2 * height - 1, HALF, stride=S2), :]
        for c in range(count):
            at = slice(c * span, (c + 1) * span)
            ends = [jnp.sum(part[at], axis=0, keepdims=True) for part in (left, right)]
            sums.append(jnp.concatenate(ends, axis=1))
    for load in loads:
        load.wait()
    for i in range(7):
        to = 4 + i // 2 if i < 4 else (6 if i < 6 else 7)
        sums[to] = sums[to] - apply(link_ref[i], sums[i], eye)
    top_ref[...] = jnp.concatenate(sums[7:9] + [jnp.zeros((6, LEAF), F32)], axis=0)
    source_ref[...] = jnp.concatenate(sums[0:7] + [jnp.zeros((1, LEAF), F32)], axis=0)


def square_kernel(
    half_ref, source_ref, square_hbm, link_hbm, out_ref, high_ref, square_ref, sems
):
    half = half_ref[0]
    loads = [
        fetch(square_hbm.at[at + 1], square_ref.at[i], sems.at[i])
        for i, at in enumerate(local_links(half))
    ]
    high = [
        fetch(square_hbm.at[0:2], high_ref.at[0:2], sems.at[7]),
        fetch(link_hbm.at[0], high_ref.at[2], sems.at[8]),
    ]
    eye = iota((128, 128), 0) == iota((128, 128), 1)
    for load in loads:
        load.wait()
    lines = [apply_t(square_ref[i], source_ref[i : i + 1, :], eye) for i in range(7)]
    out_ref[...] = jnp.concatenate(lines + [jnp.zeros((1, LEAF), F32)], axis=0)
    for load in high:
        load.wait()


def down_kernel(top_ref, other_ref, line_ref, link_ref, high_ref, out_ref):
    eye = iota((128, 128), 0) == iota((128, 128), 1)
    total = top_ref[...] + other_ref[...]
    below = total[0:1]
    root = total[1:2] - apply(high_ref[2], below, eye)
    root = apply_t(high_ref[0], root, eye)
    below = apply_t(high_ref[1], below, eye) - apply_t(high_ref[2], root, eye)
    line = line_ref[...]
    third = line[6:7] - apply_t(link_ref[6], below, eye)
    second = [line[4 + c : 5 + c] - apply_t(link_ref[4 + c], third, eye) for c in range(2)]
    lowest = [line[c : c + 1] - apply_t(link_ref[c], second[c // 2], eye) for c in range(4)]
    for j in range(S3):
        lines = []
        for g in range(8):
            value = (lowest[g // 2], second[g // 4], third, below, root)[j // 2]
            value = value[:, (j % 2) * 128 : (j % 2) * 128 + 128]
            lines.append(jnp.broadcast_to(value, (FRONT, 128)))
        out_ref[pl.ds(j, HALF, stride=S3), :] = jnp.concatenate(lines, axis=0)


def backward_kernel(
    home_ref,
    half_ref,
    recv_ref,
    rows_ref,
    idx_ref,
    gram_ref,
    inv_ref,
    below_ref,
    solved_hbm,
    other_hbm,
    out_ref,
    known,
    parts,
    moved,
    mark,
    result,
    solved_ref,
    other_ref,
    sems,
):
    loads = [fetch(solved_hbm, solved_ref, sems.at[0]), fetch(other_hbm, other_ref, sems.at[1])]
    for q in range(NLEAF):
        moved[:, q * LEAF : (q + 1) * LEAF] = mark_row(rows_ref[q : q + 1, :], PATH, 0)
    for j in range(S3):
        chunk = crossed(recv_ref[pl.ds(j, HALF, stride=S3), :], half_ref[0])
        known[:, j * 128 : (j + 1) * 128] = chunk
        parts[:, j * 128 : (j + 1) * 128] = stacked(chunk)
    for load in loads:
        load.wait()
    picked = folded(nn(parts[...], moved[...]))
    start = home_ref[0]
    tile = pl.multiple_of((start // 128) * 128, 128)
    home = pltpu.roll(known[:, pl.ds(tile, 128)], (128 - start % 128) % 128, 1)
    home = jnp.where(iota((64, 128), 1) < SHARE, home, 0.0)
    result[:, SPAN:PAD] = stacked(home)
    for q in range(NLEAF):
        cols = slice(q * LEAF, (q + 1) * LEAF)
        hi, lo = split(below_ref[q])
        rows = stacked(picked[:, cols])
        source = stacked(solved_ref[:, cols] - folded(nn(rows, hi) + nn(rows, lo)))
        hi, lo = split(inv_ref[q])
        result[:, cols] = stacked(folded(nn(source, hi) + nn(source, lo)))
    cross = folded(nt(result[...], other_ref[...]))
    cross = cross[:, 0:128] + cross[:, 128:256]
    square = both(folded(nt(result[...], result[...])))
    slots = idx_ref[...].astype(jnp.int32)
    for k in range(CAP):
        mark[:, k * DEV : (k + 1) * DEV] = mark_row(slots[k : k + 1, :], PAD, 0)
    packed = folded(nn(result[...], mark[...]))
    for j in range(8):
        pair = [packed[:, k * DEV : (k + 1) * DEV] for k in (2 * j, 2 * j + 1)]
        out_ref[pl.ds(j, DEV, stride=S4), :] = jnp.concatenate(pair, axis=0).T
    last = packed[:, 16 * DEV : 17 * DEV]
    last = jnp.concatenate([last, last], axis=0).T
    late = jnp.concatenate([square, gram_ref[64:128, :]], axis=0)
    out_ref[pl.ds(8, DEV, stride=S4), :] = jnp.where(iota((DEV, 128), 1) < 64, last, late)
    out_ref[pl.ds(9, DEV, stride=S4), :] = jnp.concatenate([cross, gram_ref[0:64, :]], axis=0)


def total_kernel(recv_ref, out_ref):
    first = jnp.sum(recv_ref[pl.ds(9, DEV, stride=S4), :], axis=0, keepdims=True)
    second = jnp.sum(recv_ref[pl.ds(8, DEV, stride=S4), :], axis=0, keepdims=True)
    out_ref[pl.ds(0, DEV, stride=2), :] = jnp.broadcast_to(first, (DEV, 128))
    out_ref[pl.ds(1, DEV, stride=2), :] = jnp.broadcast_to(second, (DEV, 128))


def unpack_kernel(key_ref, recv_ref, out_ref, mark, value):
    for k in range(CAP):
        mark[k * DEV : (k + 1) * DEV, :] = mark_row(key_ref[...], DEV, k * DEV)
    for j in range(9):
        got = recv_ref[pl.ds(j, DEV, stride=S4), :].T
        value[:, 2 * j * DEV : (2 * j + 1) * DEV] = stacked(got[0:64])
        if j < 8:
            value[:, (2 * j + 1) * DEV : (2 * j + 2) * DEV] = stacked(got[64:128])
    out_ref[...] = folded(nn(value[...], mark[...]))[:, 0:ROWS]


def finish_kernel(
    recv_ref, solved_ref, now_ref, before_ref, coupling_ref, proj_ref, factor_ref, next_ref, value
):
    first = recv_ref[pl.ds(0, DEV, stride=2), :]
    second = recv_ref[pl.ds(1, DEV, stride=2), :]
    count = 1.0 / (ROWS * DEV)
    s_b = first[0:64, 0:64] * count
    s_a = first[0:64, 64:128] * count
    b_b = first[64:128, 0:64] * count
    b_a = first[64:128, 64:128] * count
    s_s = second[0:64, 64:128] * count
    a_a = second[64:128, 64:128] * count
    coupling = coupling_ref[...]
    proj_ref[...] = s_b.T
    line_s = s_s - nt32(s_b, s_b) - nt32(coupling, s_a)
    line_b = s_b - nn32(s_b, b_b) - nt32(coupling, b_a)
    line_a = s_a - nn32(s_b, b_a) - nn32(coupling, a_a)
    gram = line_s - nt32(line_b, s_b) - nt32(line_a, coupling)
    eye = iota((64, 64), 0) == iota((64, 64), 1)
    work = jnp.concatenate([gram, jnp.where(eye, 1.0, 0.0)], axis=1)
    done = []
    for b in range(4):
        height = 64 - 16 * b
        at = 16 * b
        columns = [
            jnp.broadcast_to(work[:, at + c : at + c + 1], (height, 128)) for c in range(16)
        ]
        below = iota((height, 128), 0)
        for c in range(16):
            ratio = jnp.where(below > c, columns[c] * (1.0 / columns[c][c : c + 1, :]), 0.0)
            work = work - ratio * work[c : c + 1, :]
            for e in range(c + 1, 16):
                columns[e] = columns[e] - ratio * columns[e][c : c + 1, :]
        done.append(work[0:16])
        work = work[16:]
    work = jnp.concatenate(done, axis=0)
    scale = lax.rsqrt(jnp.sum(jnp.where(eye, work[:, 0:64], 0.0), axis=1, keepdims=True))
    work = work * scale
    factor_ref[...] = jnp.where(iota((64, 64), 0) <= iota((64, 64), 1), work[:, 0:64], 0.0)
    inverse = work[:, 64:128]
    weight = jnp.concatenate(
        [inverse, -nn32(inverse, s_b), -nn32(inverse, coupling)], axis=1
    )
    hi, lo = split(weight)
    weight = jnp.concatenate([hi, lo], axis=0)
    for b, ref in enumerate((solved_ref, now_ref, before_ref)):
        hi, lo = split(ref[...])
        value[b * 64 : (b + 1) * 64, 0:ROWS] = hi
        value[b * 64 : (b + 1) * 64, PAD : PAD + ROWS] = lo
    total = nn(weight, value[:, 0:ROWS]) + nn(weight, value[:, PAD : PAD + ROWS])
    next_ref[...] = folded(total)


def call(kernel, outs, operands, scratch=(), scalars=0, far=0, far_outs=(), limit=52, micros=4):
    kinds = [pltpu.SMEM] * scalars + [pltpu.VMEM] * (len(operands) - scalars - far)
    kinds += [pltpu.HBM] * far
    return pl.pallas_call(
        kernel,
        out_shape=[jax.ShapeDtypeStruct(shape, dtype) for shape, dtype in outs],
        in_specs=[pl.BlockSpec(memory_space=kind) for kind in kinds],
        out_specs=[
            pl.BlockSpec(memory_space=pltpu.HBM if i in far_outs else pltpu.VMEM)
            for i in range(len(outs))
        ],
        scratch_shapes=list(scratch),
        cost_estimate=pl.CostEstimate(
            flops=micros * 1000000000, bytes_accessed=micros * 3000000, transcendentals=0
        ),
        compiler_params=pltpu.CompilerParams(vmem_limit_bytes=limit * MIB),
    )(*operands)


def exchange(x, lines, axes=AXES):
    peers = x.shape[0] // lines
    return lax.all_to_all(
        x.reshape(peers, 1, lines * 128), axes, split_axis=0, concat_axis=0, tiled=True
    ).reshape(peers * lines, 128)


def per_device(
    block_now,
    block_before,
    coupling,
    vertex_to_tree,
    tree_to_vertex,
    leaf_inverse,
    leaf_below,
    leaf_rows,
    sep_inverse,
    sep_parent,
):
    my_half = lax.axis_index("half")
    my_group = my_half * 8 + lax.axis_index("group")
    my_front = lax.axis_index("front")
    home_slot = jnp.zeros((), jnp.int32)
    for bit in range(LEVELS - 1):
        home_slot = home_slot + (my_group % (2 << bit) == 0).astype(jnp.int32)
    home_at = (home_slot * LEAF + my_front * SHARE).astype(jnp.int32).reshape(1)
    half = my_half.astype(jnp.int32).reshape(1)
    V = pltpu.VMEM
    S = pltpu.SemaphoreType.DMA
    packed, key = call(
        pack_kernel,
        [((DEV * S1, 128), F32), ((1, PAD), jnp.int32)],
        (vertex_to_tree, block_now, block_before),
        [
            V((8, PAD), jnp.int32),
            V((DEV, PAD), BF16),
            V((256, PAD), BF16),
            V((PAD, PAD), BF16),
            V((64, ROWS), F32),
            V((64, ROWS), F32),
            S((2,)),
        ],
        far=2,
        limit=58,
    )
    arrived = exchange(packed, S1)
    square, link = call(
        prepare_kernel,
        [((GROUPS, LEAF, LEAF), F32), ((GROUPS - 1, LEAF, LEAF), F32)],
        (sep_inverse, sep_parent),
        [
            V((GROUPS, LEAF, LEAF), F32),
            V((GROUPS - 1, LEAF, LEAF), F32),
            V((GROUPS, LEAF, LEAF), F32),
            V((GROUPS - 1, LEAF, LEAF), F32),
            S((4 * GROUPS,)),
        ],
        far=2,
        far_outs=(0, 1),
    )
    pushed, leaf_solved, tree = call(
        forward_kernel,
        [((HALF * S2, 128), F32), ((64, SPAN), F32), ((64, PAD), F32)],
        (home_at, half, arrived, leaf_rows, leaf_inverse, leaf_below, link),
        [
            V((PAD, PAD), BF16),
            V((128, PAD), BF16),
            V((SPAN, PATH), BF16),
            V((128, SPAN), BF16),
            V((NLEAF, LEAF, LEAF), F32),
            V((NLEAF, LEAF, LEAF), F32),
            V((64, SPAN), F32),
            V((64, PAD), F32),
            S((20,)),
        ],
        2,
        far=3,
        limit=50,
        far_outs=(1, 2),
    )
    pushed = exchange(pushed, S2, NEAR)
    other, idx, gram = call(
        side_kernel,
        [((256, PAD), BF16), ((128, 128), F32), ((128, 128), F32)],
        (arrived, tree),
        [
            V((PAD, PAD), BF16),
            V((128, PAD), BF16),
            V((64, PAD), F32),
            V((256, PAD), BF16),
            S((2,)),
        ],
        far=1,
        far_outs=(0,),
    )
    small = ((8, LEAF), F32)
    top, source, links = call(
        up_kernel,
        [small, small, ((7, LEAF, LEAF), F32)],
        (half, pushed, link, other),
        [S((7,))],
        1,
        far=2,
        limit=50,
    )
    across = [(i, i ^ 12) for i in range(GROUPS)]
    other_top = lax.ppermute(top, ("half", "group"), across)
    line, high = call(
        square_kernel,
        [small, ((3, LEAF, LEAF), F32)],
        (half, source, square, link),
        [V((7, LEAF, LEAF), F32), S((9,))],
        1,
        far=2,
        limit=50,
        micros=2,
    )
    (paths,) = call(
        down_kernel,
        [((HALF * S3, 128), F32)],
        (top, other_top, line, links, high),
        limit=50,
    )
    paths = exchange(paths, S3, NEAR)
    (returning,) = call(
        backward_kernel,
        [((DEV * S4, 128), F32)],
        (
            home_at,
            half,
            paths,
            leaf_rows,
            idx,
            gram,
            leaf_inverse,
            leaf_below,
            leaf_solved,
            other,
        ),
        [
            V((64, PATH), F32),
            V((128, PATH), BF16),
            V((PATH, SPAN), BF16),
            V((PAD, PAD), BF16),
            V((128, PAD), BF16),
            V((64, SPAN), F32),
            V((256, PAD), BF16),
            S((2,)),
        ],
        2,
        far=2,
        limit=46,
    )
    returned = exchange(returning, S4)
    (sums,) = call(total_kernel, [((DEV * 2, 128), F32)], (returned,), micros=1)
    sums = exchange(sums, 2)
    (solved,) = call(
        unpack_kernel,
        [((64, ROWS), F32)],
        (key, returned),
        [V((PAD, PAD), BF16), V((128, PAD), BF16)],
    )
    return tuple(
        call(
            finish_kernel,
            [((64, 64), F32), ((64, 64), F32), ((64, ROWS), F32)],
            (sums, solved, block_now, block_before, coupling),
            [V((192, 2 * PAD), BF16)],
        )
    )


def solution(mesh):
    placed = (
        P(None, AXES),
        P(None, AXES),
        P(),
        P(AXES),
        P(AXES),
        P(AXES, None, None),
        P(AXES, None, None),
        P(AXES, None),
        P(),
        P(),
    )
    split_mesh = Mesh(mesh.devices.reshape(2, 8, 8), AXES)
    return jax.shard_map(
        per_device,
        mesh=split_mesh,
        in_specs=placed,
        out_specs=(P(), P(), P(None, AXES)),
        check_vma=False,
    )
```
